128 devices in a mesh: dp: 4 (over x), seq: 32 (over y, z, core).
Axes of the slice: x: 4, y: 4, z: 4, core: 2. Of those that a mesh axis runs over, the one named last changes fastest.
Arguments:
- activations: bfloat16 [4, 4352, 1024], P('dp', 'seq'), may hold values from -6 to 6
- qkv_weight: bfloat16 [1024, 1536], replicated, may hold values from -1 to 1
- out_weight: bfloat16 [512, 1024], replicated, may hold values from -0.25 to 0.25
- out_grad: bfloat16 [4, 4352, 1024], P('dp', 'seq'), may hold values from -6 to 6
Outputs:
- attended: bfloat16 [4, 4352, 1024], P('dp', 'seq')
- input_grad: bfloat16 [4, 4352, 1024], P('dp', 'seq')
- qkv_weight_grad: float32 [1024, 1536], P(('dp', 'seq'))
- out_weight_grad: float32 [512, 1024], P(None, ('dp', 'seq'))
The draws below stay inside these ranges and needn't reach their ends.
All inputs are finite; a program needn't handle non-finite values.
Results may differ from the reference program's by a relative error of at most 0.04.
Values may be sent and summed in bfloat16 or wider, within the bound.
A program may use at most 192 MiB of HBM per device.

```python
import math
import jax
import jax.numpy as jnp
import numpy as np
from jax import lax

D = 1024
HEADS = 8
HD = 64
LEVELS = 14
TOKENS = 4352
IMGS = 1
IMAGES = 4
N_DP = 4
N_SEQ = 32


spike_factor = 3.0


def draw_activations(key, part):
    key = jax.random.fold_in(key, 3)
    normal_key, pair_key = jax.random.split(key, 2)
    base = jnp.clip(jax.random.normal(normal_key, (IMAGES, TOKENS, D), jnp.float32), -6.0, 6.0)
    owners = N_DP * N_SEQ
    paired = jax.random.permutation(pair_key, owners)
    image_ids = jnp.arange(IMAGES, dtype=jnp.int32)[:, None]
    token_ids = jnp.arange(TOKENS, dtype=jnp.int32)[None, :]
    owner_ids = image_ids // IMGS * N_SEQ + token_ids // (TOKENS // N_SEQ)
    column_blocks = jnp.arange(D, dtype=jnp.int32) // (D // owners)
    spiked = paired[owner_ids][:, :, None] == column_blocks[None, None, :]
    base = jnp.where(spiked, jnp.clip(spike_factor * base, -6.0, 6.0), base)
    return base.astype(jnp.bfloat16)


def draw_qkv_weight(key, part):
    key = jax.random.fold_in(key, 5)
    inner_width = HEADS * HD
    weight = jnp.clip(jax.random.normal(key, (D, 3 * inner_width), jnp.float32), -6.0, 6.0) / math.sqrt(D)
    return weight.astype(jnp.bfloat16)


def with_spikes(entries, key, source, target, blocks, factor):
    owner, partner = [(jnp.arange(entries.shape[dim]) // (entries.shape[dim] // blocks)).reshape([-1 if axis == dim else 1 for axis in range(entries.ndim)]) for dim in (source, target)]
    chosen = jax.random.permutation(key, blocks)[partner]
    strong = (owner == chosen) | (owner == (partner + blocks // 2) % blocks)
    return jnp.where(strong, factor * entries, entries)


def block_levels(rng, extent, cuts, least, high):
    def one(axis_at, blocks):
        heights = jax.random.uniform(jax.random.fold_in(jax.random.fold_in(rng, 6), axis_at), (blocks,), jnp.float32, least / len(cuts), high / len(cuts))
        return jnp.repeat(jnp.exp(heights), extent[axis_at] // blocks).reshape((-1,) + (1,) * (len(extent) - axis_at - 1))

    loudness = one(*cuts[0])
    for cut in cuts[1:]:
        loudness = loudness * one(*cut)
    return loudness


def centred(stream_key, dims, deviation, limit, pieces=(), held_as=jnp.bfloat16):
    loudness = block_levels(stream_key, dims, pieces, -0.22, 0.18) if pieces else 1.0
    result = jax.random.normal(stream_key, dims, jnp.float32) * deviation * loudness
    return jnp.minimum(jnp.maximum(result, -limit), limit).astype(held_as)


def noise_with(stream_key, shape, scale, most, pieces, heavy, kind=jnp.bfloat16):
    entries = scale * jax.random.normal(stream_key, shape, jnp.float32)
    if pieces:
        entries = entries * block_levels(stream_key, shape, pieces, -0.22, 0.18)
    return jnp.clip(with_spikes(entries, jax.random.fold_in(stream_key, 3), *heavy), -most, most).astype(kind)


def setup_inputs(seed: int = 0) -> dict:
    key_of = jax.random.split(jax.random.key(seed), 5)
    activations = draw_activations(jax.random.fold_in(key_of[4], 71), 0)
    qkv_weight = draw_qkv_weight(jax.random.fold_in(key_of[4], 71), 0)
    out_weight = centred(key_of[2], (HEADS * HD, D), (HEADS * HD) ** -0.5, 0.25)
    out_grad = noise_with(key_of[3], (IMAGES, TOKENS, D), 1.0, 6.0, ((0, 4), (1, 32)), (1, 2, 32, 2.75))
    return dict(activations=activations, qkv_weight=qkv_weight, out_weight=out_weight, out_grad=out_grad)


scale_sides = (1, 2, 3, 4, 5, 8, 9, 10, 14, 16, 20, 24, 32, 40)
masked_score = -1e+30

def token_levels(positions):
    bounds = jnp.asarray(np.cumsum([side_len * side_len for side_len in scale_sides[:LEVELS]])[:-1], dtype=jnp.int32)
    return lax.optimization_barrier(jnp.sum((positions[:, None] >= bounds[None, :]).astype(jnp.int32), axis=1))

def reference(activations, qkv_weight, out_weight, out_grad):
    inner_width = HEADS * HD
    score_scale = 1.0 / math.sqrt(HD)
    levels = token_levels(jnp.arange(TOKENS, dtype=jnp.int32))
    allowed = levels[None, :] <= levels[:, None]
    shard_rows = TOKENS // N_SEQ
    outputs = []
    input_grads = []
    qkv_weight_grad = jnp.zeros((D, 3 * inner_width), jnp.float32)
    out_weight_grad = jnp.zeros((inner_width, D), jnp.float32)
    for image_index in range(IMAGES):
        source = activations[image_index]
        projected = jnp.dot(source, qkv_weight, preferred_element_type=jnp.float32).astype(jnp.bfloat16)
        per_head = projected.reshape(TOKENS, 3, HEADS, HD).transpose(1, 2, 0, 3)
        queries, key_rows, value_rows = (per_head[0], per_head[1], per_head[2])

        def forward_head(operands):
            head_q, head_k, head_v = operands
            scores = jnp.dot(head_q, head_k.T, preferred_element_type=jnp.float32) * score_scale
            scores = jnp.where(allowed, scores, masked_score)
            row_max = lax.optimization_barrier(jnp.max(scores, axis=1, keepdims=True))
            weights = jnp.exp(scores - row_max)
            row_sum = lax.optimization_barrier(jnp.sum(weights, axis=1, keepdims=True))
            mixed_rows = jnp.dot(weights.astype(jnp.bfloat16), head_v, preferred_element_type=jnp.float32) / row_sum
            return (mixed_rows.astype(jnp.bfloat16), (row_max + jnp.log(row_sum))[:, 0])
        head_context, log_totals = lax.map(forward_head, (queries, key_rows, value_rows))
        context = head_context.transpose(1, 0, 2).reshape(TOKENS, inner_width)
        outputs.append(jnp.dot(context, out_weight, preferred_element_type=jnp.float32).astype(jnp.bfloat16))
        context_grad = jnp.dot(out_grad[image_index], out_weight.T, preferred_element_type=jnp.float32).astype(jnp.bfloat16)
        row_dots = lax.optimization_barrier(jnp.sum((context_grad.astype(jnp.float32) * context.astype(jnp.float32)).reshape(TOKENS, HEADS, HD), axis=2)).T
        grad_heads = context_grad.reshape(TOKENS, HEADS, HD).transpose(1, 0, 2)

        def backward_head(operands):
            head_q, head_k, head_v, head_g, head_lse, head_dots = operands
            scores = jnp.dot(head_q, head_k.T, preferred_element_type=jnp.float32) * score_scale
            scores = jnp.where(allowed, scores, masked_score)
            probs_f = jnp.exp(scores - head_lse[:, None])
            prob_grad = jnp.dot(head_g, head_v.T, preferred_element_type=jnp.float32)
            score_grad = (probs_f * (prob_grad - head_dots[:, None]) * score_scale).astype(jnp.bfloat16)
            query_grad = jnp.dot(score_grad, head_k, preferred_element_type=jnp.float32).astype(jnp.bfloat16)
            grouped_scores = score_grad.reshape(N_SEQ, shard_rows, TOKENS).astype(jnp.float32)
            grouped_probs = probs_f.astype(jnp.bfloat16).reshape(N_SEQ, shard_rows, TOKENS).astype(jnp.float32)
            grouped_q = head_q.reshape(N_SEQ, shard_rows, HD).astype(jnp.float32)
            grouped_g = head_g.reshape(N_SEQ, shard_rows, HD).astype(jnp.float32)
            key_parts = jnp.einsum('gqk,gqd->gkd', grouped_scores, grouped_q, precision=lax.Precision.HIGHEST).astype(jnp.bfloat16)
            value_parts = jnp.einsum('gqk,gqd->gkd', grouped_probs, grouped_g, precision=lax.Precision.HIGHEST).astype(jnp.bfloat16)
            key_parts, value_parts = lax.optimization_barrier((key_parts, value_parts))
            key_grad = lax.optimization_barrier(jnp.sum(key_parts.astype(jnp.float32), axis=0)).astype(jnp.bfloat16)
            value_grad = lax.optimization_barrier(jnp.sum(value_parts.astype(jnp.float32), axis=0)).astype(jnp.bfloat16)
            return (query_grad, key_grad, value_grad)
        query_grad, key_grad, value_grad = lax.map(backward_head, (queries, key_rows, value_rows, grad_heads, log_totals, row_dots))
        qkv_grad = jnp.stack([query_grad, key_grad, value_grad]).transpose(2, 0, 1, 3).reshape(TOKENS, 3 * inner_width)
        input_grads.append(jnp.dot(qkv_grad, qkv_weight.T, preferred_element_type=jnp.float32).astype(jnp.bfloat16))
        qkv_weight_grad = qkv_weight_grad + jnp.dot(source.T, qkv_grad, preferred_element_type=jnp.float32)
        out_weight_grad = out_weight_grad + jnp.dot(context.T, out_grad[image_index], preferred_element_type=jnp.float32)
    return (jnp.stack(outputs), jnp.stack(input_grads), qkv_weight_grad, out_weight_grad)
```

```python
import functools
import math

import jax
import jax.numpy as jnp
import numpy as np
from jax import lax
from jax.experimental import pallas as pl
from jax.experimental.pallas import tpu as pltpu
from jax.sharding import PartitionSpec as P

MESH = pl.DeviceIdType.MESH
BF = jnp.bfloat16
F32 = jnp.float32

HEADS = 8
SEQ = 32
TOK = 136
PAD = 144
KEYS = SEQ * PAD
D = 1024
INNER = 512
SIDES = (1, 2, 3, 4, 5, 8, 9, 10, 14, 16, 20, 24, 32, 40)
ENDS = [int(v) for v in np.cumsum([a * a for a in SIDES])]
STARTS = [0] + ENDS[:-1]
FAR = 1 << 20
BIG = 1e30
ONE = 15
TWO = 16
CHUNK = 512
BATCHES = (
    (0, 3 * PAD, 4608),
    (3 * PAD, 2 * PAD, 3072),
    (5 * PAD, PAD, 2048),
    (6 * PAD, PAD, 1536),
    (7 * PAD, PAD, 1024),
)
ORDERS = ("xyz", "yzx", "zxy")
COLS = ((0, 384), (384, 384), (768, 256))
NT = (((1,), (1,)), ((), ()))


def dot(a, b):
    return jnp.dot(a, b, preferred_element_type=F32)


def dot_nt(a, b):
    return lax.dot_general(a, b, NT, preferred_element_type=F32)


def lane_bounds(rows):
    lane = lax.broadcasted_iota(jnp.int32, (rows, 128), 1)
    lo = jnp.full((rows, 128), -1, jnp.int32)
    hi = jnp.full((rows, 128), -1, jnp.int32)
    for i, (a, b) in enumerate(zip(STARTS, ENDS)):
        lo = jnp.where(lane == i, a, lo)
        hi = jnp.where(lane == i, b, hi)
    lo = jnp.where(lane == 14, FAR, lo)
    hi = jnp.where(lane == 14, FAR + 1, hi)
    ones = (lane == ONE) | (lane == TWO)
    lo = jnp.where(ones, 0, lo)
    hi = jnp.where(ones, ENDS[-1], hi)
    return lo, hi


def swap_pack(a, b, left):
    return (
        jnp.where(left, a, pltpu.roll(b, 64, 1)),
        jnp.where(left, pltpu.roll(a, 64, 1), b),
    )


def kernel(act_h, wqkv_h, wout_h, og_h, att_o, ing_o, wq_o, wo_o,
           al, alT, wqkv, wout, sendkv, sendqg, kvx, qg, qx, sbuf, pbuf, macc, acc, dq,
           qgT, dkT, dkvb, sibr, resb, rqc, rkv, catb, fb,
           r1a, r1b, r1c, g1a, g1b, g1c, r2a, r2b, r2c, g2a, g2b, g2c, r3a, r3b, r3c,
           fin, lsem, ssem, rsem, fs, fr):
    x = lax.axis_index("dp")
    s = lax.axis_index("seq")
    head, quarter = s // 4, s % 4
    pos, core = s // 2, s % 2
    y, z = s // 8, (s // 2) % 4
    sib = s + 1 - 2 * core

    cin = [
        pltpu.make_async_copy(act_h.at[0], al.at[0, pl.ds(0, TOK)], lsem.at[0]),
        pltpu.make_async_copy(wqkv_h, wqkv, lsem.at[1]),
        pltpu.make_async_copy(og_h.at[0], al.at[1, pl.ds(0, TOK)], lsem.at[2]),
        pltpu.make_async_copy(wout_h, wout, lsem.at[3]),
    ]
    for c in cin:
        c.start()

    bar = pltpu.get_barrier_semaphore()

    @pl.loop(1, 16)
    def _(k):
        pl.semaphore_signal(bar, inc=1, device_id=(x, 2 * ((pos + k) % 16) + core), device_id_type=MESH)

    pl.semaphore_signal(bar, inc=1, device_id=(x, sib), device_id_type=MESH)
    for k in range(1, 4):
        pl.semaphore_signal(bar, inc=1, device_id=((x + k) % 4, s), device_id_type=MESH)

    al[0, TOK:PAD, :] = jnp.zeros((PAD - TOK, D), BF)
    al[1, TOK:PAD, :] = jnp.zeros((PAD - TOK, D), BF)
    pl.semaphore_wait(bar, 19)

    def remote(src, dst, send, recv, dev):
        return pltpu.make_async_remote_copy(
            src_ref=src, dst_ref=dst, send_sem=send, recv_sem=recv, device_id=dev, device_id_type=MESH)

    def rows(ref, first, count=PAD):
        return ref.at[pl.ds(pl.multiple_of(first, 16), count)]

    def kvslot(g):
        return kvx.at[pl.ds(pl.multiple_of(g * PAD, 16), PAD), pl.ds(0, 128)]

    left = lax.broadcasted_iota(jnp.int32, (PAD, 128), 1) < 64

    cin[0].wait()
    cin[1].wait()
    kp = dot(al[0, 0:PAD, :], wqkv[:, INNER:2 * INNER])
    vp = dot(al[0, 0:PAD, :], wqkv[:, 2 * INNER:])
    for i in range(4):
        a, b = swap_pack(kp[:, 128 * i:128 * i + 128], vp[:, 128 * i:128 * i + 128], left)
        sendkv[(2 * i) * PAD:(2 * i + 1) * PAD, :] = a.astype(BF)
        sendkv[(2 * i + 1) * PAD:(2 * i + 2) * PAD, :] = b.astype(BF)

    own_kv = pltpu.make_async_copy(rows(sendkv, head * PAD), kvslot(s), lsem.at[4])
    own_kv.start()

    @pl.loop(1, 16)
    def _(k):
        to = (pos + k) % 16
        remote(rows(sendkv, (to // 2) * PAD), kvslot(s), ssem.at[0], rsem.at[0], (x, 2 * to + core)).start()

    cin[2].wait()
    cin[3].wait()
    qp = dot(al[0, 0:PAD, :], wqkv[:, 0:INNER])
    gp = dot_nt(al[1, 0:PAD, :], wout[...])
    for i in range(4):
        a, b = swap_pack(qp[:, 128 * i:128 * i + 128], gp[:, 128 * i:128 * i + 128], left)
        sendqg[(2 * i) * PAD:(2 * i + 1) * PAD, :] = a.astype(BF)
        sendqg[(2 * i + 1) * PAD:(2 * i + 2) * PAD, :] = b.astype(BF)

    slot = 7 - s // 4
    own_qg = pltpu.make_async_copy(rows(sendqg, head * PAD), rows(qg, slot * PAD), lsem.at[5])
    own_qg.start()

    @pl.loop(1, 8)
    def _(k):
        to = (head + k) % 8
        remote(rows(sendqg, to * PAD), rows(qg, slot * PAD), ssem.at[1], rsem.at[1], (x, 4 * to + quarter)).start()

    inputs_to_sib = remote(al.at[:, pl.ds(0, PAD)], al.at[:, pl.ds(PAD, PAD)], ssem.at[2], rsem.at[2], (x, sib))
    inputs_to_sib.start()

    lo, hi = lane_bounds(PAD)
    place = lax.broadcasted_iota(jnp.int32, (PAD, 128), 0)

    @pl.loop(0, SEQ)
    def _(g):
        t = jnp.where(place < TOK, place + g * TOK, FAR)
        kvx[pl.ds(pl.multiple_of(g * PAD, 16), PAD), 128:256] = jnp.where(
            (t >= lo) & (t < hi), 1.0, 0.0).astype(BF)

    own_kv.wait()
    remote(rows(dkvb, 0, 15 * PAD), rows(dkvb, 0, 15 * PAD), ssem.at[0], rsem.at[0], (x, sib)).wait_recv()

    @pl.loop(0, 16)
    def _(k):
        g = 2 * k + core
        remote(kvslot(g), kvslot(g), ssem.at[3], rsem.at[3], (x, sib)).start()

    own_qg.wait()
    remote(rows(dkvb, 0, 7 * PAD), rows(dkvb, 0, 7 * PAD), ssem.at[1], rsem.at[1], (x, sib)).wait_recv()

    @pl.loop(0, 8)
    def _(j):
        g = 4 * (7 - j) + quarter
        t = jnp.where(place < TOK, place + g * TOK, ENDS[-1] - 1)
        r = pl.ds(pl.multiple_of(j * PAD, 16), PAD)
        qx[r, 128:256] = jnp.where(lo > t, -BIG, 0.0).astype(BF)
        qx[r, 0:128] = jnp.where(left, qg[r, :].astype(F32) * 0.125, 0.0).astype(BF)

    remote(rows(dkvb, 0, 16 * PAD), rows(dkvb, 0, 16 * PAD), ssem.at[3], rsem.at[3], (x, sib)).wait()

    for number, (row0, count, keys) in enumerate(BATCHES):
        rr = slice(row0, row0 + count)
        steps = keys // CHUNK
        macc[0:count, :] = jnp.full((count, 128), -3e38, F32)

        @pl.loop(0, steps)
        def _(c):
            kk = pl.ds(pl.multiple_of(c * CHUNK, CHUNK), CHUNK)
            sc = dot_nt(qx[rr, :], kvx[kk, :])
            sbuf[0:count, kk] = sc
            top = macc[0:count, :]
            for i in range(CHUNK // 128):
                top = jnp.maximum(top, sc[:, 128 * i:128 * i + 128])
            macc[0:count, :] = top

        row_max = jnp.max(macc[0:count, :], axis=1, keepdims=True)
        acc[0:count, :] = jnp.zeros((count, 256), F32)

        @pl.loop(0, steps)
        def _(c):
            kk = pl.ds(pl.multiple_of(c * CHUNK, CHUNK), CHUNK)
            p = jnp.exp(sbuf[0:count, kk] - row_max).astype(BF)
            pbuf[0:count, kk] = p
            acc[0:count, :] += dot(p, kvx[kk, :])

        lane = lax.broadcasted_iota(jnp.int32, (count, 128), 1)
        near = lane < 64
        inv = 1.0 / acc[0:count, 128 + ONE:128 + ONE + 1]
        ctx = (acc[0:count, 0:128] * inv).astype(BF)
        qrow = qg[rr, :].astype(F32)
        dots = jnp.sum(jnp.where(near, 0.0, ctx.astype(F32) * qrow), axis=1, keepdims=True)
        dhi = dots.astype(BF).astype(F32)
        dlo = dots - dhi
        qx[rr, 0:128] = jnp.where(near, 0.0, qrow).astype(BF)
        qx[rr, 128:256] = jnp.where(lane == ONE, -dhi, jnp.where(lane == TWO, -dlo, 0.0)).astype(BF)
        qn = qrow * jnp.where(near, 0.125 * inv, inv)
        qgT[:, 0:count] = qn.T.astype(BF)
        dq[0:count, :] = jnp.zeros((count, 128), F32)

        @pl.loop(0, steps)
        def _(c):
            kk = pl.ds(pl.multiple_of(c * CHUNK, CHUNK), CHUNK)
            p = pbuf[0:count, kk]
            dpd = dot_nt(qx[rr, :], kvx[kk, :])
            ds = (p.astype(F32) * dpd).astype(BF)
            dq[0:count, :] += dot(ds, kvx[kk, 0:128])
            dk = dot(qgT[0:64, 0:count], ds)
            dv = dot(qgT[64:128, 0:count], p)
            if number == 0:
                dkT[0:64, kk] = dk
                dkT[64:128, kk] = dv
            else:
                dkT[0:64, kk] += dk
                dkT[64:128, kk] += dv

        resb[rr, :] = jnp.where(near, dq[0:count, :] * (0.125 * inv), ctx.astype(F32)).astype(BF)

    own_res = pltpu.make_async_copy(rows(resb, slot * PAD), rows(rqc, head * PAD), lsem.at[6])
    own_res.start()

    @pl.loop(1, 8)
    def _(k):
        to = (head + k) % 8
        remote(rows(resb, (7 - to) * PAD), rows(rqc, head * PAD), ssem.at[4], rsem.at[4],
               (x, 4 * to + quarter)).start()

    @pl.loop(0, KEYS // CHUNK)
    def _(c):
        kk = pl.ds(pl.multiple_of(c * CHUNK, CHUNK), CHUNK)
        dkvb[kk, :] = dkT[:, kk].T.astype(BF)

    @pl.loop(0, 16)
    def _(k):
        g = 2 * k + 1 - core
        remote(rows(dkvb, g * PAD), rows(sibr, g * PAD), ssem.at[5], rsem.at[5], (x, sib)).start()

    remote(rows(dkvb, 0, 16 * PAD), rows(sibr, 0, 16 * PAD), ssem.at[5], rsem.at[5], (x, sib)).wait_recv()

    @pl.loop(0, 16)
    def _(k):
        r = pl.ds(pl.multiple_of((2 * k + core) * PAD, 16), PAD)
        dkvb[r, :] = (dkvb[r, :].astype(F32) + sibr[r, :].astype(F32)).astype(BF)

    part = 2 * head + (pos % 2)
    own_dkv = pltpu.make_async_copy(rows(dkvb, s * PAD), rows(rkv, part * PAD), lsem.at[7])
    own_dkv.start()

    @pl.loop(1, 16)
    def _(k):
        to = 2 * ((pos + k) % 16) + core
        remote(rows(dkvb, to * PAD), rows(rkv, part * PAD), ssem.at[6], rsem.at[6], (x, to)).start()

    inputs_to_sib.wait()
    for i in range(2):
        for j in range(8):
            alT[i, 128 * j:128 * j + 128, :] = al[i, :, 128 * j:128 * j + 128].T

    own_res.wait()
    remote(rows(rqc, 0, 7 * PAD), rows(rqc, 0, 7 * PAD), ssem.at[4], rsem.at[4], (x, sib)).wait()
    for i in range(4):
        a = rqc[(2 * i) * PAD:(2 * i + 1) * PAD, :].astype(F32)
        b = rqc[(2 * i + 1) * PAD:(2 * i + 2) * PAD, :].astype(F32)
        q_pair, c_pair = swap_pack(a, b, left)
        catb[0, 0:PAD, 128 * i:128 * i + 128] = q_pair.astype(BF)
        catb[3, 0:PAD, 128 * i:128 * i + 128] = c_pair.astype(BF)
    att = dot(catb[3, 0:PAD, :], wout[...])
    att_o[0] = att[0:TOK].astype(BF)

    own_dkv.wait()
    remote(rows(rkv, 0, 15 * PAD), rows(rkv, 0, 15 * PAD), ssem.at[6], rsem.at[6], (x, sib)).wait()
    for i in range(4):
        a = rkv[(4 * i) * PAD:(4 * i + 1) * PAD, :].astype(F32) + rkv[(4 * i + 1) * PAD:(4 * i + 2) * PAD, :].astype(F32)
        b = rkv[(4 * i + 2) * PAD:(4 * i + 3) * PAD, :].astype(F32) + rkv[(4 * i + 3) * PAD:(4 * i + 4) * PAD, :].astype(F32)
        k_pair, v_pair = swap_pack(a, b, left)
        catb[1, 0:PAD, 128 * i:128 * i + 128] = k_pair.astype(BF)
        catb[2, 0:PAD, 128 * i:128 * i + 128] = v_pair.astype(BF)

    cat_to_sib = remote(catb.at[pl.ds(2 - 2 * core, 2), pl.ds(0, PAD)], catb.at[pl.ds(2 - 2 * core, 2), pl.ds(PAD, PAD)],
                        ssem.at[7], rsem.at[7], (x, sib))
    cat_to_sib.start()
    ing = dot_nt(catb[0, 0:PAD, :], wqkv[:, 0:INNER])
    ing += dot_nt(catb[1, 0:PAD, :], wqkv[:, INNER:2 * INNER])
    ing += dot_nt(catb[2, 0:PAD, :], wqkv[:, 2 * INNER:])
    ing_o[0] = ing[0:TOK].astype(BF)
    cat_to_sib.wait()

    for half in range(2):
        which = 0 if half == 0 else core
        right = catb[2 * core + half]

        @pl.loop(0, 4)
        def _(i):
            f = dot(alT[which, pl.ds(pl.multiple_of(i * 256, 256), 256), :], right)
            fb[i, :, :, :, INNER * half:INNER * half + INNER] = f.astype(BF).reshape(4, 4, 16, INNER)

    coords = {"x": x, "y": y, "z": z}

    def peer(axis, k):
        c = dict(coords)
        c[axis] = (coords[axis] + k) % 4
        return c[axis], (c["x"], c["y"] * 8 + c["z"] * 2 + core)

    def stage(o, phase, take, recv):
        for k in range(1, 4):
            there, dev = peer(ORDERS[o][phase], k)
            remote(take(there), recv.at[k - 1], fs.at[3 * phase + o], fr.at[3 * phase + o], dev).start()

    def arrived(o, phase, recv):
        remote(recv, recv, fs.at[3 * phase + o], fr.at[3 * phase + o], (x, sib)).wait()

    def total(mine, recv):
        v = mine.astype(F32)
        for k in range(3):
            v += recv[k].astype(F32)
        return v

    def cols(o):
        return pl.ds(*COLS[o])

    takes1 = (
        lambda t: fb.at[t, :, :, :, cols(0)],
        lambda t: fb.at[:, t, :, :, cols(1)],
        lambda t: fb.at[:, :, t, :, cols(2)],
    )
    r1, g1 = (r1a, r1b, r1c), (g1a, g1b, g1c)
    r2, g2 = (r2a, r2b, r2c), (g2a, g2b, g2c)
    r3 = (r3a, r3b, r3c)
    takes2 = (lambda t: g1a.at[t], lambda t: g1b.at[:, t], lambda t: g1c.at[t])
    for o in range(3):
        stage(o, 0, takes1[o], r1[o])
    for o in range(3):
        arrived(o, 0, r1[o])
        mine = coords[ORDERS[o][0]]
        g1[o][...] = total(takes1[o](mine)[...], r1[o]).astype(BF)
        stage(o, 1, takes2[o], r2[o])
    for o in range(3):
        arrived(o, 1, r2[o])
        mine = coords[ORDERS[o][1]]
        g2[o][...] = total(takes2[o](mine)[...], r2[o]).astype(BF)
        stage(o, 2, lambda t, o=o: g2[o].at[t], r3[o])
    for o in range(3):
        arrived(o, 2, r3[o])
        mine = coords[ORDERS[o][2]]
        v = total(g2[o][mine], r3[o])
        a, n = COLS[o]
        fin[core, 0, :, a:a + n] = v[0:8]
        fin[core, 1, :, a:a + n] = v[8:16]

    last = remote(fin.at[core, 1 - core], fin.at[core, 1 - core], ssem.at[8], rsem.at[8], (x, sib))
    last.start()
    last.wait()
    wq_o[:, 0:D] = fin[0, core]
    wq_o[:, D:] = fin[1, core, :, 0:INNER]
    wo_o[...] = fin[1, core, :, INNER:]

    remote(rows(dkvb, 0, 15 * PAD), rows(dkvb, 0, 15 * PAD), ssem.at[0], rsem.at[0], (x, sib)).wait_send()
    remote(rows(dkvb, 0, 7 * PAD), rows(dkvb, 0, 7 * PAD), ssem.at[1], rsem.at[1], (x, sib)).wait_send()
    remote(rows(dkvb, 0, 16 * PAD), rows(dkvb, 0, 16 * PAD), ssem.at[5], rsem.at[5], (x, sib)).wait_send()


def shards(activations, qkv_weight, out_weight, out_grad):
    any_spec = pl.BlockSpec(memory_space=pl.ANY)
    vmem = pl.BlockSpec(memory_space=pltpu.VMEM)
    V = pltpu.VMEM
    widths = [c[1] for c in COLS]
    scratch = [
        V((2, 2 * PAD, D), BF),
        V((2, D, 2 * PAD), BF),
        V((D, 3 * INNER), BF),
        V((INNER, D), BF),
        V((8 * PAD, 128), BF),
        V((8 * PAD, 128), BF),
        V((KEYS, 256), BF),
        V((8 * PAD, 128), BF),
        V((8 * PAD, 256), BF),
        V((3 * PAD, KEYS), F32),
        V((3 * PAD, KEYS), BF),
        V((3 * PAD, 128), F32),
        V((3 * PAD, 256), F32),
        V((3 * PAD, 128), F32),
        V((128, 3 * PAD), BF),
        V((128, KEYS), F32),
        V((KEYS, 128), BF),
        V((KEYS, 128), BF),
        V((8 * PAD, 128), BF),
        V((8 * PAD, 128), BF),
        V((16 * PAD, 128), BF),
        V((4, 2 * PAD, INNER), BF),
        V((4, 4, 4, 16, D), BF),
    ]
    scratch += [V((3, 4, 4, 16, w), BF) for w in widths]
    scratch += [V((4, 4, 16, w), BF) for w in widths]
    scratch += [V((3, 4, 16, w), BF) for w in widths]
    scratch += [V((4, 16, w), BF) for w in widths]
    scratch += [V((3, 16, w), BF) for w in widths]
    scratch += [
        V((2, 2, 8, D), F32),
        pltpu.SemaphoreType.DMA((8,)),
        pltpu.SemaphoreType.DMA((9,)),
        pltpu.SemaphoreType.DMA((9,)),
        pltpu.SemaphoreType.DMA((9,)),
        pltpu.SemaphoreType.DMA((9,)),
    ]
    att, ing, wq, wo = pl.pallas_call(
        kernel,
        out_shape=(
            jax.ShapeDtypeStruct((1, TOK, D), BF),
            jax.ShapeDtypeStruct((1, TOK, D), BF),
            jax.ShapeDtypeStruct((8, 3 * INNER), F32),
            jax.ShapeDtypeStruct((8, INNER), F32),
        ),
        in_specs=[any_spec] * 4,
        out_specs=(vmem,) * 4,
        scratch_shapes=scratch,
        compiler_params=pltpu.CompilerParams(
            collective_id=0, has_side_effects=True, vmem_limit_bytes=56 * 1024 * 1024),
        name="attention_sublayer",
    )(activations, qkv_weight, out_weight, out_grad)
    return att, ing, wq, wo.T


def solution(mesh):
    return jax.shard_map(
        shards,
        mesh=mesh,
        in_specs=(P("dp", "seq", None), P(), P(), P("dp", "seq", None)),
        out_specs=(
            P("dp", "seq", None),
            P("dp", "seq", None),
            P(("dp", "seq"), None),
            P(None, ("dp", "seq")),
        ),
        check_vma=False,
    )
```

```python
import functools
import math

import jax
import jax.numpy as jnp
import numpy as np
from jax import lax
from jax.experimental import pallas as pl
from jax.experimental.pallas import tpu as pltpu
from jax.sharding import PartitionSpec as P

MESH = pl.DeviceIdType.MESH
BF = jnp.bfloat16
F32 = jnp.float32

HEADS = 8
SEQ = 32
TOK = 136
PAD = 144
KEYS = SEQ * PAD
D = 1024
INNER = 512
SIDES = (1, 2, 3, 4, 5, 8, 9, 10, 14, 16, 20, 24, 32, 40)
ENDS = [int(v) for v in np.cumsum([a * a for a in SIDES])]
STARTS = [0] + ENDS[:-1]
FAR = 1 << 20
BIG = 1e30
ONE = 15
TWO = 16
BATCHES = (
    (0, 3, 4608, 2304, 22, 32),
    (3, 2, 3072, 1536, 14, 22),
    (5, 3, 1920, 1920, 0, 14),
)
ORDERS = ("xyz", "yzx", "zxy")
COLS = ((0, 384), (384, 384), (768, 256))
NT = (((1,), (1,)), ((), ()))


def dot(a, b):
    return jnp.dot(a, b, preferred_element_type=F32)


def dot_nt(a, b):
    return lax.dot_general(a, b, NT, preferred_element_type=F32)


def lane_bounds(rows):
    lane = lax.broadcasted_iota(jnp.int32, (rows, 128), 1)
    lo = jnp.full((rows, 128), -1, jnp.int32)
    hi = jnp.full((rows, 128), -1, jnp.int32)
    for i, (a, b) in enumerate(zip(STARTS, ENDS)):
        lo = jnp.where(lane == i, a, lo)
        hi = jnp.where(lane == i, b, hi)
    lo = jnp.where(lane == 14, FAR, lo)
    hi = jnp.where(lane == 14, FAR + 1, hi)
    ones = (lane == ONE) | (lane == TWO)
    lo = jnp.where(ones, 0, lo)
    hi = jnp.where(ones, ENDS[-1], hi)
    return lo, hi


def swap_pack(a, b, left):
    return (
        jnp.where(left, a, pltpu.roll(b, 64, 1)),
        jnp.where(left, pltpu.roll(a, 64, 1), b),
    )


def kernel(act_h, wqkv_h, wout_h, og_h, att_o, ing_o, wq_o, wo_o,
           al, alT, wqkv, wout, sendkv, sendqg, kvx, qg, qx, sbuf, pbuf, macc, acc, dq,
           qgT, dkT, dkvb, sibr, resb, rqc, rkv, catb, fb,
           r1a, r1b, r1c, g1a, g1b, g1c, r2a, r2b, r2c, g2a, g2b, g2c, r3a, r3b, r3c,
           fin, attb, ingb, wob, lsem, ssem, rsem, fs, fr, ksem, dsem):
    x = lax.axis_index("dp")
    s = lax.axis_index("seq")
    head, quarter = s // 4, s % 4
    pos, core = s // 2, s % 2
    y, z = s // 8, (s // 2) % 4
    sib = s + 1 - 2 * core

    cin = [
        pltpu.make_async_copy(act_h.at[0], al.at[0, pl.ds(0, TOK)], lsem.at[0]),
        pltpu.make_async_copy(wqkv_h, wqkv, lsem.at[1]),
        pltpu.make_async_copy(og_h.at[0], al.at[1, pl.ds(0, TOK)], lsem.at[2]),
        pltpu.make_async_copy(wout_h, wout, lsem.at[3]),
    ]
    for c in cin:
        c.start()

    bar = pltpu.get_barrier_semaphore()

    @pl.loop(1, 16)
    def _(k):
        pl.semaphore_signal(bar, inc=1, device_id=(x, 2 * ((pos + k) % 16) + core), device_id_type=MESH)

    pl.semaphore_signal(bar, inc=1, device_id=(x, sib), device_id_type=MESH)
    for k in range(1, 4):
        pl.semaphore_signal(bar, inc=1, device_id=((x + k) % 4, s), device_id_type=MESH)

    al[0, TOK:PAD, :] = jnp.zeros((PAD - TOK, D), BF)
    al[1, TOK:PAD, :] = jnp.zeros((PAD - TOK, D), BF)
    pl.semaphore_wait(bar, 19)

    def remote(src, dst, send, recv, dev):
        return pltpu.make_async_remote_copy(
            src_ref=src, dst_ref=dst, send_sem=send, recv_sem=recv, device_id=dev, device_id_type=MESH)

    def rows(ref, first, count=PAD):
        return ref.at[pl.ds(pl.multiple_of(first, 16), count)]

    def kvslot(g):
        return kvx.at[pl.ds(pl.multiple_of(g * PAD, 16), PAD), pl.ds(0, 128)]

    left = lax.broadcasted_iota(jnp.int32, (PAD, 128), 1) < 64

    cin[0].wait()
    cin[1].wait()
    kp = dot(al[0, 0:PAD, :], wqkv[:, INNER:2 * INNER])
    vp = dot(al[0, 0:PAD, :], wqkv[:, 2 * INNER:])
    for i in range(4):
        a, b = swap_pack(kp[:, 128 * i:128 * i + 128], vp[:, 128 * i:128 * i + 128], left)
        sendkv[(2 * i) * PAD:(2 * i + 1) * PAD, :] = a.astype(BF)
        sendkv[(2 * i + 1) * PAD:(2 * i + 2) * PAD, :] = b.astype(BF)

    own_kv = pltpu.make_async_copy(rows(sendkv, head * PAD), kvslot(s), lsem.at[4])
    own_kv.start()
    remote(rows(sendkv, head * PAD), kvslot(s), ssem.at[3], rsem.at[3], (x, sib)).start()

    @pl.loop(1, 16)
    def _(k):
        to = (pos + k) % 16
        remote(rows(sendkv, (to // 2) * PAD), kvslot(s), ssem.at[0], ksem.at[pos], (x, 2 * to + core)).start()

    cin[2].wait()
    inputs_to_sib = remote(al.at[:, pl.ds(0, PAD)], al.at[:, pl.ds(PAD, PAD)], ssem.at[2], rsem.at[2], (x, sib))
    inputs_to_sib.start()
    cin[3].wait()
    qp = dot(al[0, 0:PAD, :], wqkv[:, 0:INNER])
    gp = dot_nt(al[1, 0:PAD, :], wout[...])
    for i in range(4):
        a, b = swap_pack(qp[:, 128 * i:128 * i + 128], gp[:, 128 * i:128 * i + 128], left)
        sendqg[(2 * i) * PAD:(2 * i + 1) * PAD, :] = a.astype(BF)
        sendqg[(2 * i + 1) * PAD:(2 * i + 2) * PAD, :] = b.astype(BF)

    slot = 7 - s // 4
    own_qg = pltpu.make_async_copy(rows(sendqg, head * PAD), rows(qg, slot * PAD), lsem.at[5])
    own_qg.start()

    @pl.loop(1, 8)
    def _(k):
        to = (head + k) % 8
        remote(rows(sendqg, to * PAD), rows(qg, slot * PAD), ssem.at[1], rsem.at[1], (x, 4 * to + quarter)).start()

    lo, hi = lane_bounds(PAD)
    place = lax.broadcasted_iota(jnp.int32, (PAD, 128), 0)

    @pl.loop(0, SEQ)
    def _(g):
        t = jnp.where(place < TOK, place + g * TOK, FAR)
        kvx[pl.ds(pl.multiple_of(g * PAD, 16), PAD), 128:256] = jnp.where(
            (t >= lo) & (t < hi), 1.0, 0.0).astype(BF)

    @pl.loop(1, 16)
    def _(k):
        frm = (pos + 16 - k) % 16
        g = 2 * frm + core
        remote(kvslot(g), kvslot(g), ssem.at[0], ksem.at[frm], (x, sib)).wait_recv()
        remote(kvslot(g), kvslot(g), ssem.at[3], rsem.at[3], (x, sib)).start()

    own_kv.wait()
    inputs_to_sib.wait()
    for i in range(2):
        for j in range(8):
            alT[i, 128 * j:128 * j + 128, :] = al[i, :, 128 * j:128 * j + 128].T

    own_qg.wait()
    remote(rows(dkvb, 0, 7 * PAD), rows(dkvb, 0, 7 * PAD), ssem.at[1], rsem.at[1], (x, sib)).wait_recv()

    @pl.loop(0, 8)
    def _(j):
        g = 4 * (7 - j) + quarter
        t = jnp.where(place < TOK, place + g * TOK, ENDS[-1] - 1)
        r = pl.ds(pl.multiple_of(j * PAD, 16), PAD)
        qx[r, 128:256] = jnp.where(lo > t, -BIG, 0.0).astype(BF)
        qx[r, 0:128] = jnp.where(left, qg[r, :].astype(F32) * 0.125, 0.0).astype(BF)

    remote(rows(dkvb, 0, 16 * PAD), rows(dkvb, 0, 16 * PAD), ssem.at[3], rsem.at[3], (x, sib)).wait()

    part = 2 * head + (pos % 2)

    def finish(lo_group, hi_group):
        lo_row, hi_row = lo_group * PAD, hi_group * PAD
        for blk in range(lo_row // 128, -(-hi_row // 128)):
            a, b = max(lo_row - 128 * blk, 0), min(hi_row - 128 * blk, 128)
            v = dkT[:, 128 * blk:128 * blk + 128].T
            dkvb[128 * blk + a:128 * blk + b, :] = v[a:b].astype(BF)

    def to_sibling(number, lo_group, hi_group):
        @pl.loop(lo_group // 2, hi_group // 2)
        def _(k):
            g = 2 * k + 1 - core
            remote(rows(dkvb, g * PAD), rows(sibr, g * PAD), ssem.at[5], dsem.at[number], (x, sib)).start()

    def to_owners(number, lo_group, hi_group):
        n = (hi_group - lo_group) // 2 * PAD
        remote(rows(dkvb, 0, n), rows(sibr, 0, n), ssem.at[5], dsem.at[number], (x, sib)).wait_recv()

        @pl.loop(lo_group // 2, hi_group // 2)
        def _(k):
            g = 2 * k + core
            r = pl.ds(pl.multiple_of(g * PAD, 16), PAD)
            dkvb[r, :] = (dkvb[r, :].astype(F32) + sibr[r, :].astype(F32)).astype(BF)

            @pl.when(k != pos)
            def _():
                remote(rows(dkvb, g * PAD), rows(rkv, part * PAD), ssem.at[6], rsem.at[6], (x, g)).start()

            @pl.when(k == pos)
            def _():
                pltpu.make_async_copy(rows(dkvb, g * PAD), rows(rkv, part * PAD), lsem.at[7]).start()

    for number, (slot0, slots, keys, CHUNK, lo_group, hi_group) in enumerate(BATCHES):
        row0, count = slot0 * PAD, slots * PAD
        rr = slice(row0, row0 + count)
        steps = keys // CHUNK
        macc[0:count, :] = jnp.full((count, 128), -3e38, F32)

        @pl.loop(0, steps)
        def _(c):
            kk = pl.ds(pl.multiple_of(c * CHUNK, 128), CHUNK)
            sc = dot_nt(qx[rr, :], kvx[kk, :])
            sbuf[0:count, kk] = sc
            top = macc[0:count, :]
            for i in range(CHUNK // 128):
                top = jnp.maximum(top, sc[:, 128 * i:128 * i + 128])
            macc[0:count, :] = top

        row_max = jnp.max(macc[0:count, :], axis=1, keepdims=True)
        acc[0:count, :] = jnp.zeros((count, 256), F32)

        @pl.loop(0, steps)
        def _(c):
            kk = pl.ds(pl.multiple_of(c * CHUNK, 128), CHUNK)
            p = jnp.exp(sbuf[0:count, kk] - row_max).astype(BF)
            pbuf[0:count, kk] = p
            acc[0:count, :] += dot(p, kvx[kk, :])

        lane = lax.broadcasted_iota(jnp.int32, (count, 128), 1)
        near = lane < 64
        inv = 1.0 / acc[0:count, 128 + ONE:128 + ONE + 1]
        ctx = (acc[0:count, 0:128] * inv).astype(BF)
        qrow = qg[rr, :].astype(F32)
        dots = jnp.sum(jnp.where(near, 0.0, ctx.astype(F32) * qrow), axis=1, keepdims=True)
        dhi = dots.astype(BF).astype(F32)
        dlo = dots - dhi
        qx[rr, 0:128] = jnp.where(near, 0.0, qrow).astype(BF)
        qx[rr, 128:256] = jnp.where(lane == ONE, -dhi, jnp.where(lane == TWO, -dlo, 0.0)).astype(BF)
        qn = qrow * jnp.where(near, 0.125 * inv, inv)
        qgT[:, 0:count] = qn.T.astype(BF)
        dq[0:count, :] = jnp.zeros((count, 128), F32)

        @pl.loop(0, steps)
        def _(c):
            kk = pl.ds(pl.multiple_of(c * CHUNK, 128), CHUNK)
            p = pbuf[0:count, kk]
            dpd = dot_nt(qx[rr, :], kvx[kk, :])
            ds = (p.astype(F32) * dpd).astype(BF)
            dq[0:count, :] += dot(ds, kvx[kk, 0:128])
            dk = dot(qgT[0:64, 0:count], ds)
            dv = dot(qgT[64:128, 0:count], p)
            if number == 0:
                dkT[0:64, kk] = dk
                dkT[64:128, kk] = dv
            else:
                dkT[0:64, kk] += dk
                dkT[64:128, kk] += dv

        resb[rr, :] = jnp.where(near, dq[0:count, :] * (0.125 * inv), ctx.astype(F32)).astype(BF)

        for j in range(slot0, slot0 + slots):
            to = 7 - j

            @pl.when(head != to)
            def _():
                remote(rows(resb, j * PAD), rows(rqc, head * PAD), ssem.at[4], rsem.at[4],
                       (x, 4 * to + quarter)).start()

            @pl.when(head == to)
            def _():
                pltpu.make_async_copy(rows(resb, j * PAD), rows(rqc, head * PAD), lsem.at[6]).start()

        finish(lo_group, hi_group)
        to_sibling(number, lo_group, hi_group)
        if number > 0:
            to_owners(number - 1, *BATCHES[number - 1][4:])

    to_owners(len(BATCHES) - 1, *BATCHES[-1][4:])

    pltpu.make_async_copy(rows(resb, 0), rows(rqc, 0), lsem.at[6]).wait()
    remote(rows(rqc, 0, 7 * PAD), rows(rqc, 0, 7 * PAD), ssem.at[4], rsem.at[4], (x, sib)).wait()
    for i in range(4):
        a = rqc[(2 * i) * PAD:(2 * i + 1) * PAD, :].astype(F32)
        b = rqc[(2 * i + 1) * PAD:(2 * i + 2) * PAD, :].astype(F32)
        q_pair, c_pair = swap_pack(a, b, left)
        catb[0, 0:PAD, 128 * i:128 * i + 128] = q_pair.astype(BF)
        catb[3, 0:PAD, 128 * i:128 * i + 128] = c_pair.astype(BF)
    att = dot(catb[3, 0:PAD, :], wout[...])
    attb[...] = att[0:TOK].astype(BF)
    outs = [
        pltpu.make_async_copy(attb, att_o.at[0], lsem.at[0]),
        pltpu.make_async_copy(ingb, ing_o.at[0], lsem.at[1]),
        pltpu.make_async_copy(wob.at[:, pl.ds(0, 3 * INNER)], wq_o, lsem.at[2]),
        pltpu.make_async_copy(wob.at[:, pl.ds(3 * INNER, INNER)], wo_o, lsem.at[3]),
    ]
    outs[0].start()

    pltpu.make_async_copy(rows(dkvb, 0), rows(rkv, 0), lsem.at[7]).wait()
    remote(rows(rkv, 0, 15 * PAD), rows(rkv, 0, 15 * PAD), ssem.at[6], rsem.at[6], (x, sib)).wait()
    for i in range(4):
        a = rkv[(4 * i) * PAD:(4 * i + 1) * PAD, :].astype(F32) + rkv[(4 * i + 1) * PAD:(4 * i + 2) * PAD, :].astype(F32)
        b = rkv[(4 * i + 2) * PAD:(4 * i + 3) * PAD, :].astype(F32) + rkv[(4 * i + 3) * PAD:(4 * i + 4) * PAD, :].astype(F32)
        k_pair, v_pair = swap_pack(a, b, left)
        catb[1, 0:PAD, 128 * i:128 * i + 128] = k_pair.astype(BF)
        catb[2, 0:PAD, 128 * i:128 * i + 128] = v_pair.astype(BF)

    cat_to_sib = remote(catb.at[pl.ds(2 - 2 * core, 2), pl.ds(0, PAD)], catb.at[pl.ds(2 - 2 * core, 2), pl.ds(PAD, PAD)],
                        ssem.at[7], rsem.at[7], (x, sib))
    cat_to_sib.start()
    ing = dot_nt(catb[0, 0:PAD, :], wqkv[:, 0:INNER])
    ing += dot_nt(catb[1, 0:PAD, :], wqkv[:, INNER:2 * INNER])
    ing += dot_nt(catb[2, 0:PAD, :], wqkv[:, 2 * INNER:])
    ingb[...] = ing[0:TOK].astype(BF)
    outs[1].start()
    cat_to_sib.wait()

    for half in range(2):
        which = 0 if half == 0 else core
        right = catb[2 * core + half]

        @pl.loop(0, 4)
        def _(i):
            f = dot(alT[which, pl.ds(pl.multiple_of(i * 256, 256), 256), :], right)
            fb[i, :, :, :, INNER * half:INNER * half + INNER] = f.astype(BF).reshape(4, 4, 16, INNER)

    coords = {"x": x, "y": y, "z": z}

    def peer(axis, k):
        c = dict(coords)
        c[axis] = (coords[axis] + k) % 4
        return c[axis], (c["x"], c["y"] * 8 + c["z"] * 2 + core)

    def stage(o, phase, take, recv):
        for k in range(1, 4):
            there, dev = peer(ORDERS[o][phase], k)
            remote(take(there), recv.at[k - 1], fs.at[3 * phase + o], fr.at[3 * phase + o], dev).start()

    def arrived(o, phase, recv):
        remote(recv, recv, fs.at[3 * phase + o], fr.at[3 * phase + o], (x, sib)).wait()

    def total(mine, recv):
        v = mine.astype(F32)
        for k in range(3):
            v += recv[k].astype(F32)
        return v

    def cols(o):
        return pl.ds(*COLS[o])

    takes1 = (
        lambda t: fb.at[t, :, :, :, cols(0)],
        lambda t: fb.at[:, t, :, :, cols(1)],
        lambda t: fb.at[:, :, t, :, cols(2)],
    )
    r1, g1 = (r1a, r1b, r1c), (g1a, g1b, g1c)
    r2, g2 = (r2a, r2b, r2c), (g2a, g2b, g2c)
    r3 = (r3a, r3b, r3c)
    takes2 = (lambda t: g1a.at[t], lambda t: g1b.at[:, t], lambda t: g1c.at[t])
    for o in range(3):
        stage(o, 0, takes1[o], r1[o])
    for o in range(3):
        arrived(o, 0, r1[o])
        mine = coords[ORDERS[o][0]]
        g1[o][...] = total(takes1[o](mine)[...], r1[o]).astype(BF)
        stage(o, 1, takes2[o], r2[o])
    for o in range(3):
        arrived(o, 1, r2[o])
        mine = coords[ORDERS[o][1]]
        g2[o][...] = total(takes2[o](mine)[...], r2[o]).astype(BF)
        stage(o, 2, lambda t, o=o: g2[o].at[t], r3[o])
    for o in range(3):
        arrived(o, 2, r3[o])
        mine = coords[ORDERS[o][2]]
        v = total(g2[o][mine], r3[o])
        a, n = COLS[o]
        fin[core, 0, :, a:a + n] = v[0:8]
        fin[core, 1, :, a:a + n] = v[8:16]

    last = remote(fin.at[core, 1 - core], fin.at[core, 1 - core], ssem.at[8], rsem.at[8], (x, sib))
    last.start()
    last.wait()
    wob[:, 0:D] = fin[0, core]
    wob[:, D:] = fin[1, core]
    outs[2].start()
    outs[3].start()

    remote(rows(dkvb, 0, 15 * PAD), rows(dkvb, 0, 15 * PAD), ssem.at[0], rsem.at[0], (x, sib)).wait_send()
    remote(rows(dkvb, 0, 7 * PAD), rows(dkvb, 0, 7 * PAD), ssem.at[1], rsem.at[1], (x, sib)).wait_send()
    remote(rows(dkvb, 0, 16 * PAD), rows(dkvb, 0, 16 * PAD), ssem.at[5], rsem.at[5], (x, sib)).wait_send()
    for c in outs:
        c.wait()


def hand_out(*refs):
    sems = refs[8]
    copies = [pltpu.make_async_copy(refs[i], refs[4 + i], sems.at[i]) for i in range(4)]
    for c in copies:
        c.start()
    for c in copies:
        c.wait()


def shards(activations, qkv_weight, out_weight, out_grad):
    any_spec = pl.BlockSpec(memory_space=pl.ANY)
    V = pltpu.VMEM
    widths = [c[1] for c in COLS]
    scratch = [
        V((2, 2 * PAD, D), BF),
        V((2, D, 2 * PAD), BF),
        V((D, 3 * INNER), BF),
        V((INNER, D), BF),
        V((8 * PAD, 128), BF),
        V((8 * PAD, 128), BF),
        V((KEYS, 256), BF),
        V((8 * PAD, 128), BF),
        V((8 * PAD, 256), BF),
        V((3 * PAD, KEYS), F32),
        V((3 * PAD, KEYS), BF),
        V((3 * PAD, 128), F32),
        V((3 * PAD, 256), F32),
        V((3 * PAD, 128), F32),
        V((128, 3 * PAD), BF),
        V((128, KEYS), F32),
        V((KEYS, 128), BF),
        V((KEYS, 128), BF),
        V((8 * PAD, 128), BF),
        V((8 * PAD, 128), BF),
        V((16 * PAD, 128), BF),
        V((4, 2 * PAD, INNER), BF),
        V((4, 4, 4, 16, D), BF),
    ]
    scratch += [V((3, 4, 4, 16, w), BF) for w in widths]
    scratch += [V((4, 4, 16, w), BF) for w in widths]
    scratch += [V((3, 4, 16, w), BF) for w in widths]
    scratch += [V((4, 16, w), BF) for w in widths]
    scratch += [V((3, 16, w), BF) for w in widths]
    scratch += [
        V((2, 2, 8, D), F32),
        V((TOK, D), BF),
        V((TOK, D), BF),
        V((8, 2 * D), F32),
        pltpu.SemaphoreType.DMA((8,)),
        pltpu.SemaphoreType.DMA((9,)),
        pltpu.SemaphoreType.DMA((9,)),
        pltpu.SemaphoreType.DMA((9,)),
        pltpu.SemaphoreType.DMA((9,)),
        pltpu.SemaphoreType.DMA((16,)),
        pltpu.SemaphoreType.DMA((3,)),
    ]
    made = pl.pallas_call(
        kernel,
        out_shape=(
            jax.ShapeDtypeStruct((1, TOK, D), BF),
            jax.ShapeDtypeStruct((1, TOK, D), BF),
            jax.ShapeDtypeStruct((8, 3 * INNER), F32),
            jax.ShapeDtypeStruct((8, INNER), F32),
        ),
        in_specs=[any_spec] * 4,
        out_specs=(any_spec,) * 4,
        scratch_shapes=scratch,
        compiler_params=pltpu.CompilerParams(
            collective_id=0, has_side_effects=True, vmem_limit_bytes=56 * 1024 * 1024),
        name="attention_sublayer",
    )(activations, qkv_weight, out_weight, out_grad)
    att, ing, wq, wo = pl.pallas_call(
        hand_out,
        out_shape=tuple(jax.ShapeDtypeStruct(a.shape, a.dtype) for a in made),
        in_specs=[any_spec] * 4,
        out_specs=(any_spec,) * 4,
        scratch_shapes=[pltpu.SemaphoreType.DMA((4,))],
        name="hand_out",
    )(*made)
    return att, ing, wq, wo.T


def solution(mesh):
    return jax.shard_map(
        shards,
        mesh=mesh,
        in_specs=(P("dp", "seq", None), P(), P(), P("dp", "seq", None)),
        out_specs=(
            P("dp", "seq", None),
            P("dp", "seq", None),
            P(("dp", "seq"), None),
            P(None, ("dp", "seq")),
        ),
        check_vma=False,
    )
```

```python
import functools
import math

import jax
import jax.numpy as jnp
import numpy as np
from jax import lax
from jax.experimental import pallas as pl
from jax.experimental.pallas import tpu as pltpu
from jax.sharding import PartitionSpec as P

MESH = pl.DeviceIdType.MESH
BF = jnp.bfloat16
F32 = jnp.float32

HEADS = 8
SEQ = 32
TOK = 136
PAD = 144
KEYS = SEQ * PAD
D = 1024
INNER = 512
SIDES = (1, 2, 3, 4, 5, 8, 9, 10, 14, 16, 20, 24, 32, 40)
ENDS = [int(v) for v in np.cumsum([a * a for a in SIDES])]
STARTS = [0] + ENDS[:-1]
FAR = 1 << 20
BIG = 1e30
ONE = 15
TWO = 16
BATCHES = (
    (0, 3, 4608, 2304, 22, 32),
    (3, 2, 3072, 1536, 14, 22),
    (5, 3, 1920, 1920, 0, 14),
)
ORDERS = ("xyz", "yzx", "zxy")
COLS = ((0, 384), (384, 384), (768, 256))
NT = (((1,), (1,)), ((), ()))


def dot(a, b):
    return jnp.dot(a, b, preferred_element_type=F32)


def dot_nt(a, b):
    return lax.dot_general(a, b, NT, preferred_element_type=F32)


def lane_bounds(rows):
    lane = lax.broadcasted_iota(jnp.int32, (rows, 128), 1)
    lo = jnp.full((rows, 128), -1, jnp.int32)
    hi = jnp.full((rows, 128), -1, jnp.int32)
    for i, (a, b) in enumerate(zip(STARTS, ENDS)):
        lo = jnp.where(lane == i, a, lo)
        hi = jnp.where(lane == i, b, hi)
    lo = jnp.where(lane == 14, FAR, lo)
    hi = jnp.where(lane == 14, FAR + 1, hi)
    ones = (lane == ONE) | (lane == TWO)
    lo = jnp.where(ones, 0, lo)
    hi = jnp.where(ones, ENDS[-1], hi)
    return lo, hi


def swap_pack(a, b, left):
    return (
        jnp.where(left, a, pltpu.roll(b, 64, 1)),
        jnp.where(left, pltpu.roll(a, 64, 1), b),
    )


def kernel(act_h, wqkv_h, wout_h, og_h, att_o, ing_o, wq_o, wo_o,
           al, alT, wqkv, wout, sendkv, sendqg, kvx, qg, qx, sbuf, pbuf, macc, acc, dq,
           qgT, dkT, dkvb, sibr, resb, rqc, rkv, catb, fb,
           r1a, r1b, r1c, g1a, g1b, g1c, r2a, r2b, r2c, g2a, g2b, g2c, r3a, r3b, r3c,
           fin, attb, ingb, wob, lsem, ssem, rsem, fs, fr, ksem, dsem):
    x = lax.axis_index("dp")
    s = lax.axis_index("seq")
    head, quarter = s // 4, s % 4
    pos, core = s // 2, s % 2
    y, z = s // 8, (s // 2) % 4
    sib = s + 1 - 2 * core

    cin = [
        pltpu.make_async_copy(act_h.at[0], al.at[0, pl.ds(0, TOK)], lsem.at[0]),
        pltpu.make_async_copy(wqkv_h, wqkv, lsem.at[1]),
        pltpu.make_async_copy(og_h.at[0], al.at[1, pl.ds(0, TOK)], lsem.at[2]),
        pltpu.make_async_copy(wout_h, wout, lsem.at[3]),
    ]
    for c in cin:
        c.start()

    bar = pltpu.get_barrier_semaphore()

    @pl.loop(1, 16)
    def _(k):
        pl.semaphore_signal(bar, inc=1, device_id=(x, 2 * ((pos + k) % 16) + core), device_id_type=MESH)

    pl.semaphore_signal(bar, inc=1, device_id=(x, sib), device_id_type=MESH)
    for k in range(1, 4):
        pl.semaphore_signal(bar, inc=1, device_id=((x + k) % 4, s), device_id_type=MESH)

    al[0, TOK:PAD, :] = jnp.zeros((PAD - TOK, D), BF)
    al[1, TOK:PAD, :] = jnp.zeros((PAD - TOK, D), BF)
    pl.semaphore_wait(bar, 19)

    def remote(src, dst, send, recv, dev):
        return pltpu.make_async_remote_copy(
            src_ref=src, dst_ref=dst, send_sem=send, recv_sem=recv, device_id=dev, device_id_type=MESH)

    def rows(ref, first, count=PAD):
        return ref.at[pl.ds(pl.multiple_of(first, 16), count)]

    def kvslot(g):
        return kvx.at[pl.ds(pl.multiple_of(g * PAD, 16), PAD), pl.ds(0, 128)]

    left = lax.broadcasted_iota(jnp.int32, (PAD, 128), 1) < 64

    cin[0].wait()
    cin[1].wait()
    kp = dot(al[0, 0:PAD, :], wqkv[:, INNER:2 * INNER])
    vp = dot(al[0, 0:PAD, :], wqkv[:, 2 * INNER:])
    for i in range(4):
        a, b = swap_pack(kp[:, 128 * i:128 * i + 128], vp[:, 128 * i:128 * i + 128], left)
        sendkv[(2 * i) * PAD:(2 * i + 1) * PAD, :] = a.astype(BF)
        sendkv[(2 * i + 1) * PAD:(2 * i + 2) * PAD, :] = b.astype(BF)

    own_kv = pltpu.make_async_copy(rows(sendkv, head * PAD), kvslot(s), lsem.at[4])
    own_kv.start()
    remote(rows(sendkv, head * PAD), kvslot(s), ssem.at[3], rsem.at[3], (x, sib)).start()

    @pl.loop(1, 16)
    def _(k):
        to = (pos + k) % 16
        remote(rows(sendkv, (to // 2) * PAD), kvslot(s), ssem.at[0], ksem.at[pos], (x, 2 * to + core)).start()

    cin[2].wait()
    inputs_to_sib = remote(al.at[:, pl.ds(0, PAD)], al.at[:, pl.ds(PAD, PAD)], ssem.at[2], rsem.at[2], (x, sib))
    inputs_to_sib.start()
    cin[3].wait()
    qp = dot(al[0, 0:PAD, :], wqkv[:, 0:INNER])
    gp = dot_nt(al[1, 0:PAD, :], wout[...])
    for i in range(4):
        a, b = swap_pack(qp[:, 128 * i:128 * i + 128], gp[:, 128 * i:128 * i + 128], left)
        sendqg[(2 * i) * PAD:(2 * i + 1) * PAD, :] = a.astype(BF)
        sendqg[(2 * i + 1) * PAD:(2 * i + 2) * PAD, :] = b.astype(BF)

    slot = 7 - s // 4
    own_qg = pltpu.make_async_copy(rows(sendqg, head * PAD), rows(qg, slot * PAD), lsem.at[5])
    own_qg.start()

    @pl.loop(1, 8)
    def _(k):
        to = (head + k) % 8
        remote(rows(sendqg, to * PAD), rows(qg, slot * PAD), ssem.at[1], rsem.at[1], (x, 4 * to + quarter)).start()

    lo, hi = lane_bounds(PAD)
    place = lax.broadcasted_iota(jnp.int32, (PAD, 128), 0)

    @pl.loop(0, SEQ)
    def _(g):
        t = jnp.where(place < TOK, place + g * TOK, FAR)
        kvx[pl.ds(pl.multiple_of(g * PAD, 16), PAD), 128:256] = jnp.where(
            (t >= lo) & (t < hi), 1.0, 0.0).astype(BF)

    @pl.loop(1, 16)
    def _(k):
        frm = (pos + 16 - k) % 16
        g = 2 * frm + core
        remote(kvslot(g), kvslot(g), ssem.at[0], ksem.at[frm], (x, sib)).wait_recv()
        remote(kvslot(g), kvslot(g), ssem.at[3], rsem.at[3], (x, sib)).start()

    own_kv.wait()
    inputs_to_sib.wait()
    for i in range(2):
        for j in range(8):
            alT[i, 128 * j:128 * j + 128, :] = al[i, :, 128 * j:128 * j + 128].T

    own_qg.wait()
    remote(rows(dkvb, 0, 7 * PAD), rows(dkvb, 0, 7 * PAD), ssem.at[1], rsem.at[1], (x, sib)).wait_recv()

    @pl.loop(0, 8)
    def _(j):
        g = 4 * (7 - j) + quarter
        t = jnp.where(place < TOK, place + g * TOK, ENDS[-1] - 1)
        r = pl.ds(pl.multiple_of(j * PAD, 16), PAD)
        qx[r, 128:256] = jnp.where(lo > t, -BIG, 0.0).astype(BF)
        qx[r, 0:128] = jnp.where(left, qg[r, :].astype(F32) * 0.125, 0.0).astype(BF)

    remote(rows(dkvb, 0, 16 * PAD), rows(dkvb, 0, 16 * PAD), ssem.at[3], rsem.at[3], (x, sib)).wait()

    part = 2 * head + (pos % 2)

    def finish(lo_group, hi_group):
        lo_row, hi_row = lo_group * PAD, hi_group * PAD
        for blk in range(lo_row // 128, -(-hi_row // 128)):
            a, b = max(lo_row - 128 * blk, 0), min(hi_row - 128 * blk, 128)
            v = dkT[:, 128 * blk:128 * blk + 128].T
            dkvb[128 * blk + a:128 * blk + b, :] = v[a:b].astype(BF)

    def to_sibling(number, lo_group, hi_group):
        @pl.loop(lo_group // 2, hi_group // 2)
        def _(k):
            g = 2 * k + 1 - core
            remote(rows(dkvb, g * PAD), rows(sibr, g * PAD), ssem.at[5], dsem.at[number], (x, sib)).start()

    def to_owners(number, lo_group, hi_group):
        n = (hi_group - lo_group) // 2 * PAD
        remote(rows(dkvb, 0, n), rows(sibr, 0, n), ssem.at[5], dsem.at[number], (x, sib)).wait_recv()

        @pl.loop(lo_group // 2, hi_group // 2)
        def _(k):
            g = 2 * k + core
            r = pl.ds(pl.multiple_of(g * PAD, 16), PAD)
            dkvb[r, :] = (dkvb[r, :].astype(F32) + sibr[r, :].astype(F32)).astype(BF)

            @pl.when(k != pos)
            def _():
                remote(rows(dkvb, g * PAD), rows(rkv, part * PAD), ssem.at[6], rsem.at[6], (x, g)).start()

            @pl.when(k == pos)
            def _():
                pltpu.make_async_copy(rows(dkvb, g * PAD), rows(rkv, part * PAD), lsem.at[7]).start()

    for number, (slot0, slots, keys, CHUNK, lo_group, hi_group) in enumerate(BATCHES):
        row0, count = slot0 * PAD, slots * PAD
        rr = slice(row0, row0 + count)
        steps = keys // CHUNK
        macc[0:count, :] = jnp.full((count, 128), -3e38, F32)

        @pl.loop(0, steps)
        def _(c):
            kk = pl.ds(pl.multiple_of(c * CHUNK, 128), CHUNK)
            sc = dot_nt(qx[rr, :], kvx[kk, :])
            sbuf[0:count, kk] = sc
            top = macc[0:count, :]
            for i in range(CHUNK // 128):
                top = jnp.maximum(top, sc[:, 128 * i:128 * i + 128])
            macc[0:count, :] = top

        row_max = jnp.max(macc[0:count, :], axis=1, keepdims=True)
        acc[0:count, :] = jnp.zeros((count, 256), F32)

        @pl.loop(0, steps)
        def _(c):
            kk = pl.ds(pl.multiple_of(c * CHUNK, 128), CHUNK)
            p = jnp.exp(sbuf[0:count, kk] - row_max).astype(BF)
            pbuf[0:count, kk] = p
            acc[0:count, :] += dot(p, kvx[kk, :])

        lane = lax.broadcasted_iota(jnp.int32, (count, 128), 1)
        near = lane < 64
        inv = 1.0 / acc[0:count, 128 + ONE:128 + ONE + 1]
        ctx = (acc[0:count, 0:128] * inv).astype(BF)
        qrow = qg[rr, :].astype(F32)
        dots = jnp.sum(jnp.where(near, 0.0, ctx.astype(F32) * qrow), axis=1, keepdims=True)
        dhi = dots.astype(BF).astype(F32)
        dlo = dots - dhi
        qx[rr, 0:128] = jnp.where(near, 0.0, qrow).astype(BF)
        qx[rr, 128:256] = jnp.where(lane == ONE, -dhi, jnp.where(lane == TWO, -dlo, 0.0)).astype(BF)
        qn = qrow * jnp.where(near, 0.125 * inv, inv)
        qgT[:, 0:count] = qn.T.astype(BF)
        dq[0:count, :] = jnp.zeros((count, 128), F32)

        @pl.loop(0, steps)
        def _(c):
            kk = pl.ds(pl.multiple_of(c * CHUNK, 128), CHUNK)
            p = pbuf[0:count, kk]
            dpd = dot_nt(qx[rr, :], kvx[kk, :])
            ds = (p.astype(F32) * dpd).astype(BF)
            dq[0:count, :] += dot(ds, kvx[kk, 0:128])
            dk = dot(qgT[0:64, 0:count], ds)
            dv = dot(qgT[64:128, 0:count], p)
            if number == 0:
                dkT[0:64, kk] = dk
                dkT[64:128, kk] = dv
            else:
                dkT[0:64, kk] += dk
                dkT[64:128, kk] += dv

        resb[rr, :] = jnp.where(near, dq[0:count, :] * (0.125 * inv), ctx.astype(F32)).astype(BF)

        for j in range(slot0, slot0 + slots):
            to = 7 - j

            @pl.when(head != to)
            def _():
                remote(rows(resb, j * PAD), rows(rqc, head * PAD), ssem.at[4], rsem.at[4],
                       (x, 4 * to + quarter)).start()

            @pl.when(head == to)
            def _():
                pltpu.make_async_copy(rows(resb, j * PAD), rows(rqc, head * PAD), lsem.at[6]).start()

        finish(lo_group, hi_group)
        to_sibling(number, lo_group, hi_group)
        if number > 0:
            to_owners(number - 1, *BATCHES[number - 1][4:])

    to_owners(len(BATCHES) - 1, *BATCHES[-1][4:])

    pltpu.make_async_copy(rows(resb, 0), rows(rqc, 0), lsem.at[6]).wait()
    remote(rows(rqc, 0, 7 * PAD), rows(rqc, 0, 7 * PAD), ssem.at[4], rsem.at[4], (x, sib)).wait()
    for i in range(4):
        a = rqc[(2 * i) * PAD:(2 * i + 1) * PAD, :].astype(F32)
        b = rqc[(2 * i + 1) * PAD:(2 * i + 2) * PAD, :].astype(F32)
        q_pair, c_pair = swap_pack(a, b, left)
        catb[0, 0:PAD, 128 * i:128 * i + 128] = q_pair.astype(BF)
        catb[3, 0:PAD, 128 * i:128 * i + 128] = c_pair.astype(BF)
    att = dot(catb[3, 0:PAD, :], wout[...])
    attb[...] = att[0:TOK].astype(BF)
    outs = [
        pltpu.make_async_copy(attb, att_o.at[0], lsem.at[0]),
        pltpu.make_async_copy(ingb, ing_o.at[0], lsem.at[1]),
        pltpu.make_async_copy(wob.at[:, pl.ds(0, 3 * INNER)], wq_o, lsem.at[2]),
        pltpu.make_async_copy(wob.at[:, pl.ds(3 * INNER, INNER)], wo_o, lsem.at[3]),
    ]
    outs[0].start()

    pltpu.make_async_copy(rows(dkvb, 0), rows(rkv, 0), lsem.at[7]).wait()
    remote(rows(rkv, 0, 15 * PAD), rows(rkv, 0, 15 * PAD), ssem.at[6], rsem.at[6], (x, sib)).wait()
    for i in range(4):
        a = rkv[(4 * i) * PAD:(4 * i + 1) * PAD, :].astype(F32) + rkv[(4 * i + 1) * PAD:(4 * i + 2) * PAD, :].astype(F32)
        b = rkv[(4 * i + 2) * PAD:(4 * i + 3) * PAD, :].astype(F32) + rkv[(4 * i + 3) * PAD:(4 * i + 4) * PAD, :].astype(F32)
        k_pair, v_pair = swap_pack(a, b, left)
        catb[1, 0:PAD, 128 * i:128 * i + 128] = k_pair.astype(BF)
        catb[2, 0:PAD, 128 * i:128 * i + 128] = v_pair.astype(BF)

    cat_to_sib = remote(catb.at[pl.ds(2 - 2 * core, 2), pl.ds(0, PAD)], catb.at[pl.ds(2 - 2 * core, 2), pl.ds(PAD, PAD)],
                        ssem.at[7], rsem.at[7], (x, sib))
    cat_to_sib.start()
    ing = dot_nt(catb[0, 0:PAD, :], wqkv[:, 0:INNER])
    ing += dot_nt(catb[1, 0:PAD, :], wqkv[:, INNER:2 * INNER])
    ing += dot_nt(catb[2, 0:PAD, :], wqkv[:, 2 * INNER:])
    ingb[...] = ing[0:TOK].astype(BF)
    outs[1].start()
    cat_to_sib.wait()

    for half in range(2):
        which = 0 if half == 0 else core
        right = catb[2 * core + half]

        @pl.loop(0, 4)
        def _(i):
            f = dot(alT[which, pl.ds(pl.multiple_of(i * 256, 256), 256), :], right)
            fb[i, :, :, :, INNER * half:INNER * half + INNER] = f.astype(BF).reshape(4, 4, 16, INNER)

    coords = {"x": x, "y": y, "z": z}

    def peer(axis, k):
        c = dict(coords)
        c[axis] = (coords[axis] + k) % 4
        return c[axis], (c["x"], c["y"] * 8 + c["z"] * 2 + core)

    def stage(o, phase, take, recv):
        for k in range(1, 4):
            there, dev = peer(ORDERS[o][phase], k)
            remote(take(there), recv.at[k - 1], fs.at[3 * phase + o], fr.at[3 * phase + o], dev).start()

    def arrived(o, phase, recv):
        remote(recv, recv, fs.at[3 * phase + o], fr.at[3 * phase + o], (x, sib)).wait()

    def total(mine, recv):
        v = mine.astype(F32)
        for k in range(3):
            v += recv[k].astype(F32)
        return v

    def cols(o):
        return pl.ds(*COLS[o])

    takes1 = (
        lambda t: fb.at[t, :, :, :, cols(0)],
        lambda t: fb.at[:, t, :, :, cols(1)],
        lambda t: fb.at[:, :, t, :, cols(2)],
    )
    r1, g1 = (r1a, r1b, r1c), (g1a, g1b, g1c)
    r2, g2 = (r2a, r2b, r2c), (g2a, g2b, g2c)
    r3 = (r3a, r3b, r3c)
    takes2 = (lambda t: g1a.at[t], lambda t: g1b.at[:, t], lambda t: g1c.at[t])
    for o in range(3):
        stage(o, 0, takes1[o], r1[o])
    for o in range(3):
        arrived(o, 0, r1[o])
        mine = coords[ORDERS[o][0]]
        g1[o][...] = total(takes1[o](mine)[...], r1[o]).astype(BF)
        stage(o, 1, takes2[o], r2[o])
    for o in range(3):
        arrived(o, 1, r2[o])
        mine = coords[ORDERS[o][1]]
        g2[o][...] = total(takes2[o](mine)[...], r2[o]).astype(BF)
        stage(o, 2, lambda t, o=o: g2[o].at[t], r3[o])
    for o in range(3):
        arrived(o, 2, r3[o])
        mine = coords[ORDERS[o][2]]
        v = total(g2[o][mine], r3[o])
        a, n = COLS[o]
        fin[core, 0, :, a:a + n] = v[0:8]
        fin[core, 1, :, a:a + n] = v[8:16]

    last = remote(fin.at[core, 1 - core], fin.at[core, 1 - core], ssem.at[8], rsem.at[8], (x, sib))
    last.start()
    last.wait()
    wob[:, 0:D] = fin[0, core]
    wob[:, D:] = fin[1, core]
    outs[2].start()
    outs[3].start()

    remote(rows(dkvb, 0, 15 * PAD), rows(dkvb, 0, 15 * PAD), ssem.at[0], rsem.at[0], (x, sib)).wait_send()
    remote(rows(dkvb, 0, 7 * PAD), rows(dkvb, 0, 7 * PAD), ssem.at[1], rsem.at[1], (x, sib)).wait_send()
    remote(rows(dkvb, 0, 16 * PAD), rows(dkvb, 0, 16 * PAD), ssem.at[5], rsem.at[5], (x, sib)).wait_send()
    for c in outs:
        c.wait()


def hand_out(*refs):
    came, gone, held, sems = refs[0:4], refs[4:8], refs[8:12], refs[12]
    ins = [pltpu.make_async_copy(came[i], held[i], sems.at[i]) for i in range(4)]
    outs = [pltpu.make_async_copy(held[i], gone[i], sems.at[4 + i]) for i in range(4)]
    for c in ins:
        c.start()
    for i in range(4):
        ins[i].wait()
        outs[i].start()
    for c in outs:
        c.wait()


def shards(activations, qkv_weight, out_weight, out_grad):
    any_spec = pl.BlockSpec(memory_space=pl.ANY)
    V = pltpu.VMEM
    widths = [c[1] for c in COLS]
    scratch = [
        V((2, 2 * PAD, D), BF),
        V((2, D, 2 * PAD), BF),
        V((D, 3 * INNER), BF),
        V((INNER, D), BF),
        V((8 * PAD, 128), BF),
        V((8 * PAD, 128), BF),
        V((KEYS, 256), BF),
        V((8 * PAD, 128), BF),
        V((8 * PAD, 256), BF),
        V((3 * PAD, KEYS), F32),
        V((3 * PAD, KEYS), BF),
        V((3 * PAD, 128), F32),
        V((3 * PAD, 256), F32),
        V((3 * PAD, 128), F32),
        V((128, 3 * PAD), BF),
        V((128, KEYS), F32),
        V((KEYS, 128), BF),
        V((KEYS, 128), BF),
        V((8 * PAD, 128), BF),
        V((8 * PAD, 128), BF),
        V((16 * PAD, 128), BF),
        V((4, 2 * PAD, INNER), BF),
        V((4, 4, 4, 16, D), BF),
    ]
    scratch += [V((3, 4, 4, 16, w), BF) for w in widths]
    scratch += [V((4, 4, 16, w), BF) for w in widths]
    scratch += [V((3, 4, 16, w), BF) for w in widths]
    scratch += [V((4, 16, w), BF) for w in widths]
    scratch += [V((3, 16, w), BF) for w in widths]
    scratch += [
        V((2, 2, 8, D), F32),
        V((TOK, D), BF),
        V((TOK, D), BF),
        V((8, 2 * D), F32),
        pltpu.SemaphoreType.DMA((8,)),
        pltpu.SemaphoreType.DMA((9,)),
        pltpu.SemaphoreType.DMA((9,)),
        pltpu.SemaphoreType.DMA((9,)),
        pltpu.SemaphoreType.DMA((9,)),
        pltpu.SemaphoreType.DMA((16,)),
        pltpu.SemaphoreType.DMA((3,)),
    ]
    made = pl.pallas_call(
        kernel,
        out_shape=(
            jax.ShapeDtypeStruct((1, TOK, D), BF),
            jax.ShapeDtypeStruct((1, TOK, D), BF),
            jax.ShapeDtypeStruct((8, 3 * INNER), F32),
            jax.ShapeDtypeStruct((8, INNER), F32),
        ),
        in_specs=[any_spec] * 4,
        out_specs=(any_spec,) * 4,
        scratch_shapes=scratch,
        compiler_params=pltpu.CompilerParams(
            collective_id=0, has_side_effects=True, vmem_limit_bytes=56 * 1024 * 1024),
        name="attention_sublayer",
    )(activations, qkv_weight, out_weight, out_grad)
    att, ing, wq, wo = pl.pallas_call(
        hand_out,
        out_shape=tuple(jax.ShapeDtypeStruct(a.shape, a.dtype) for a in made),
        in_specs=[any_spec] * 4,
        out_specs=(any_spec,) * 4,
        scratch_shapes=[V(a.shape, a.dtype) for a in made] + [pltpu.SemaphoreType.DMA((8,))],
        name="hand_out",
    )(*made)
    return att, ing, wq, wo.T


def solution(mesh):
    return jax.shard_map(
        shards,
        mesh=mesh,
        in_specs=(P("dp", "seq", None), P(), P(), P("dp", "seq", None)),
        out_specs=(
            P("dp", "seq", None),
            P("dp", "seq", None),
            P(("dp", "seq"), None),
            P(None, ("dp", "seq")),
        ),
        check_vma=False,
    )
```

```python
import functools
import math

import jax
import jax.numpy as jnp
import numpy as np
from jax import lax
from jax.experimental import pallas as pl
from jax.experimental.pallas import tpu as pltpu
from jax.sharding import PartitionSpec as P

MESH = pl.DeviceIdType.MESH
BF = jnp.bfloat16
F32 = jnp.float32

HEADS = 8
SEQ = 32
TOK = 136
PAD = 144
KEYS = SEQ * PAD
D = 1024
INNER = 512
SIDES = (1, 2, 3, 4, 5, 8, 9, 10, 14, 16, 20, 24, 32, 40)
ENDS = [int(v) for v in np.cumsum([a * a for a in SIDES])]
STARTS = [0] + ENDS[:-1]
FAR = 1 << 20
BIG = 1e30
ONE = 15
TWO = 16
BATCHES = (
    (0, 3, 4608, 2304, 22, 32),
    (3, 2, 3072, 1536, 14, 22),
    (5, 3, 1920, 1920, 0, 14),
)
NT = (((1,), (1,)), ((), ()))


def dot(a, b):
    return jnp.dot(a, b, preferred_element_type=F32)


def dot_nt(a, b):
    return lax.dot_general(a, b, NT, preferred_element_type=F32)


def lane_bounds(rows):
    lane = lax.broadcasted_iota(jnp.int32, (rows, 128), 1)
    lo = jnp.full((rows, 128), -1, jnp.int32)
    hi = jnp.full((rows, 128), -1, jnp.int32)
    for i, (a, b) in enumerate(zip(STARTS, ENDS)):
        lo = jnp.where(lane == i, a, lo)
        hi = jnp.where(lane == i, b, hi)
    lo = jnp.where(lane == 14, FAR, lo)
    hi = jnp.where(lane == 14, FAR + 1, hi)
    ones = (lane == ONE) | (lane == TWO)
    lo = jnp.where(ones, 0, lo)
    hi = jnp.where(ones, ENDS[-1], hi)
    return lo, hi


def swap_pack(a, b, left):
    return (
        jnp.where(left, a, pltpu.roll(b, 64, 1)),
        jnp.where(left, pltpu.roll(a, 64, 1), b),
    )


def kernel(act_h, wqkv_h, wout_h, og_h, att_o, ing_o, wq_o, wo_o,
           al, alT, wqkv, wout, sendkv, sendqg, kvx, qg, qx, sbuf, pbuf, macc, acc, dq,
           qgT, dkT, dkvb, sibr, resb, rqc, rkv, catp, cgx, fb, fr, fo, fi,
           attb, ingb, wob, lsem, ssem, rsem, ksem, dsem, xsem):
    x = lax.axis_index("dp")
    s = lax.axis_index("seq")
    head, quarter = s // 4, s % 4
    pos, core = s // 2, s % 2
    sib = s + 1 - 2 * core
    spot = 2 * x + core

    cin = [
        pltpu.make_async_copy(act_h.at[0], al.at[0, spot, pl.ds(0, TOK)], lsem.at[0]),
        pltpu.make_async_copy(wqkv_h, wqkv, lsem.at[1]),
        pltpu.make_async_copy(og_h.at[0], al.at[1, spot, pl.ds(0, TOK)], lsem.at[2]),
        pltpu.make_async_copy(wout_h, wout, lsem.at[3]),
    ]
    for c in cin:
        c.start()

    bar = pltpu.get_barrier_semaphore()

    @pl.loop(1, 16)
    def _(k):
        pl.semaphore_signal(bar, inc=1, device_id=(x, 2 * ((pos + k) % 16) + core), device_id_type=MESH)

    def at_spot(q):
        return (q // 2, 2 * pos + q % 2)

    @pl.loop(1, 8)
    def _(k):
        pl.semaphore_signal(bar, inc=1, device_id=at_spot((spot + k) % 8), device_id_type=MESH)

    for i in range(2):
        al[i, spot, TOK:PAD, :] = jnp.zeros((PAD - TOK, D), BF)

    def remote(src, dst, send, recv, dev):
        return pltpu.make_async_remote_copy(
            src_ref=src, dst_ref=dst, send_sem=send, recv_sem=recv, device_id=dev, device_id_type=MESH)

    def rows(ref, first, count=PAD):
        return ref.at[pl.ds(pl.multiple_of(first, 16), count)]

    def kvslot(g):
        return kvx.at[pl.ds(pl.multiple_of(g * PAD, 16), PAD), pl.ds(0, 128)]

    left = lax.broadcasted_iota(jnp.int32, (PAD, 128), 1) < 64

    cin[0].wait()
    cin[1].wait()
    kp = dot(al[0, spot], wqkv[:, INNER:2 * INNER])
    vp = dot(al[0, spot], wqkv[:, 2 * INNER:])
    for i in range(4):
        a, b = swap_pack(kp[:, 128 * i:128 * i + 128], vp[:, 128 * i:128 * i + 128], left)
        sendkv[(2 * i) * PAD:(2 * i + 1) * PAD, :] = a.astype(BF)
        sendkv[(2 * i + 1) * PAD:(2 * i + 2) * PAD, :] = b.astype(BF)

    pl.semaphore_wait(bar, 22)
    own_kv = pltpu.make_async_copy(rows(sendkv, head * PAD), kvslot(s), lsem.at[4])
    own_kv.start()
    remote(rows(sendkv, head * PAD), kvslot(s), ssem.at[3], rsem.at[3], (x, sib)).start()

    @pl.loop(1, 16)
    def _(k):
        to = (pos + k) % 16
        remote(rows(sendkv, (to // 2) * PAD), kvslot(s), ssem.at[0], ksem.at[pos], (x, 2 * to + core)).start()

    cin[2].wait()
    cin[3].wait()
    qp = dot(al[0, spot], wqkv[:, 0:INNER])
    gp = dot_nt(al[1, spot], wout[...])
    for i in range(4):
        a, b = swap_pack(qp[:, 128 * i:128 * i + 128], gp[:, 128 * i:128 * i + 128], left)
        sendqg[(2 * i) * PAD:(2 * i + 1) * PAD, :] = a.astype(BF)
        sendqg[(2 * i + 1) * PAD:(2 * i + 2) * PAD, :] = b.astype(BF)

    @pl.loop(1, 4)
    def _(k):
        remote(al.at[:, spot], al.at[:, spot], ssem.at[2], xsem.at[x], ((x + k) % 4, s)).start()

    remote(al.at[:, spot], al.at[:, spot], ssem.at[7], rsem.at[7], (x, sib)).start()

    slot = 7 - s // 4
    own_qg = pltpu.make_async_copy(rows(sendqg, head * PAD), rows(qg, slot * PAD), lsem.at[5])
    own_qg.start()

    @pl.loop(1, 8)
    def _(k):
        to = (head + k) % 8
        remote(rows(sendqg, to * PAD), rows(qg, slot * PAD), ssem.at[1], rsem.at[1], (x, 4 * to + quarter)).start()

    lo, hi = lane_bounds(PAD)
    place = lax.broadcasted_iota(jnp.int32, (PAD, 128), 0)

    @pl.loop(0, SEQ)
    def _(g):
        t = jnp.where(place < TOK, place + g * TOK, FAR)
        kvx[pl.ds(pl.multiple_of(g * PAD, 16), PAD), 128:256] = jnp.where(
            (t >= lo) & (t < hi), 1.0, 0.0).astype(BF)

    @pl.loop(1, 16)
    def _(k):
        frm = (pos + 16 - k) % 16
        g = 2 * frm + core
        remote(kvslot(g), kvslot(g), ssem.at[0], ksem.at[frm], (x, sib)).wait_recv()
        remote(kvslot(g), kvslot(g), ssem.at[3], rsem.at[3], (x, sib)).start()

    own_kv.wait()
    own_qg.wait()
    remote(rows(dkvb, 0, 7 * PAD), rows(dkvb, 0, 7 * PAD), ssem.at[1], rsem.at[1], (x, sib)).wait_recv()

    @pl.loop(0, 8)
    def _(j):
        g = 4 * (7 - j) + quarter
        t = jnp.where(place < TOK, place + g * TOK, ENDS[-1] - 1)
        r = pl.ds(pl.multiple_of(j * PAD, 16), PAD)
        qx[r, 128:256] = jnp.where(lo > t, -BIG, 0.0).astype(BF)
        qx[r, 0:128] = jnp.where(left, qg[r, :].astype(F32) * 0.125, 0.0).astype(BF)

    remote(rows(dkvb, 0, 16 * PAD), rows(dkvb, 0, 16 * PAD), ssem.at[3], rsem.at[3], (x, sib)).wait()

    part = 2 * head + (pos % 2)

    def finish(lo_group, hi_group):
        lo_row, hi_row = lo_group * PAD, hi_group * PAD
        for blk in range(lo_row // 128, -(-hi_row // 128)):
            a, b = max(lo_row - 128 * blk, 0), min(hi_row - 128 * blk, 128)
            v = dkT[:, 128 * blk:128 * blk + 128].T
            dkvb[128 * blk + a:128 * blk + b, :] = v[a:b].astype(BF)

    def to_sibling(number, lo_group, hi_group):
        @pl.loop(lo_group // 2, hi_group // 2)
        def _(k):
            g = 2 * k + 1 - core
            remote(rows(dkvb, g * PAD), rows(sibr, g * PAD), ssem.at[5], dsem.at[number], (x, sib)).start()

    def to_owners(number, lo_group, hi_group):
        n = (hi_group - lo_group) // 2 * PAD
        remote(rows(dkvb, 0, n), rows(sibr, 0, n), ssem.at[5], dsem.at[number], (x, sib)).wait_recv()

        @pl.loop(lo_group // 2, hi_group // 2)
        def _(k):
            g = 2 * k + core
            r = pl.ds(pl.multiple_of(g * PAD, 16), PAD)
            dkvb[r, :] = (dkvb[r, :].astype(F32) + sibr[r, :].astype(F32)).astype(BF)

            @pl.when(k != pos)
            def _():
                remote(rows(dkvb, g * PAD), rows(rkv, part * PAD), ssem.at[6], rsem.at[6], (x, g)).start()

            @pl.when(k == pos)
            def _():
                pltpu.make_async_copy(rows(dkvb, g * PAD), rows(rkv, part * PAD), lsem.at[7]).start()

    for number, (slot0, slots, keys, CHUNK, lo_group, hi_group) in enumerate(BATCHES):
        row0, count = slot0 * PAD, slots * PAD
        rr = slice(row0, row0 + count)
        steps = keys // CHUNK
        macc[0:count, :] = jnp.full((count, 128), -3e38, F32)

        @pl.loop(0, steps)
        def _(c):
            kk = pl.ds(pl.multiple_of(c * CHUNK, 128), CHUNK)
            sc = dot_nt(qx[rr, :], kvx[kk, :])
            sbuf[0:count, kk] = sc
            top = macc[0:count, :]
            for i in range(CHUNK // 128):
                top = jnp.maximum(top, sc[:, 128 * i:128 * i + 128])
            macc[0:count, :] = top

        if number > 0:
            to_owners(number - 1, *BATCHES[number - 1][4:])
        row_max = jnp.max(macc[0:count, :], axis=1, keepdims=True)
        acc[0:count, :] = jnp.zeros((count, 256), F32)

        @pl.loop(0, steps)
        def _(c):
            kk = pl.ds(pl.multiple_of(c * CHUNK, 128), CHUNK)
            p = jnp.exp(sbuf[0:count, kk] - row_max).astype(BF)
            pbuf[0:count, kk] = p
            acc[0:count, :] += dot(p, kvx[kk, :])

        lane = lax.broadcasted_iota(jnp.int32, (count, 128), 1)
        near = lane < 64
        inv = 1.0 / acc[0:count, 128 + ONE:128 + ONE + 1]
        ctx = (acc[0:count, 0:128] * inv).astype(BF)
        qrow = qg[rr, :].astype(F32)
        dots = jnp.sum(jnp.where(near, 0.0, ctx.astype(F32) * qrow), axis=1, keepdims=True)
        dhi = dots.astype(BF).astype(F32)
        dlo = dots - dhi
        qx[rr, 0:128] = jnp.where(near, 0.0, qrow).astype(BF)
        qx[rr, 128:256] = jnp.where(lane == ONE, -dhi, jnp.where(lane == TWO, -dlo, 0.0)).astype(BF)
        qn = qrow * jnp.where(near, 0.125 * inv, inv)
        qgT[:, 0:count] = qn.T.astype(BF)
        dq[0:count, :] = jnp.zeros((count, 128), F32)

        @pl.loop(0, steps)
        def _(c):
            kk = pl.ds(pl.multiple_of(c * CHUNK, 128), CHUNK)
            p = pbuf[0:count, kk]
            dpd = dot_nt(qx[rr, :], kvx[kk, :])
            ds = (p.astype(F32) * dpd).astype(BF)
            dq[0:count, :] += dot(ds, kvx[kk, 0:128])
            dk = dot(qgT[0:64, 0:count], ds)
            dv = dot(qgT[64:128, 0:count], p)
            if number == 0:
                dkT[0:64, kk] = dk
                dkT[64:128, kk] = dv
            else:
                dkT[0:64, kk] += dk
                dkT[64:128, kk] += dv

        resb[rr, :] = jnp.where(near, dq[0:count, :] * (0.125 * inv), ctx.astype(F32)).astype(BF)

        for j in range(slot0, slot0 + slots):
            to = 7 - j

            @pl.when(head != to)
            def _():
                remote(rows(resb, j * PAD), rows(rqc, head * PAD), ssem.at[4], rsem.at[4],
                       (x, 4 * to + quarter)).start()

            @pl.when(head == to)
            def _():
                pltpu.make_async_copy(rows(resb, j * PAD), rows(rqc, head * PAD), lsem.at[6]).start()

        finish(lo_group, hi_group)
        to_sibling(number, lo_group, hi_group)
        if number == 1:
            @pl.loop(1, 4)
            def _(k):
                frm = (x + k) % 4
                q = 2 * frm + core
                remote(al.at[:, q], al.at[:, q], ssem.at[2], xsem.at[frm], (x, sib)).wait_recv()
                remote(al.at[:, q], al.at[:, q], ssem.at[7], rsem.at[7], (x, sib)).start()

    remote(al.at[:, pl.ds(0, 4)], al.at[:, pl.ds(0, 4)], ssem.at[7], rsem.at[7], (x, sib)).wait()

    def transpose_inputs(i):
        for j in range(8):
            alT[i, 128 * j:128 * j + 128, :] = al[i, :, :, 128 * j:128 * j + 128].reshape(8 * PAD, 128).T

    transpose_inputs(0)

    @pl.when(core == 1)
    def _():
        transpose_inputs(1)

    to_owners(len(BATCHES) - 1, *BATCHES[-1][4:])

    pltpu.make_async_copy(rows(resb, 0), rows(rqc, 0), lsem.at[6]).wait()
    remote(rows(rqc, 0, 7 * PAD), rows(rqc, 0, 7 * PAD), ssem.at[4], rsem.at[4], (x, sib)).wait()
    for i in range(4):
        a = rqc[(2 * i) * PAD:(2 * i + 1) * PAD, :].astype(F32)
        b = rqc[(2 * i + 1) * PAD:(2 * i + 2) * PAD, :].astype(F32)
        q_pair, c_pair = swap_pack(a, b, left)
        catp[0, i] = q_pair.astype(BF)
        catp[3, i] = c_pair.astype(BF)

    def wide(i):
        return jnp.concatenate([catp[i, j] for j in range(4)], axis=1)

    def exchange(u, blocks):
        own = pltpu.make_async_copy(catp.at[blocks[0] + (blocks[1] - blocks[0]) * core, x], cgx.at[u, spot], lsem.at[4 + u])
        own.start()

        @pl.loop(1, 8)
        def _(k):
            q = (spot + k) % 8
            block = blocks[0] + (blocks[1] - blocks[0]) * (q % 2)
            remote(catp.at[block, q // 2], cgx.at[u, spot], ssem.at[8 + u], rsem.at[8 + u], at_spot(q)).start()

        return own

    def partial_sums(u, own, lhs):
        own.wait()
        seven = cgx.at[u, pl.ds(0, 7)]
        remote(seven, seven, ssem.at[8 + u], rsem.at[8 + u], (x, sib)).wait()
        right = cgx[u].reshape(8 * PAD, 128)
        for i in range(4):
            f = dot(alT[lhs, 256 * i:256 * i + 256, :], right)
            fb[u, :, i] = f.astype(BF).reshape(16, 16, 128)

        @pl.loop(1, 16)
        def _(k):
            to = (pos + k) % 16
            remote(fb.at[u, to], fr.at[u, k - 1], ssem.at[10 + u], rsem.at[10 + u], (x, 2 * to + core)).start()

    def sums(u):
        remote(fr.at[u], fr.at[u], ssem.at[10 + u], rsem.at[10 + u], (x, sib)).wait()
        v = fb[u, pos].astype(F32)
        for k in range(15):
            v += fr[u, k].astype(F32)
        for i in range(4):
            for c in range(2):
                fo[2 * i + c, u] = v[i, 8 * c:8 * c + 8]

    early = exchange(0, (0, 3))
    att = dot(wide(3), wout[...])
    attb[...] = att[0:TOK].astype(BF)
    outs = [
        pltpu.make_async_copy(attb, att_o.at[0], lsem.at[0]),
        pltpu.make_async_copy(ingb, ing_o.at[0], lsem.at[1]),
        pltpu.make_async_copy(wob.at[:, pl.ds(0, 3 * INNER)], wq_o, lsem.at[2]),
        pltpu.make_async_copy(wob.at[:, pl.ds(3 * INNER, INNER)], wo_o, lsem.at[3]),
    ]
    outs[0].start()
    partial_sums(0, early, core)

    pltpu.make_async_copy(rows(dkvb, 0), rows(rkv, 0), lsem.at[7]).wait()
    remote(rows(rkv, 0, 15 * PAD), rows(rkv, 0, 15 * PAD), ssem.at[6], rsem.at[6], (x, sib)).wait()
    for i in range(4):
        a = rkv[(4 * i) * PAD:(4 * i + 1) * PAD, :].astype(F32) + rkv[(4 * i + 1) * PAD:(4 * i + 2) * PAD, :].astype(F32)
        b = rkv[(4 * i + 2) * PAD:(4 * i + 3) * PAD, :].astype(F32) + rkv[(4 * i + 3) * PAD:(4 * i + 4) * PAD, :].astype(F32)
        k_pair, v_pair = swap_pack(a, b, left)
        catp[1, i] = k_pair.astype(BF)
        catp[2, i] = v_pair.astype(BF)

    late = exchange(1, (1, 2))
    ing = dot_nt(wide(0), wqkv[:, 0:INNER])
    ing += dot_nt(wide(1), wqkv[:, INNER:2 * INNER])
    ing += dot_nt(wide(2), wqkv[:, 2 * INNER:])
    ingb[...] = ing[0:TOK].astype(BF)
    outs[1].start()
    partial_sums(1, late, 0)
    sums(0)
    sums(1)

    fi[spot] = fo[spot]

    @pl.loop(1, 8)
    def _(k):
        q = (spot + k) % 8
        remote(fo.at[q], fi.at[spot], ssem.at[12], rsem.at[12], at_spot(q)).start()

    remote(fi.at[pl.ds(0, 7)], fi.at[pl.ds(0, 7)], ssem.at[12], rsem.at[12], (x, sib)).wait()
    for i in range(4):
        for block, (c, u) in enumerate(((0, 0), (0, 1), (1, 1), (1, 0))):
            wob[:, INNER * block + 128 * i:INNER * block + 128 * i + 128] = fi[2 * i + c, u]
    outs[2].start()
    outs[3].start()

    remote(rows(dkvb, 0, 15 * PAD), rows(dkvb, 0, 15 * PAD), ssem.at[0], rsem.at[0], (x, sib)).wait_send()
    remote(rows(dkvb, 0, 7 * PAD), rows(dkvb, 0, 7 * PAD), ssem.at[1], rsem.at[1], (x, sib)).wait_send()
    remote(rows(dkvb, 0, 16 * PAD), rows(dkvb, 0, 16 * PAD), ssem.at[5], rsem.at[5], (x, sib)).wait_send()
    remote(al.at[:, pl.ds(0, 3)], al.at[:, pl.ds(0, 3)], ssem.at[2], rsem.at[2], (x, sib)).wait_send()
    for c in outs:
        c.wait()


def hand_out(*refs):
    came, gone, held, sems = refs[0:4], refs[4:8], refs[8:12], refs[12]
    ins = [pltpu.make_async_copy(came[i], held[i], sems.at[i]) for i in range(4)]
    outs = [pltpu.make_async_copy(held[i], gone[i], sems.at[4 + i]) for i in range(4)]
    for c in ins:
        c.start()
    for i in range(4):
        ins[i].wait()
        outs[i].start()
    for c in outs:
        c.wait()


def shards(activations, qkv_weight, out_weight, out_grad):
    any_spec = pl.BlockSpec(memory_space=pl.ANY)
    V = pltpu.VMEM
    scratch = [
        V((2, 8, PAD, D), BF),
        V((2, D, 8 * PAD), BF),
        V((D, 3 * INNER), BF),
        V((INNER, D), BF),
        V((8 * PAD, 128), BF),
        V((8 * PAD, 128), BF),
        V((KEYS, 256), BF),
        V((8 * PAD, 128), BF),
        V((8 * PAD, 256), BF),
        V((3 * PAD, KEYS), F32),
        V((3 * PAD, KEYS), BF),
        V((3 * PAD, 128), F32),
        V((3 * PAD, 256), F32),
        V((3 * PAD, 128), F32),
        V((128, 3 * PAD), BF),
        V((128, KEYS), F32),
        V((KEYS, 128), BF),
        V((KEYS, 128), BF),
        V((8 * PAD, 128), BF),
        V((8 * PAD, 128), BF),
        V((16 * PAD, 128), BF),
        V((4, 4, PAD, 128), BF),
        V((2, 8, PAD, 128), BF),
        V((2, 16, 4, 16, 128), BF),
        V((2, 15, 4, 16, 128), BF),
        V((8, 2, 8, 128), F32),
        V((8, 2, 8, 128), F32),
        V((TOK, D), BF),
        V((TOK, D), BF),
        V((8, 2 * D), F32),
        pltpu.SemaphoreType.DMA((8,)),
        pltpu.SemaphoreType.DMA((13,)),
        pltpu.SemaphoreType.DMA((13,)),
        pltpu.SemaphoreType.DMA((16,)),
        pltpu.SemaphoreType.DMA((3,)),
        pltpu.SemaphoreType.DMA((4,)),
    ]
    made = pl.pallas_call(
        kernel,
        out_shape=(
            jax.ShapeDtypeStruct((1, TOK, D), BF),
            jax.ShapeDtypeStruct((1, TOK, D), BF),
            jax.ShapeDtypeStruct((8, 3 * INNER), F32),
            jax.ShapeDtypeStruct((8, INNER), F32),
        ),
        in_specs=[any_spec] * 4,
        out_specs=(any_spec,) * 4,
        scratch_shapes=scratch,
        compiler_params=pltpu.CompilerParams(
            collective_id=0, has_side_effects=True, vmem_limit_bytes=56 * 1024 * 1024),
        name="attention_sublayer",
    )(activations, qkv_weight, out_weight, out_grad)
    att, ing, wq, wo = pl.pallas_call(
        hand_out,
        out_shape=tuple(jax.ShapeDtypeStruct(a.shape, a.dtype) for a in made),
        in_specs=[any_spec] * 4,
        out_specs=(any_spec,) * 4,
        scratch_shapes=[V(a.shape, a.dtype) for a in made] + [pltpu.SemaphoreType.DMA((8,))],
        name="hand_out",
    )(*made)
    return att, ing, wq, wo.T


def solution(mesh):
    return jax.shard_map(
        shards,
        mesh=mesh,
        in_specs=(P("dp", "seq", None), P(), P(), P("dp", "seq", None)),
        out_specs=(
            P("dp", "seq", None),
            P("dp", "seq", None),
            P(("dp", "seq"), None),
            P(None, ("dp", "seq")),
        ),
        check_vma=False,
    )
```

```python
import functools
import math

import jax
import jax.numpy as jnp
import numpy as np
from jax import lax
from jax.experimental import pallas as pl
from jax.experimental.pallas import tpu as pltpu
from jax.sharding import PartitionSpec as P

MESH = pl.DeviceIdType.MESH
BF = jnp.bfloat16
F32 = jnp.float32

HEADS = 8
SEQ = 32
TOK = 136
PAD = 144
KEYS = SEQ * PAD
D = 1024
INNER = 512
SIDES = (1, 2, 3, 4, 5, 8, 9, 10, 14, 16, 20, 24, 32, 40)
ENDS = [int(v) for v in np.cumsum([a * a for a in SIDES])]
STARTS = [0] + ENDS[:-1]
FAR = 1 << 20
BIG = 1e30
ONE = 15
TWO = 16
BATCHES = (
    (0, 3, 4608, 2304, 22, 32),
    (3, 2, 3072, 1536, 14, 22),
    (5, 3, 1920, 1920, 0, 14),
)
NT = (((1,), (1,)), ((), ()))


def dot(a, b):
    return jnp.dot(a, b, preferred_element_type=F32)


def dot_nt(a, b):
    return lax.dot_general(a, b, NT, preferred_element_type=F32)


def lane_bounds(rows):
    lane = lax.broadcasted_iota(jnp.int32, (rows, 128), 1)
    lo = jnp.full((rows, 128), -1, jnp.int32)
    hi = jnp.full((rows, 128), -1, jnp.int32)
    for i, (a, b) in enumerate(zip(STARTS, ENDS)):
        lo = jnp.where(lane == i, a, lo)
        hi = jnp.where(lane == i, b, hi)
    lo = jnp.where(lane == 14, FAR, lo)
    hi = jnp.where(lane == 14, FAR + 1, hi)
    ones = (lane == ONE) | (lane == TWO)
    lo = jnp.where(ones, 0, lo)
    hi = jnp.where(ones, ENDS[-1], hi)
    return lo, hi


def swap_pack(a, b, left):
    return (
        jnp.where(left, a, pltpu.roll(b, 64, 1)),
        jnp.where(left, pltpu.roll(a, 64, 1), b),
    )


def kernel(act_h, wqkv_h, wout_h, og_h, att_o, ing_o, wq_o, wo_o,
           al, alT, wqkv, wout, sendkv, sendqg, kvx, qg, qx, sbuf, pbuf, macc, acc, dq,
           qgT, dkT, dkvb, sibr, resb, rqc, rkv, catp, cgx, fb, fr, fo, fi,
           attb, ingb, wob, lsem, ssem, rsem, ksem, dsem, xsem):
    x = lax.axis_index("dp")
    s = lax.axis_index("seq")
    head, quarter = s // 4, s % 4
    pos, core = s // 2, s % 2
    sib = s + 1 - 2 * core
    spot = 2 * x + core

    cin = [
        pltpu.make_async_copy(act_h.at[0], al.at[0, spot, pl.ds(0, TOK)], lsem.at[0]),
        pltpu.make_async_copy(wqkv_h, wqkv, lsem.at[1]),
        pltpu.make_async_copy(og_h.at[0], al.at[1, spot, pl.ds(0, TOK)], lsem.at[2]),
        pltpu.make_async_copy(wout_h, wout, lsem.at[3]),
    ]
    for c in cin:
        c.start()

    bar = pltpu.get_barrier_semaphore()

    @pl.loop(1, 16)
    def _(k):
        pl.semaphore_signal(bar, inc=1, device_id=(x, 2 * ((pos + k) % 16) + core), device_id_type=MESH)

    def at_spot(q):
        return (q // 2, 2 * pos + q % 2)

    @pl.loop(1, 8)
    def _(k):
        pl.semaphore_signal(bar, inc=1, device_id=at_spot((spot + k) % 8), device_id_type=MESH)

    for i in range(2):
        al[i, spot, TOK:PAD, :] = jnp.zeros((PAD - TOK, D), BF)

    def remote(src, dst, send, recv, dev):
        return pltpu.make_async_remote_copy(
            src_ref=src, dst_ref=dst, send_sem=send, recv_sem=recv, device_id=dev, device_id_type=MESH)

    def rows(ref, first, count=PAD):
        return ref.at[pl.ds(pl.multiple_of(first, 16), count)]

    def kvslot(g):
        return kvx.at[pl.ds(pl.multiple_of(g * PAD, 16), PAD), pl.ds(0, 128)]

    left = lax.broadcasted_iota(jnp.int32, (PAD, 128), 1) < 64

    cin[0].wait()
    cin[1].wait()
    kp = dot(al[0, spot], wqkv[:, INNER:2 * INNER])
    vp = dot(al[0, spot], wqkv[:, 2 * INNER:])
    for i in range(4):
        a, b = swap_pack(kp[:, 128 * i:128 * i + 128], vp[:, 128 * i:128 * i + 128], left)
        sendkv[(2 * i) * PAD:(2 * i + 1) * PAD, :] = a.astype(BF)
        sendkv[(2 * i + 1) * PAD:(2 * i + 2) * PAD, :] = b.astype(BF)

    cin[2].wait()
    cin[3].wait()
    qp = dot(al[0, spot], wqkv[:, 0:INNER])
    gp = dot_nt(al[1, spot], wout[...])
    for i in range(4):
        a, b = swap_pack(qp[:, 128 * i:128 * i + 128], gp[:, 128 * i:128 * i + 128], left)
        sendqg[(2 * i) * PAD:(2 * i + 1) * PAD, :] = a.astype(BF)
        sendqg[(2 * i + 1) * PAD:(2 * i + 2) * PAD, :] = b.astype(BF)

    lo, hi = lane_bounds(PAD)
    place = lax.broadcasted_iota(jnp.int32, (PAD, 128), 0)

    @pl.loop(0, SEQ)
    def _(g):
        t = jnp.where(place < TOK, place + g * TOK, FAR)
        kvx[pl.ds(pl.multiple_of(g * PAD, 16), PAD), 128:256] = jnp.where(
            (t >= lo) & (t < hi), 1.0, 0.0).astype(BF)

    pl.semaphore_wait(bar, 22)
    own_kv = pltpu.make_async_copy(rows(sendkv, head * PAD), kvslot(s), lsem.at[4])
    own_kv.start()
    remote(rows(sendkv, head * PAD), kvslot(s), ssem.at[3], rsem.at[3], (x, sib)).start()

    @pl.loop(1, 16)
    def _(k):
        to = (pos + k) % 16
        remote(rows(sendkv, (to // 2) * PAD), kvslot(s), ssem.at[0], ksem.at[pos], (x, 2 * to + core)).start()

    @pl.loop(1, 4)
    def _(k):
        remote(al.at[:, spot], al.at[:, spot], ssem.at[2], xsem.at[x], ((x + k) % 4, s)).start()

    remote(al.at[:, spot], al.at[:, spot], ssem.at[7], rsem.at[7], (x, sib)).start()

    slot = 7 - s // 4
    own_qg = pltpu.make_async_copy(rows(sendqg, head * PAD), rows(qg, slot * PAD), lsem.at[5])
    own_qg.start()

    @pl.loop(1, 8)
    def _(k):
        to = (head + k) % 8
        remote(rows(sendqg, to * PAD), rows(qg, slot * PAD), ssem.at[1], rsem.at[1], (x, 4 * to + quarter)).start()

    @pl.loop(1, 16)
    def _(k):
        frm = (pos + 16 - k) % 16
        g = 2 * frm + core
        remote(kvslot(g), kvslot(g), ssem.at[0], ksem.at[frm], (x, sib)).wait_recv()
        remote(kvslot(g), kvslot(g), ssem.at[3], rsem.at[3], (x, sib)).start()

    own_kv.wait()
    own_qg.wait()
    remote(rows(dkvb, 0, 7 * PAD), rows(dkvb, 0, 7 * PAD), ssem.at[1], rsem.at[1], (x, sib)).wait_recv()

    @pl.loop(0, 8)
    def _(j):
        g = 4 * (7 - j) + quarter
        t = jnp.where(place < TOK, place + g * TOK, ENDS[-1] - 1)
        r = pl.ds(pl.multiple_of(j * PAD, 16), PAD)
        qx[r, 128:256] = jnp.where(lo > t, -BIG, 0.0).astype(BF)
        qx[r, 0:128] = jnp.where(left, qg[r, :].astype(F32) * 0.125, 0.0).astype(BF)

    remote(rows(dkvb, 0, 16 * PAD), rows(dkvb, 0, 16 * PAD), ssem.at[3], rsem.at[3], (x, sib)).wait()

    part = 2 * head + (pos % 2)

    def finish(lo_group, hi_group):
        lo_row, hi_row = lo_group * PAD, hi_group * PAD
        for blk in range(lo_row // 128, -(-hi_row // 128)):
            a, b = max(lo_row - 128 * blk, 0), min(hi_row - 128 * blk, 128)
            v = dkT[:, 128 * blk:128 * blk + 128].T
            dkvb[128 * blk + a:128 * blk + b, :] = v[a:b].astype(BF)

    def to_sibling(number, lo_group, hi_group):
        @pl.loop(lo_group // 2, hi_group // 2)
        def _(k):
            g = 2 * k + 1 - core
            remote(rows(dkvb, g * PAD), rows(sibr, g * PAD), ssem.at[5], dsem.at[number], (x, sib)).start()

    def to_owners(number, lo_group, hi_group):
        n = (hi_group - lo_group) // 2 * PAD
        remote(rows(dkvb, 0, n), rows(sibr, 0, n), ssem.at[5], dsem.at[number], (x, sib)).wait_recv()

        @pl.loop(lo_group // 2, hi_group // 2)
        def _(k):
            g = 2 * k + core
            r = pl.ds(pl.multiple_of(g * PAD, 16), PAD)
            dkvb[r, :] = (dkvb[r, :].astype(F32) + sibr[r, :].astype(F32)).astype(BF)

            @pl.when(k != pos)
            def _():
                remote(rows(dkvb, g * PAD), rows(rkv, part * PAD), ssem.at[6], rsem.at[6], (x, g)).start()

            @pl.when(k == pos)
            def _():
                pltpu.make_async_copy(rows(dkvb, g * PAD), rows(rkv, part * PAD), lsem.at[7]).start()

    for number, (slot0, slots, keys, CHUNK, lo_group, hi_group) in enumerate(BATCHES):
        row0, count = slot0 * PAD, slots * PAD
        rr = slice(row0, row0 + count)
        steps = keys // CHUNK
        macc[0:count, :] = jnp.full((count, 128), -3e38, F32)

        @pl.loop(0, steps)
        def _(c):
            kk = pl.ds(pl.multiple_of(c * CHUNK, 128), CHUNK)
            sc = dot_nt(qx[rr, :], kvx[kk, :])
            sbuf[0:count, kk] = sc
            top = macc[0:count, :]
            for i in range(CHUNK // 128):
                top = jnp.maximum(top, sc[:, 128 * i:128 * i + 128])
            macc[0:count, :] = top

        if number > 0:
            to_owners(number - 1, *BATCHES[number - 1][4:])
        row_max = jnp.max(macc[0:count, :], axis=1, keepdims=True)
        acc[0:count, :] = jnp.zeros((count, 256), F32)

        @pl.loop(0, steps)
        def _(c):
            kk = pl.ds(pl.multiple_of(c * CHUNK, 128), CHUNK)
            p = jnp.exp(sbuf[0:count, kk] - row_max).astype(BF)
            pbuf[0:count, kk] = p
            acc[0:count, :] += dot(p, kvx[kk, :])

        if number == 2:
            @pl.loop(1, 4)
            def _(k):
                frm = (x + k) % 4
                q = 2 * frm + core
                remote(al.at[:, q], al.at[:, q], ssem.at[2], xsem.at[frm], (x, sib)).wait_recv()
                remote(al.at[:, q], al.at[:, q], ssem.at[7], rsem.at[7], (x, sib)).start()

        lane = lax.broadcasted_iota(jnp.int32, (count, 128), 1)
        near = lane < 64
        inv = 1.0 / acc[0:count, 128 + ONE:128 + ONE + 1]
        ctx = (acc[0:count, 0:128] * inv).astype(BF)
        qrow = qg[rr, :].astype(F32)
        dots = jnp.sum(jnp.where(near, 0.0, ctx.astype(F32) * qrow), axis=1, keepdims=True)
        dhi = dots.astype(BF).astype(F32)
        dlo = dots - dhi
        qx[rr, 0:128] = jnp.where(near, 0.0, qrow).astype(BF)
        qx[rr, 128:256] = jnp.where(lane == ONE, -dhi, jnp.where(lane == TWO, -dlo, 0.0)).astype(BF)
        qn = qrow * jnp.where(near, 0.125 * inv, inv)
        qgT[:, 0:count] = qn.T.astype(BF)
        dq[0:count, :] = jnp.zeros((count, 128), F32)

        @pl.loop(0, steps)
        def _(c):
            kk = pl.ds(pl.multiple_of(c * CHUNK, 128), CHUNK)
            p = pbuf[0:count, kk]
            dpd = dot_nt(qx[rr, :], kvx[kk, :])
            ds = (p.astype(F32) * dpd).astype(BF)
            dq[0:count, :] += dot(ds, kvx[kk, 0:128])
            dk = dot(qgT[0:64, 0:count], ds)
            dv = dot(qgT[64:128, 0:count], p)
            if number == 0:
                dkT[0:64, kk] = dk
                dkT[64:128, kk] = dv
            else:
                dkT[0:64, kk] += dk
                dkT[64:128, kk] += dv

        resb[rr, :] = jnp.where(near, dq[0:count, :] * (0.125 * inv), ctx.astype(F32)).astype(BF)

        for j in range(slot0, slot0 + slots):
            to = 7 - j

            @pl.when(head != to)
            def _():
                remote(rows(resb, j * PAD), rows(rqc, head * PAD), ssem.at[4], rsem.at[4],
                       (x, 4 * to + quarter)).start()

            @pl.when(head == to)
            def _():
                pltpu.make_async_copy(rows(resb, j * PAD), rows(rqc, head * PAD), lsem.at[6]).start()

        finish(lo_group, hi_group)
        to_sibling(number, lo_group, hi_group)
    to_owners(len(BATCHES) - 1, *BATCHES[-1][4:])

    remote(al.at[:, pl.ds(0, 4)], al.at[:, pl.ds(0, 4)], ssem.at[7], rsem.at[7], (x, sib)).wait()

    def transpose_inputs(i):
        for j in range(8):
            alT[i, 128 * j:128 * j + 128, :] = al[i, :, :, 128 * j:128 * j + 128].reshape(8 * PAD, 128).T

    transpose_inputs(0)

    @pl.when(core == 1)
    def _():
        transpose_inputs(1)

    pltpu.make_async_copy(rows(resb, 0), rows(rqc, 0), lsem.at[6]).wait()
    remote(rows(rqc, 0, 7 * PAD), rows(rqc, 0, 7 * PAD), ssem.at[4], rsem.at[4], (x, sib)).wait()
    for i in range(4):
        a = rqc[(2 * i) * PAD:(2 * i + 1) * PAD, :].astype(F32)
        b = rqc[(2 * i + 1) * PAD:(2 * i + 2) * PAD, :].astype(F32)
        q_pair, c_pair = swap_pack(a, b, left)
        catp[0, i] = q_pair.astype(BF)
        catp[3, i] = c_pair.astype(BF)

    def wide(i):
        return jnp.concatenate([catp[i, j] for j in range(4)], axis=1)

    def exchange(u, blocks):
        own = pltpu.make_async_copy(catp.at[blocks[0] + (blocks[1] - blocks[0]) * core, x], cgx.at[u, spot], lsem.at[4 + u])
        own.start()

        @pl.loop(1, 8)
        def _(k):
            q = (spot + k) % 8
            block = blocks[0] + (blocks[1] - blocks[0]) * (q % 2)
            remote(catp.at[block, q // 2], cgx.at[u, spot], ssem.at[8 + u], rsem.at[8 + u], at_spot(q)).start()

        return own

    def partial_sums(u, own, lhs):
        own.wait()
        seven = cgx.at[u, pl.ds(0, 7)]
        remote(seven, seven, ssem.at[8 + u], rsem.at[8 + u], (x, sib)).wait()
        right = cgx[u].reshape(8 * PAD, 128)
        for i in range(4):
            f = dot(alT[lhs, 256 * i:256 * i + 256, :], right)
            fb[u, :, i] = f.astype(BF).reshape(16, 16, 128)

        @pl.loop(1, 16)
        def _(k):
            to = (pos + k) % 16
            remote(fb.at[u, to], fr.at[u, k - 1], ssem.at[10 + u], rsem.at[10 + u], (x, 2 * to + core)).start()

    def sums(u):
        remote(fr.at[u], fr.at[u], ssem.at[10 + u], rsem.at[10 + u], (x, sib)).wait()
        v = fb[u, pos].astype(F32)
        for k in range(15):
            v += fr[u, k].astype(F32)
        for i in range(4):
            for c in range(2):
                fo[2 * i + c, u] = v[i, 8 * c:8 * c + 8]

    early = exchange(0, (0, 3))
    att = dot(wide(3), wout[...])
    attb[...] = att[0:TOK].astype(BF)
    outs = [
        pltpu.make_async_copy(attb, att_o.at[0], lsem.at[0]),
        pltpu.make_async_copy(ingb, ing_o.at[0], lsem.at[1]),
        pltpu.make_async_copy(wob.at[:, pl.ds(0, 3 * INNER)], wq_o, lsem.at[2]),
        pltpu.make_async_copy(wob.at[:, pl.ds(3 * INNER, INNER)], wo_o, lsem.at[3]),
    ]
    outs[0].start()

    pltpu.make_async_copy(rows(dkvb, 0), rows(rkv, 0), lsem.at[7]).wait()
    remote(rows(rkv, 0, 15 * PAD), rows(rkv, 0, 15 * PAD), ssem.at[6], rsem.at[6], (x, sib)).wait()
    for i in range(4):
        a = rkv[(4 * i) * PAD:(4 * i + 1) * PAD, :].astype(F32) + rkv[(4 * i + 1) * PAD:(4 * i + 2) * PAD, :].astype(F32)
        b = rkv[(4 * i + 2) * PAD:(4 * i + 3) * PAD, :].astype(F32) + rkv[(4 * i + 3) * PAD:(4 * i + 4) * PAD, :].astype(F32)
        k_pair, v_pair = swap_pack(a, b, left)
        catp[1, i] = k_pair.astype(BF)
        catp[2, i] = v_pair.astype(BF)

    late = exchange(1, (1, 2))
    ing = dot_nt(wide(0), wqkv[:, 0:INNER])
    ing += dot_nt(wide(1), wqkv[:, INNER:2 * INNER])
    ing += dot_nt(wide(2), wqkv[:, 2 * INNER:])
    ingb[...] = ing[0:TOK].astype(BF)
    outs[1].start()
    partial_sums(0, early, core)
    partial_sums(1, late, 0)
    sums(0)
    sums(1)

    fi[spot] = fo[spot]

    @pl.loop(1, 8)
    def _(k):
        q = (spot + k) % 8
        remote(fo.at[q], fi.at[spot], ssem.at[12], rsem.at[12], at_spot(q)).start()

    remote(fi.at[pl.ds(0, 7)], fi.at[pl.ds(0, 7)], ssem.at[12], rsem.at[12], (x, sib)).wait()
    for i in range(4):
        for block, (c, u) in enumerate(((0, 0), (0, 1), (1, 1), (1, 0))):
            wob[:, INNER * block + 128 * i:INNER * block + 128 * i + 128] = fi[2 * i + c, u]
    outs[2].start()
    outs[3].start()

    remote(rows(dkvb, 0, 15 * PAD), rows(dkvb, 0, 15 * PAD), ssem.at[0], rsem.at[0], (x, sib)).wait_send()
    remote(rows(dkvb, 0, 7 * PAD), rows(dkvb, 0, 7 * PAD), ssem.at[1], rsem.at[1], (x, sib)).wait_send()
    remote(rows(dkvb, 0, 16 * PAD), rows(dkvb, 0, 16 * PAD), ssem.at[5], rsem.at[5], (x, sib)).wait_send()
    remote(al.at[:, pl.ds(0, 3)], al.at[:, pl.ds(0, 3)], ssem.at[2], rsem.at[2], (x, sib)).wait_send()
    for c in outs:
        c.wait()


def hand_out(*refs):
    came, gone, held, sems = refs[0:4], refs[4:8], refs[8:12], refs[12]
    ins = [pltpu.make_async_copy(came[i], held[i], sems.at[i]) for i in range(4)]
    outs = [pltpu.make_async_copy(held[i], gone[i], sems.at[4 + i]) for i in range(4)]
    for c in ins:
        c.start()
    for i in range(4):
        ins[i].wait()
        outs[i].start()
    for c in outs:
        c.wait()


def shards(activations, qkv_weight, out_weight, out_grad):
    any_spec = pl.BlockSpec(memory_space=pl.ANY)
    V = pltpu.VMEM
    scratch = [
        V((2, 8, PAD, D), BF),
        V((2, D, 8 * PAD), BF),
        V((D, 3 * INNER), BF),
        V((INNER, D), BF),
        V((8 * PAD, 128), BF),
        V((8 * PAD, 128), BF),
        V((KEYS, 256), BF),
        V((8 * PAD, 128), BF),
        V((8 * PAD, 256), BF),
        V((3 * PAD, KEYS), F32),
        V((3 * PAD, KEYS), BF),
        V((3 * PAD, 128), F32),
        V((3 * PAD, 256), F32),
        V((3 * PAD, 128), F32),
        V((128, 3 * PAD), BF),
        V((128, KEYS), F32),
        V((KEYS, 128), BF),
        V((KEYS, 128), BF),
        V((8 * PAD, 128), BF),
        V((8 * PAD, 128), BF),
        V((16 * PAD, 128), BF),
        V((4, 4, PAD, 128), BF),
        V((2, 8, PAD, 128), BF),
        V((2, 16, 4, 16, 128), BF),
        V((2, 15, 4, 16, 128), BF),
        V((8, 2, 8, 128), F32),
        V((8, 2, 8, 128), F32),
        V((TOK, D), BF),
        V((TOK, D), BF),
        V((8, 2 * D), F32),
        pltpu.SemaphoreType.DMA((8,)),
        pltpu.SemaphoreType.DMA((13,)),
        pltpu.SemaphoreType.DMA((13,)),
        pltpu.SemaphoreType.DMA((16,)),
        pltpu.SemaphoreType.DMA((3,)),
        pltpu.SemaphoreType.DMA((4,)),
    ]
    made = pl.pallas_call(
        kernel,
        out_shape=(
            jax.ShapeDtypeStruct((1, TOK, D), BF),
            jax.ShapeDtypeStruct((1, TOK, D), BF),
            jax.ShapeDtypeStruct((8, 3 * INNER), F32),
            jax.ShapeDtypeStruct((8, INNER), F32),
        ),
        in_specs=[any_spec] * 4,
        out_specs=(any_spec,) * 4,
        scratch_shapes=scratch,
        compiler_params=pltpu.CompilerParams(
            collective_id=0, has_side_effects=True, vmem_limit_bytes=56 * 1024 * 1024),
        name="attention_sublayer",
    )(activations, qkv_weight, out_weight, out_grad)
    att, ing, wq, wo = pl.pallas_call(
        hand_out,
        out_shape=tuple(jax.ShapeDtypeStruct(a.shape, a.dtype) for a in made),
        in_specs=[any_spec] * 4,
        out_specs=(any_spec,) * 4,
        scratch_shapes=[V(a.shape, a.dtype) for a in made] + [pltpu.SemaphoreType.DMA((8,))],
        name="hand_out",
    )(*made)
    return att, ing, wq, wo.T


def solution(mesh):
    return jax.shard_map(
        shards,
        mesh=mesh,
        in_specs=(P("dp", "seq", None), P(), P(), P("dp", "seq", None)),
        out_specs=(
            P("dp", "seq", None),
            P("dp", "seq", None),
            P(("dp", "seq"), None),
            P(None, ("dp", "seq")),
        ),
        check_vma=False,
    )
```

```python
import functools
import math

import jax
import jax.numpy as jnp
import numpy as np
from jax import lax
from jax.experimental import pallas as pl
from jax.experimental.pallas import tpu as pltpu
from jax.sharding import PartitionSpec as P

MESH = pl.DeviceIdType.MESH
BF = jnp.bfloat16
F32 = jnp.float32

HEADS = 8
SEQ = 32
TOK = 136
PAD = 144
KEYS = SEQ * PAD
D = 1024
INNER = 512
SIDES = (1, 2, 3, 4, 5, 8, 9, 10, 14, 16, 20, 24, 32, 40)
ENDS = [int(v) for v in np.cumsum([a * a for a in SIDES])]
STARTS = [0] + ENDS[:-1]
FAR = 1 << 20
BIG = 1e30
ONE = 15
TWO = 16
BATCHES = (
    (0, 3, 4608, 2304, 22, 32),
    (3, 2, 3072, 1536, 14, 22),
    (5, 3, 1920, 1920, 0, 14),
)
NT = (((1,), (1,)), ((), ()))


def dot(a, b):
    return jnp.dot(a, b, preferred_element_type=F32)


def dot_nt(a, b):
    return lax.dot_general(a, b, NT, preferred_element_type=F32)


def lane_bounds(rows):
    lane = lax.broadcasted_iota(jnp.int32, (rows, 128), 1)
    lo = jnp.full((rows, 128), -1, jnp.int32)
    hi = jnp.full((rows, 128), -1, jnp.int32)
    for i, (a, b) in enumerate(zip(STARTS, ENDS)):
        lo = jnp.where(lane == i, a, lo)
        hi = jnp.where(lane == i, b, hi)
    lo = jnp.where(lane == 14, FAR, lo)
    hi = jnp.where(lane == 14, FAR + 1, hi)
    ones = (lane == ONE) | (lane == TWO)
    lo = jnp.where(ones, 0, lo)
    hi = jnp.where(ones, ENDS[-1], hi)
    return lo, hi


def swap_pack(a, b, left):
    return (
        jnp.where(left, a, pltpu.roll(b, 64, 1)),
        jnp.where(left, pltpu.roll(a, 64, 1), b),
    )


def kernel(act_h, wqkv_h, wout_h, og_h, att_o, ing_o, wq_o, wo_o,
           al, alT, wqkv, wout, sendkv, sendqg, kvx, qg, qx, sbuf, pbuf, macc, acc, dq,
           qgT, dkT, dkvb, sibr, resb, rqc, rkv, catp, cge, cgl, cgx, fb, fr, fo, fi,
           attb, ingb, wob, lsem, ssem, rsem, ksem, dsem, xsem):
    x = lax.axis_index("dp")
    s = lax.axis_index("seq")
    head, quarter = s // 4, s % 4
    pos, core = s // 2, s % 2
    sib = s + 1 - 2 * core
    spot = 2 * x + core

    cin = [
        pltpu.make_async_copy(act_h.at[0], al.at[0, spot, pl.ds(0, TOK)], lsem.at[0]),
        pltpu.make_async_copy(wqkv_h, wqkv, lsem.at[1]),
        pltpu.make_async_copy(og_h.at[0], al.at[1, spot, pl.ds(0, TOK)], lsem.at[2]),
        pltpu.make_async_copy(wout_h, wout, lsem.at[3]),
    ]
    for c in cin:
        c.start()

    bar = pltpu.get_barrier_semaphore()

    @pl.loop(1, 16)
    def _(k):
        pl.semaphore_signal(bar, inc=1, device_id=(x, 2 * ((pos + k) % 16) + core), device_id_type=MESH)

    def at_spot(q):
        return (q // 2, 2 * pos + q % 2)

    @pl.loop(1, 8)
    def _(k):
        pl.semaphore_signal(bar, inc=1, device_id=at_spot((spot + k) % 8), device_id_type=MESH)

    @pl.loop(0, 16)
    def _(k):
        @pl.when((k // 4 != x) | (4 * spot + k % 4 != s))
        def _():
            pl.semaphore_signal(bar, inc=1, device_id=(k // 4, 4 * spot + k % 4), device_id_type=MESH)

    for i in range(2):
        al[i, spot, TOK:PAD, :] = jnp.zeros((PAD - TOK, D), BF)

    def remote(src, dst, send, recv, dev):
        return pltpu.make_async_remote_copy(
            src_ref=src, dst_ref=dst, send_sem=send, recv_sem=recv, device_id=dev, device_id_type=MESH)

    def rows(ref, first, count=PAD):
        return ref.at[pl.ds(pl.multiple_of(first, 16), count)]

    def kvslot(g):
        return kvx.at[pl.ds(pl.multiple_of(g * PAD, 16), PAD), pl.ds(0, 128)]

    left = lax.broadcasted_iota(jnp.int32, (PAD, 128), 1) < 64

    cin[0].wait()
    cin[1].wait()
    kp = dot(al[0, spot], wqkv[:, INNER:2 * INNER])
    vp = dot(al[0, spot], wqkv[:, 2 * INNER:])
    for i in range(4):
        a, b = swap_pack(kp[:, 128 * i:128 * i + 128], vp[:, 128 * i:128 * i + 128], left)
        sendkv[(2 * i) * PAD:(2 * i + 1) * PAD, :] = a.astype(BF)
        sendkv[(2 * i + 1) * PAD:(2 * i + 2) * PAD, :] = b.astype(BF)

    cin[2].wait()
    cin[3].wait()
    qp = dot(al[0, spot], wqkv[:, 0:INNER])
    gp = dot_nt(al[1, spot], wout[...])
    for i in range(4):
        a, b = swap_pack(qp[:, 128 * i:128 * i + 128], gp[:, 128 * i:128 * i + 128], left)
        sendqg[(2 * i) * PAD:(2 * i + 1) * PAD, :] = a.astype(BF)
        sendqg[(2 * i + 1) * PAD:(2 * i + 2) * PAD, :] = b.astype(BF)

    lo, hi = lane_bounds(PAD)
    place = lax.broadcasted_iota(jnp.int32, (PAD, 128), 0)

    @pl.loop(0, SEQ)
    def _(g):
        t = jnp.where(place < TOK, place + g * TOK, FAR)
        kvx[pl.ds(pl.multiple_of(g * PAD, 16), PAD), 128:256] = jnp.where(
            (t >= lo) & (t < hi), 1.0, 0.0).astype(BF)

    pl.semaphore_wait(bar, jnp.where(head == spot, 37, 38))
    own_kv = pltpu.make_async_copy(rows(sendkv, head * PAD), kvslot(s), lsem.at[4])
    own_kv.start()
    remote(rows(sendkv, head * PAD), kvslot(s), ssem.at[3], rsem.at[3], (x, sib)).start()

    @pl.loop(1, 16)
    def _(k):
        to = (pos + k) % 16
        remote(rows(sendkv, (to // 2) * PAD), kvslot(s), ssem.at[0], ksem.at[pos], (x, 2 * to + core)).start()

    @pl.loop(1, 4)
    def _(k):
        remote(al.at[:, spot], al.at[:, spot], ssem.at[2], xsem.at[x], ((x + k) % 4, s)).start()

    remote(al.at[:, spot], al.at[:, spot], ssem.at[7], rsem.at[7], (x, sib)).start()

    slot = 7 - s // 4
    own_qg = pltpu.make_async_copy(rows(sendqg, head * PAD), rows(qg, slot * PAD), lsem.at[5])
    own_qg.start()

    @pl.loop(1, 8)
    def _(k):
        to = (head + k) % 8
        remote(rows(sendqg, to * PAD), rows(qg, slot * PAD), ssem.at[1], rsem.at[1], (x, 4 * to + quarter)).start()

    @pl.loop(1, 16)
    def _(k):
        frm = (pos + 16 - k) % 16
        g = 2 * frm + core
        remote(kvslot(g), kvslot(g), ssem.at[0], ksem.at[frm], (x, sib)).wait_recv()
        remote(kvslot(g), kvslot(g), ssem.at[3], rsem.at[3], (x, sib)).start()

    own_kv.wait()
    own_qg.wait()
    remote(rows(dkvb, 0, 7 * PAD), rows(dkvb, 0, 7 * PAD), ssem.at[1], rsem.at[1], (x, sib)).wait_recv()

    @pl.loop(0, 8)
    def _(j):
        g = 4 * (7 - j) + quarter
        t = jnp.where(place < TOK, place + g * TOK, ENDS[-1] - 1)
        r = pl.ds(pl.multiple_of(j * PAD, 16), PAD)
        qx[r, 128:256] = jnp.where(lo > t, -BIG, 0.0).astype(BF)
        qx[r, 0:128] = jnp.where(left, qg[r, :].astype(F32) * 0.125, 0.0).astype(BF)

    remote(rows(dkvb, 0, 16 * PAD), rows(dkvb, 0, 16 * PAD), ssem.at[3], rsem.at[3], (x, sib)).wait()

    part = 2 * head + (pos % 2)

    def to_summer(block, place, held, group_pos, n):
        here = (head == spot) & (group_pos == pos)

        @pl.when(jnp.logical_not(here))
        def _():
            remote(block, rows(held, place * PAD), ssem.at[8 + n], rsem.at[8 + n],
                   (head // 2, 2 * group_pos + head % 2)).start()

        @pl.when(here)
        def _():
            pltpu.make_async_copy(block, rows(held, place * PAD), lsem.at[4 + n]).start()

    def all_summed(held, count, n):
        @pl.when(head == spot)
        def _():
            some = rows(held, 0, (count - 1) * PAD)
            remote(some, some, ssem.at[8 + n], rsem.at[8 + n], (x, sib)).wait()
            pltpu.make_async_copy(rows(dkvb, 0), rows(held, 0), lsem.at[4 + n]).wait()

        @pl.when(head != spot)
        def _():
            remote(held, held, ssem.at[8 + n], rsem.at[8 + n], (x, sib)).wait()

    def finish(lo_group, hi_group):
        lo_row, hi_row = lo_group * PAD, hi_group * PAD
        for blk in range(lo_row // 128, -(-hi_row // 128)):
            a, b = max(lo_row - 128 * blk, 0), min(hi_row - 128 * blk, 128)
            v = dkT[:, 128 * blk:128 * blk + 128].T
            dkvb[128 * blk + a:128 * blk + b, :] = v[a:b].astype(BF)

    def to_sibling(number, lo_group, hi_group):
        @pl.loop(lo_group // 2, hi_group // 2)
        def _(k):
            g = 2 * k + 1 - core
            remote(rows(dkvb, g * PAD), rows(sibr, g * PAD), ssem.at[5], dsem.at[number], (x, sib)).start()

    def to_owners(number, lo_group, hi_group):
        n = (hi_group - lo_group) // 2 * PAD
        remote(rows(dkvb, 0, n), rows(sibr, 0, n), ssem.at[5], dsem.at[number], (x, sib)).wait_recv()

        @pl.loop(lo_group // 2, hi_group // 2)
        def _(k):
            g = 2 * k + core
            r = pl.ds(pl.multiple_of(g * PAD, 16), PAD)
            dkvb[r, :] = (dkvb[r, :].astype(F32) + sibr[r, :].astype(F32)).astype(BF)

            @pl.when(k != pos)
            def _():
                remote(rows(dkvb, g * PAD), rows(rkv, part * PAD), ssem.at[6], rsem.at[6], (x, g)).start()

            @pl.when(k == pos)
            def _():
                pltpu.make_async_copy(rows(dkvb, g * PAD), rows(rkv, part * PAD), lsem.at[7]).start()

            to_summer(rows(dkvb, g * PAD), 2 * spot + pos % 2, cgl, k, 1)

    for number, (slot0, slots, keys, CHUNK, lo_group, hi_group) in enumerate(BATCHES):
        row0, count = slot0 * PAD, slots * PAD
        rr = slice(row0, row0 + count)
        steps = keys // CHUNK
        macc[0:count, :] = jnp.full((count, 128), -3e38, F32)

        @pl.loop(0, steps)
        def _(c):
            kk = pl.ds(pl.multiple_of(c * CHUNK, 128), CHUNK)
            sc = dot_nt(qx[rr, :], kvx[kk, :])
            sbuf[0:count, kk] = sc
            top = macc[0:count, :]
            for i in range(CHUNK // 128):
                top = jnp.maximum(top, sc[:, 128 * i:128 * i + 128])
            macc[0:count, :] = top

        if number > 0:
            to_owners(number - 1, *BATCHES[number - 1][4:])
        row_max = jnp.max(macc[0:count, :], axis=1, keepdims=True)
        acc[0:count, :] = jnp.zeros((count, 256), F32)

        @pl.loop(0, steps)
        def _(c):
            kk = pl.ds(pl.multiple_of(c * CHUNK, 128), CHUNK)
            p = jnp.exp(sbuf[0:count, kk] - row_max).astype(BF)
            pbuf[0:count, kk] = p
            acc[0:count, :] += dot(p, kvx[kk, :])

        if number == 2:
            @pl.loop(1, 4)
            def _(k):
                frm = (x + k) % 4
                q = 2 * frm + core
                remote(al.at[:, q], al.at[:, q], ssem.at[2], xsem.at[frm], (x, sib)).wait_recv()
                remote(al.at[:, q], al.at[:, q], ssem.at[7], rsem.at[7], (x, sib)).start()

        lane = lax.broadcasted_iota(jnp.int32, (count, 128), 1)
        near = lane < 64
        inv = 1.0 / acc[0:count, 128 + ONE:128 + ONE + 1]
        ctx = (acc[0:count, 0:128] * inv).astype(BF)
        qrow = qg[rr, :].astype(F32)
        dots = jnp.sum(jnp.where(near, 0.0, ctx.astype(F32) * qrow), axis=1, keepdims=True)
        dhi = dots.astype(BF).astype(F32)
        dlo = dots - dhi
        qx[rr, 0:128] = jnp.where(near, 0.0, qrow).astype(BF)
        qx[rr, 128:256] = jnp.where(lane == ONE, -dhi, jnp.where(lane == TWO, -dlo, 0.0)).astype(BF)
        qn = qrow * jnp.where(near, 0.125 * inv, inv)
        qgT[:, 0:count] = qn.T.astype(BF)
        dq[0:count, :] = jnp.zeros((count, 128), F32)

        @pl.loop(0, steps)
        def _(c):
            kk = pl.ds(pl.multiple_of(c * CHUNK, 128), CHUNK)
            p = pbuf[0:count, kk]
            dpd = dot_nt(qx[rr, :], kvx[kk, :])
            ds = (p.astype(F32) * dpd).astype(BF)
            dq[0:count, :] += dot(ds, kvx[kk, 0:128])
            dk = dot(qgT[0:64, 0:count], ds)
            dv = dot(qgT[64:128, 0:count], p)
            if number == 0:
                dkT[0:64, kk] = dk
                dkT[64:128, kk] = dv
            else:
                dkT[0:64, kk] += dk
                dkT[64:128, kk] += dv

        resb[rr, :] = jnp.where(near, dq[0:count, :] * (0.125 * inv), ctx.astype(F32)).astype(BF)

        for j in range(slot0, slot0 + slots):
            to = 7 - j

            @pl.when(head != to)
            def _():
                remote(rows(resb, j * PAD), rows(rqc, head * PAD), ssem.at[4], rsem.at[4],
                       (x, 4 * to + quarter)).start()

            @pl.when(head == to)
            def _():
                pltpu.make_async_copy(rows(resb, j * PAD), rows(rqc, head * PAD), lsem.at[6]).start()

            to_summer(rows(resb, j * PAD), spot, cge, 2 * to + quarter // 2, 0)

        finish(lo_group, hi_group)
        to_sibling(number, lo_group, hi_group)
    to_owners(len(BATCHES) - 1, *BATCHES[-1][4:])

    remote(al.at[:, pl.ds(0, 4)], al.at[:, pl.ds(0, 4)], ssem.at[7], rsem.at[7], (x, sib)).wait()

    def transpose_inputs(i):
        for j in range(8):
            alT[i, 128 * j:128 * j + 128, :] = al[i, :, :, 128 * j:128 * j + 128].reshape(8 * PAD, 128).T

    transpose_inputs(0)
    transpose_inputs(1)

    def reduced(u, i, f):
        fb[u, :, i] = f.astype(BF).reshape(16, 16, 128)

    def spread(u):
        @pl.loop(1, 16)
        def _(k):
            to = (pos + k) % 16
            remote(fb.at[u, to], fr.at[u, k - 1], ssem.at[10 + u], rsem.at[10 + u], (x, 2 * to + core)).start()

    all_summed(cge, 8, 0)
    wide_left = lax.broadcasted_iota(jnp.int32, (256, 128), 1) < 64
    for i in range(4):
        rr = slice(256 * i, 256 * i + 256)
        reduced(0, i, jnp.where(wide_left, dot(alT[0, rr, :], cge[...]), dot(alT[1, rr, :], cge[...])))
    spread(0)

    pltpu.make_async_copy(rows(resb, 0), rows(rqc, 0), lsem.at[6]).wait()
    remote(rows(rqc, 0, 7 * PAD), rows(rqc, 0, 7 * PAD), ssem.at[4], rsem.at[4], (x, sib)).wait()
    for i in range(4):
        a = rqc[(2 * i) * PAD:(2 * i + 1) * PAD, :].astype(F32)
        b = rqc[(2 * i + 1) * PAD:(2 * i + 2) * PAD, :].astype(F32)
        q_pair, c_pair = swap_pack(a, b, left)
        catp[0, i] = q_pair.astype(BF)
        catp[3, i] = c_pair.astype(BF)

    def wide(i):
        return jnp.concatenate([catp[i, j] for j in range(4)], axis=1)

    att = dot(wide(3), wout[...])
    attb[...] = att[0:TOK].astype(BF)
    outs = [
        pltpu.make_async_copy(attb, att_o.at[0], lsem.at[0]),
        pltpu.make_async_copy(ingb, ing_o.at[0], lsem.at[1]),
        pltpu.make_async_copy(wob.at[:, pl.ds(0, 3 * INNER)], wq_o, lsem.at[2]),
        pltpu.make_async_copy(wob.at[:, pl.ds(3 * INNER, INNER)], wo_o, lsem.at[3]),
    ]
    outs[0].start()

    all_summed(cgl, 16, 1)
    for q in range(8):
        cgx[q * PAD:(q + 1) * PAD, :] = (
            cgl[(2 * q) * PAD:(2 * q + 1) * PAD, :].astype(F32) + cgl[(2 * q + 1) * PAD:(2 * q + 2) * PAD, :].astype(F32)
        ).astype(BF)
    for i in range(4):
        reduced(1, i, dot(alT[0, 256 * i:256 * i + 256, :], cgx[...]))
    spread(1)

    pltpu.make_async_copy(rows(dkvb, 0), rows(rkv, 0), lsem.at[7]).wait()
    remote(rows(rkv, 0, 15 * PAD), rows(rkv, 0, 15 * PAD), ssem.at[6], rsem.at[6], (x, sib)).wait()
    for i in range(4):
        a = rkv[(4 * i) * PAD:(4 * i + 1) * PAD, :].astype(F32) + rkv[(4 * i + 1) * PAD:(4 * i + 2) * PAD, :].astype(F32)
        b = rkv[(4 * i + 2) * PAD:(4 * i + 3) * PAD, :].astype(F32) + rkv[(4 * i + 3) * PAD:(4 * i + 4) * PAD, :].astype(F32)
        k_pair, v_pair = swap_pack(a, b, left)
        catp[1, i] = k_pair.astype(BF)
        catp[2, i] = v_pair.astype(BF)

    ing = dot_nt(wide(0), wqkv[:, 0:INNER])
    ing += dot_nt(wide(1), wqkv[:, INNER:2 * INNER])
    ing += dot_nt(wide(2), wqkv[:, 2 * INNER:])
    ingb[...] = ing[0:TOK].astype(BF)
    outs[1].start()
    def sums(u):
        remote(fr.at[u], fr.at[u], ssem.at[10 + u], rsem.at[10 + u], (x, sib)).wait()
        v = fb[u, pos].astype(F32)
        for k in range(15):
            v += fr[u, k].astype(F32)
        for i in range(4):
            for c in range(2):
                fo[2 * i + c, u] = v[i, 8 * c:8 * c + 8]

    sums(0)
    sums(1)

    fi[spot] = fo[spot]

    @pl.loop(1, 8)
    def _(k):
        q = (spot + k) % 8
        remote(fo.at[q], fi.at[spot], ssem.at[12], rsem.at[12], at_spot(q)).start()

    remote(fi.at[pl.ds(0, 7)], fi.at[pl.ds(0, 7)], ssem.at[12], rsem.at[12], (x, sib)).wait()
    for i in range(4):
        for u, blocks in enumerate(((0, 3), (1, 2))):
            pair = swap_pack(fi[2 * i, u], fi[2 * i + 1, u], left[0:8])
            for block, v in zip(blocks, pair):
                wob[:, INNER * block + 128 * i:INNER * block + 128 * i + 128] = v
    outs[2].start()
    outs[3].start()

    remote(rows(dkvb, 0, 15 * PAD), rows(dkvb, 0, 15 * PAD), ssem.at[0], rsem.at[0], (x, sib)).wait_send()
    remote(rows(dkvb, 0, 7 * PAD), rows(dkvb, 0, 7 * PAD), ssem.at[1], rsem.at[1], (x, sib)).wait_send()
    remote(rows(dkvb, 0, 16 * PAD), rows(dkvb, 0, 16 * PAD), ssem.at[5], rsem.at[5], (x, sib)).wait_send()
    remote(al.at[:, pl.ds(0, 3)], al.at[:, pl.ds(0, 3)], ssem.at[2], rsem.at[2], (x, sib)).wait_send()
    for c in outs:
        c.wait()


def hand_out(*refs):
    came, gone, held, sems = refs[0:4], refs[4:8], refs[8:12], refs[12]
    ins = [pltpu.make_async_copy(came[i], held[i], sems.at[i]) for i in range(4)]
    outs = [pltpu.make_async_copy(held[i], gone[i], sems.at[4 + i]) for i in range(4)]
    for c in ins:
        c.start()
    for i in range(4):
        ins[i].wait()
        outs[i].start()
    for c in outs:
        c.wait()


def shards(activations, qkv_weight, out_weight, out_grad):
    any_spec = pl.BlockSpec(memory_space=pl.ANY)
    V = pltpu.VMEM
    scratch = [
        V((2, 8, PAD, D), BF),
        V((2, D, 8 * PAD), BF),
        V((D, 3 * INNER), BF),
        V((INNER, D), BF),
        V((8 * PAD, 128), BF),
        V((8 * PAD, 128), BF),
        V((KEYS, 256), BF),
        V((8 * PAD, 128), BF),
        V((8 * PAD, 256), BF),
        V((3 * PAD, KEYS), F32),
        V((3 * PAD, KEYS), BF),
        V((3 * PAD, 128), F32),
        V((3 * PAD, 256), F32),
        V((3 * PAD, 128), F32),
        V((128, 3 * PAD), BF),
        V((128, KEYS), F32),
        V((KEYS, 128), BF),
        V((KEYS, 128), BF),
        V((8 * PAD, 128), BF),
        V((8 * PAD, 128), BF),
        V((16 * PAD, 128), BF),
        V((4, 4, PAD, 128), BF),
        V((8 * PAD, 128), BF),
        V((16 * PAD, 128), BF),
        V((8 * PAD, 128), BF),
        V((2, 16, 4, 16, 128), BF),
        V((2, 15, 4, 16, 128), BF),
        V((8, 2, 8, 128), F32),
        V((8, 2, 8, 128), F32),
        V((TOK, D), BF),
        V((TOK, D), BF),
        V((8, 2 * D), F32),
        pltpu.SemaphoreType.DMA((8,)),
        pltpu.SemaphoreType.DMA((13,)),
        pltpu.SemaphoreType.DMA((13,)),
        pltpu.SemaphoreType.DMA((16,)),
        pltpu.SemaphoreType.DMA((3,)),
        pltpu.SemaphoreType.DMA((4,)),
    ]
    made = pl.pallas_call(
        kernel,
        out_shape=(
            jax.ShapeDtypeStruct((1, TOK, D), BF),
            jax.ShapeDtypeStruct((1, TOK, D), BF),
            jax.ShapeDtypeStruct((8, 3 * INNER), F32),
            jax.ShapeDtypeStruct((8, INNER), F32),
        ),
        in_specs=[any_spec] * 4,
        out_specs=(any_spec,) * 4,
        scratch_shapes=scratch,
        compiler_params=pltpu.CompilerParams(
            collective_id=0, has_side_effects=True, vmem_limit_bytes=56 * 1024 * 1024),
        name="attention_sublayer",
    )(activations, qkv_weight, out_weight, out_grad)
    att, ing, wq, wo = pl.pallas_call(
        hand_out,
        out_shape=tuple(jax.ShapeDtypeStruct(a.shape, a.dtype) for a in made),
        in_specs=[any_spec] * 4,
        out_specs=(any_spec,) * 4,
        scratch_shapes=[V(a.shape, a.dtype) for a in made] + [pltpu.SemaphoreType.DMA((8,))],
        name="hand_out",
    )(*made)
    return att, ing, wq, wo.T


def solution(mesh):
    return jax.shard_map(
        shards,
        mesh=mesh,
        in_specs=(P("dp", "seq", None), P(), P(), P("dp", "seq", None)),
        out_specs=(
            P("dp", "seq", None),
            P("dp", "seq", None),
            P(("dp", "seq"), None),
            P(None, ("dp", "seq")),
        ),
        check_vma=False,
    )
```

```python
import functools
import math

import jax
import jax.numpy as jnp
import numpy as np
from jax import lax
from jax.experimental import pallas as pl
from jax.experimental.pallas import tpu as pltpu
from jax.sharding import PartitionSpec as P

MESH = pl.DeviceIdType.MESH
BF = jnp.bfloat16
F32 = jnp.float32

HEADS = 8
SEQ = 32
TOK = 136
PAD = 144
KEYS = SEQ * PAD
D = 1024
INNER = 512
SIDES = (1, 2, 3, 4, 5, 8, 9, 10, 14, 16, 20, 24, 32, 40)
ENDS = [int(v) for v in np.cumsum([a * a for a in SIDES])]
STARTS = [0] + ENDS[:-1]
FAR = 1 << 20
BIG = 1e30
ONE = 15
TWO = 16
BATCHES = (
    (0, 3, 4608, 2304, 22, 32),
    (3, 2, 3072, 1536, 14, 22),
    (5, 3, 1920, 1920, 0, 14),
)
NT = (((1,), (1,)), ((), ()))


def dot(a, b):
    return jnp.dot(a, b, preferred_element_type=F32)


def dot_nt(a, b):
    return lax.dot_general(a, b, NT, preferred_element_type=F32)


def lane_bounds(rows):
    lane = lax.broadcasted_iota(jnp.int32, (rows, 128), 1)
    lo = jnp.full((rows, 128), -1, jnp.int32)
    hi = jnp.full((rows, 128), -1, jnp.int32)
    for i, (a, b) in enumerate(zip(STARTS, ENDS)):
        lo = jnp.where(lane == i, a, lo)
        hi = jnp.where(lane == i, b, hi)
    lo = jnp.where(lane == 14, FAR, lo)
    hi = jnp.where(lane == 14, FAR + 1, hi)
    ones = (lane == ONE) | (lane == TWO)
    lo = jnp.where(ones, 0, lo)
    hi = jnp.where(ones, ENDS[-1], hi)
    return lo, hi


def swap_pack(a, b, left):
    return (
        jnp.where(left, a, pltpu.roll(b, 64, 1)),
        jnp.where(left, pltpu.roll(a, 64, 1), b),
    )


def kernel(act_h, wqkv_h, wout_h, og_h, att_o, ing_o, wq_o, wo_o,
           al, alT, wqkv, wout, sendkv, sendqg, kvx, qg, qx, sbuf, pbuf, macc, acc, dq,
           qgT, dkT, dkvb, sibr, resb, rqc, rkv, catp, cge, cgl, cgx, fb, fr, fo, fi,
           attb, ingb, wob, lsem, ssem, rsem, ksem, dsem, xsem):
    x = lax.axis_index("dp")
    s = lax.axis_index("seq")
    head, quarter = s // 4, s % 4
    pos, core = s // 2, s % 2
    sib = s + 1 - 2 * core
    spot = 2 * x + core

    cin = [
        pltpu.make_async_copy(act_h.at[0], al.at[0, spot, pl.ds(0, TOK)], lsem.at[0]),
        pltpu.make_async_copy(wqkv_h, wqkv, lsem.at[1]),
        pltpu.make_async_copy(og_h.at[0], al.at[1, spot, pl.ds(0, TOK)], lsem.at[2]),
        pltpu.make_async_copy(wout_h, wout, lsem.at[3]),
    ]
    for c in cin:
        c.start()

    bar = pltpu.get_barrier_semaphore()

    @pl.loop(1, 16)
    def _(k):
        pl.semaphore_signal(bar, inc=1, device_id=(x, 2 * ((pos + k) % 16) + core), device_id_type=MESH)

    def at_spot(q):
        return (q // 2, 2 * pos + q % 2)

    @pl.loop(1, 8)
    def _(k):
        pl.semaphore_signal(bar, inc=1, device_id=at_spot((spot + k) % 8), device_id_type=MESH)

    def summer(h, at):
        return (h // 2 + at // 4 + at % 4) % 4, 2 * at + h % 2

    mine = 2 * ((x + 8 - pos // 4 - pos % 4) % 4) + core

    @pl.loop(0, 16)
    def _(k):
        @pl.when((k // 4 != x) | (4 * mine + k % 4 != s))
        def _():
            pl.semaphore_signal(bar, inc=1, device_id=(k // 4, 4 * mine + k % 4), device_id_type=MESH)

    @pl.loop(1, 16)
    def _(k):
        pl.semaphore_signal(bar, inc=1, device_id=summer(mine, (pos + k) % 16), device_id_type=MESH)

    for i in range(2):
        al[i, spot, TOK:PAD, :] = jnp.zeros((PAD - TOK, D), BF)

    def remote(src, dst, send, recv, dev):
        return pltpu.make_async_remote_copy(
            src_ref=src, dst_ref=dst, send_sem=send, recv_sem=recv, device_id=dev, device_id_type=MESH)

    def rows(ref, first, count=PAD):
        return ref.at[pl.ds(pl.multiple_of(first, 16), count)]

    def kvslot(g):
        return kvx.at[pl.ds(pl.multiple_of(g * PAD, 16), PAD), pl.ds(0, 128)]

    left = lax.broadcasted_iota(jnp.int32, (PAD, 128), 1) < 64

    cin[0].wait()
    cin[1].wait()
    kp = dot(al[0, spot], wqkv[:, INNER:2 * INNER])
    vp = dot(al[0, spot], wqkv[:, 2 * INNER:])
    for i in range(4):
        a, b = swap_pack(kp[:, 128 * i:128 * i + 128], vp[:, 128 * i:128 * i + 128], left)
        sendkv[(2 * i) * PAD:(2 * i + 1) * PAD, :] = a.astype(BF)
        sendkv[(2 * i + 1) * PAD:(2 * i + 2) * PAD, :] = b.astype(BF)

    cin[2].wait()
    cin[3].wait()
    qp = dot(al[0, spot], wqkv[:, 0:INNER])
    gp = dot_nt(al[1, spot], wout[...])
    for i in range(4):
        a, b = swap_pack(qp[:, 128 * i:128 * i + 128], gp[:, 128 * i:128 * i + 128], left)
        sendqg[(2 * i) * PAD:(2 * i + 1) * PAD, :] = a.astype(BF)
        sendqg[(2 * i + 1) * PAD:(2 * i + 2) * PAD, :] = b.astype(BF)

    lo, hi = lane_bounds(PAD)
    place = lax.broadcasted_iota(jnp.int32, (PAD, 128), 0)

    @pl.loop(0, SEQ)
    def _(g):
        t = jnp.where(place < TOK, place + g * TOK, FAR)
        kvx[pl.ds(pl.multiple_of(g * PAD, 16), PAD), 128:256] = jnp.where(
            (t >= lo) & (t < hi), 1.0, 0.0).astype(BF)

    pl.semaphore_wait(bar, jnp.where(head == mine, 52, 53))
    own_kv = pltpu.make_async_copy(rows(sendkv, head * PAD), kvslot(s), lsem.at[4])
    own_kv.start()
    remote(rows(sendkv, head * PAD), kvslot(s), ssem.at[3], rsem.at[3], (x, sib)).start()

    @pl.loop(1, 16)
    def _(k):
        to = (pos + k) % 16
        remote(rows(sendkv, (to // 2) * PAD), kvslot(s), ssem.at[0], ksem.at[pos], (x, 2 * to + core)).start()

    @pl.loop(1, 4)
    def _(k):
        remote(al.at[:, spot], al.at[:, spot], ssem.at[2], xsem.at[x], ((x + k) % 4, s)).start()

    remote(al.at[:, spot], al.at[:, spot], ssem.at[7], rsem.at[7], (x, sib)).start()

    slot = 7 - s // 4
    own_qg = pltpu.make_async_copy(rows(sendqg, head * PAD), rows(qg, slot * PAD), lsem.at[5])
    own_qg.start()

    @pl.loop(1, 8)
    def _(k):
        to = (head + k) % 8
        remote(rows(sendqg, to * PAD), rows(qg, slot * PAD), ssem.at[1], rsem.at[1], (x, 4 * to + quarter)).start()

    @pl.loop(1, 16)
    def _(k):
        frm = (pos + 16 - k) % 16
        g = 2 * frm + core
        remote(kvslot(g), kvslot(g), ssem.at[0], ksem.at[frm], (x, sib)).wait_recv()
        remote(kvslot(g), kvslot(g), ssem.at[3], rsem.at[3], (x, sib)).start()

    own_kv.wait()
    own_qg.wait()
    remote(rows(dkvb, 0, 7 * PAD), rows(dkvb, 0, 7 * PAD), ssem.at[1], rsem.at[1], (x, sib)).wait_recv()

    @pl.loop(0, 8)
    def _(j):
        g = 4 * (7 - j) + quarter
        t = jnp.where(place < TOK, place + g * TOK, ENDS[-1] - 1)
        r = pl.ds(pl.multiple_of(j * PAD, 16), PAD)
        qx[r, 128:256] = jnp.where(lo > t, -BIG, 0.0).astype(BF)
        qx[r, 0:128] = jnp.where(left, qg[r, :].astype(F32) * 0.125, 0.0).astype(BF)

    remote(rows(dkvb, 0, 16 * PAD), rows(dkvb, 0, 16 * PAD), ssem.at[3], rsem.at[3], (x, sib)).wait()

    part = 2 * head + (pos % 2)

    def to_summer(block, place, held, group_pos, n):
        here = (head == mine) & (group_pos == pos)

        @pl.when(jnp.logical_not(here))
        def _():
            remote(block, rows(held, place * PAD), ssem.at[8 + n], rsem.at[8 + n],
                   summer(head, group_pos)).start()

        @pl.when(here)
        def _():
            pltpu.make_async_copy(block, rows(held, place * PAD), lsem.at[4 + n]).start()

    def all_summed(held, count, n):
        @pl.when(head == mine)
        def _():
            some = rows(held, 0, (count - 1) * PAD)
            remote(some, some, ssem.at[8 + n], rsem.at[8 + n], (x, sib)).wait()
            pltpu.make_async_copy(rows(dkvb, 0), rows(held, 0), lsem.at[4 + n]).wait()

        @pl.when(head != mine)
        def _():
            remote(held, held, ssem.at[8 + n], rsem.at[8 + n], (x, sib)).wait()

    def finish(lo_group, hi_group):
        lo_row, hi_row = lo_group * PAD, hi_group * PAD
        for blk in range(lo_row // 128, -(-hi_row // 128)):
            a, b = max(lo_row - 128 * blk, 0), min(hi_row - 128 * blk, 128)
            v = dkT[:, 128 * blk:128 * blk + 128].T
            dkvb[128 * blk + a:128 * blk + b, :] = v[a:b].astype(BF)

    def to_sibling(number, lo_group, hi_group):
        @pl.loop(lo_group // 2, hi_group // 2)
        def _(k):
            g = 2 * k + 1 - core
            remote(rows(dkvb, g * PAD), rows(sibr, g * PAD), ssem.at[5], dsem.at[number], (x, sib)).start()

    def to_owners(number, lo_group, hi_group):
        n = (hi_group - lo_group) // 2 * PAD
        remote(rows(dkvb, 0, n), rows(sibr, 0, n), ssem.at[5], dsem.at[number], (x, sib)).wait_recv()

        @pl.loop(lo_group // 2, hi_group // 2)
        def _(k):
            g = 2 * k + core
            r = pl.ds(pl.multiple_of(g * PAD, 16), PAD)
            dkvb[r, :] = (dkvb[r, :].astype(F32) + sibr[r, :].astype(F32)).astype(BF)

            @pl.when(k != pos)
            def _():
                remote(rows(dkvb, g * PAD), rows(rkv, part * PAD), ssem.at[6], rsem.at[6], (x, g)).start()

            @pl.when(k == pos)
            def _():
                pltpu.make_async_copy(rows(dkvb, g * PAD), rows(rkv, part * PAD), lsem.at[7]).start()

            to_summer(rows(dkvb, g * PAD), 2 * spot + pos % 2, cgl, k, 1)

    for number, (slot0, slots, keys, CHUNK, lo_group, hi_group) in enumerate(BATCHES):
        row0, count = slot0 * PAD, slots * PAD
        rr = slice(row0, row0 + count)
        steps = keys // CHUNK
        macc[0:count, :] = jnp.full((count, 128), -3e38, F32)

        @pl.loop(0, steps)
        def _(c):
            kk = pl.ds(pl.multiple_of(c * CHUNK, 128), CHUNK)
            sc = dot_nt(qx[rr, :], kvx[kk, :])
            sbuf[0:count, kk] = sc
            top = macc[0:count, :]
            for i in range(CHUNK // 128):
                top = jnp.maximum(top, sc[:, 128 * i:128 * i + 128])
            macc[0:count, :] = top

        if number > 0:
            to_owners(number - 1, *BATCHES[number - 1][4:])
        row_max = jnp.max(macc[0:count, :], axis=1, keepdims=True)
        acc[0:count, :] = jnp.zeros((count, 256), F32)

        @pl.loop(0, steps)
        def _(c):
            kk = pl.ds(pl.multiple_of(c * CHUNK, 128), CHUNK)
            p = jnp.exp(sbuf[0:count, kk] - row_max).astype(BF)
            pbuf[0:count, kk] = p
            acc[0:count, :] += dot(p, kvx[kk, :])

        if number == 2:
            @pl.loop(1, 4)
            def _(k):
                frm = (x + k) % 4
                q = 2 * frm + core
                remote(al.at[:, q], al.at[:, q], ssem.at[2], xsem.at[frm], (x, sib)).wait_recv()
                remote(al.at[:, q], al.at[:, q], ssem.at[7], rsem.at[7], (x, sib)).start()

        lane = lax.broadcasted_iota(jnp.int32, (count, 128), 1)
        near = lane < 64
        inv = 1.0 / acc[0:count, 128 + ONE:128 + ONE + 1]
        ctx = (acc[0:count, 0:128] * inv).astype(BF)
        qrow = qg[rr, :].astype(F32)
        dots = jnp.sum(jnp.where(near, 0.0, ctx.astype(F32) * qrow), axis=1, keepdims=True)
        dhi = dots.astype(BF).astype(F32)
        dlo = dots - dhi
        qx[rr, 0:128] = jnp.where(near, 0.0, qrow).astype(BF)
        qx[rr, 128:256] = jnp.where(lane == ONE, -dhi, jnp.where(lane == TWO, -dlo, 0.0)).astype(BF)
        qn = qrow * jnp.where(near, 0.125 * inv, inv)
        qgT[:, 0:count] = qn.T.astype(BF)
        dq[0:count, :] = jnp.zeros((count, 128), F32)

        @pl.loop(0, steps)
        def _(c):
            kk = pl.ds(pl.multiple_of(c * CHUNK, 128), CHUNK)
            p = pbuf[0:count, kk]
            dpd = dot_nt(qx[rr, :], kvx[kk, :])
            ds = (p.astype(F32) * dpd).astype(BF)
            dq[0:count, :] += dot(ds, kvx[kk, 0:128])
            dk = dot(qgT[0:64, 0:count], ds)
            dv = dot(qgT[64:128, 0:count], p)
            if number == 0:
                dkT[0:64, kk] = dk
                dkT[64:128, kk] = dv
            else:
                dkT[0:64, kk] += dk
                dkT[64:128, kk] += dv

        resb[rr, :] = jnp.where(near, dq[0:count, :] * (0.125 * inv), ctx.astype(F32)).astype(BF)

        for j in range(slot0, slot0 + slots):
            to = 7 - j

            @pl.when(head != to)
            def _():
                remote(rows(resb, j * PAD), rows(rqc, head * PAD), ssem.at[4], rsem.at[4],
                       (x, 4 * to + quarter)).start()

            @pl.when(head == to)
            def _():
                pltpu.make_async_copy(rows(resb, j * PAD), rows(rqc, head * PAD), lsem.at[6]).start()

            to_summer(rows(resb, j * PAD), spot, cge, 2 * to + quarter // 2, 0)

        finish(lo_group, hi_group)
        to_sibling(number, lo_group, hi_group)
    to_owners(len(BATCHES) - 1, *BATCHES[-1][4:])

    remote(al.at[:, pl.ds(0, 4)], al.at[:, pl.ds(0, 4)], ssem.at[7], rsem.at[7], (x, sib)).wait()

    def transpose_inputs(i):
        for j in range(8):
            alT[i, 128 * j:128 * j + 128, :] = al[i, :, :, 128 * j:128 * j + 128].reshape(8 * PAD, 128).T

    transpose_inputs(0)
    transpose_inputs(1)

    def reduced(u, i, f):
        fb[u, :, i] = f.astype(BF).reshape(16, 16, 128)

    def spread(u):
        @pl.loop(1, 16)
        def _(k):
            to = (pos + k) % 16
            remote(fb.at[u, to], fr.at[u, k - 1], ssem.at[10 + u], rsem.at[10 + u], summer(mine, to)).start()

    all_summed(cge, 8, 0)
    wide_left = lax.broadcasted_iota(jnp.int32, (256, 128), 1) < 64
    for i in range(4):
        rr = slice(256 * i, 256 * i + 256)
        reduced(0, i, jnp.where(wide_left, dot(alT[0, rr, :], cge[...]), dot(alT[1, rr, :], cge[...])))
    spread(0)

    pltpu.make_async_copy(rows(resb, 0), rows(rqc, 0), lsem.at[6]).wait()
    remote(rows(rqc, 0, 7 * PAD), rows(rqc, 0, 7 * PAD), ssem.at[4], rsem.at[4], (x, sib)).wait()
    for i in range(4):
        a = rqc[(2 * i) * PAD:(2 * i + 1) * PAD, :].astype(F32)
        b = rqc[(2 * i + 1) * PAD:(2 * i + 2) * PAD, :].astype(F32)
        q_pair, c_pair = swap_pack(a, b, left)
        catp[0, i] = q_pair.astype(BF)
        catp[3, i] = c_pair.astype(BF)

    def wide(i):
        return jnp.concatenate([catp[i, j] for j in range(4)], axis=1)

    att = dot(wide(3), wout[...])
    attb[...] = att[0:TOK].astype(BF)
    outs = [
        pltpu.make_async_copy(attb, att_o.at[0], lsem.at[0]),
        pltpu.make_async_copy(ingb, ing_o.at[0], lsem.at[1]),
        pltpu.make_async_copy(wob.at[:, pl.ds(0, 3 * INNER)], wq_o, lsem.at[2]),
        pltpu.make_async_copy(wob.at[:, pl.ds(3 * INNER, INNER)], wo_o, lsem.at[3]),
    ]
    outs[0].start()

    all_summed(cgl, 16, 1)
    for q in range(8):
        cgx[q * PAD:(q + 1) * PAD, :] = (
            cgl[(2 * q) * PAD:(2 * q + 1) * PAD, :].astype(F32) + cgl[(2 * q + 1) * PAD:(2 * q + 2) * PAD, :].astype(F32)
        ).astype(BF)
    for i in range(4):
        reduced(1, i, dot(alT[0, 256 * i:256 * i + 256, :], cgx[...]))
    spread(1)

    pltpu.make_async_copy(rows(dkvb, 0), rows(rkv, 0), lsem.at[7]).wait()
    remote(rows(rkv, 0, 15 * PAD), rows(rkv, 0, 15 * PAD), ssem.at[6], rsem.at[6], (x, sib)).wait()
    for i in range(4):
        a = rkv[(4 * i) * PAD:(4 * i + 1) * PAD, :].astype(F32) + rkv[(4 * i + 1) * PAD:(4 * i + 2) * PAD, :].astype(F32)
        b = rkv[(4 * i + 2) * PAD:(4 * i + 3) * PAD, :].astype(F32) + rkv[(4 * i + 3) * PAD:(4 * i + 4) * PAD, :].astype(F32)
        k_pair, v_pair = swap_pack(a, b, left)
        catp[1, i] = k_pair.astype(BF)
        catp[2, i] = v_pair.astype(BF)

    ing = dot_nt(wide(0), wqkv[:, 0:INNER])
    ing += dot_nt(wide(1), wqkv[:, INNER:2 * INNER])
    ing += dot_nt(wide(2), wqkv[:, 2 * INNER:])
    ingb[...] = ing[0:TOK].astype(BF)
    outs[1].start()
    def sums(u):
        remote(fr.at[u], fr.at[u], ssem.at[10 + u], rsem.at[10 + u], (x, sib)).wait()
        v = fb[u, pos].astype(F32)
        for k in range(15):
            v += fr[u, k].astype(F32)
        for i in range(4):
            for c in range(2):
                fo[2 * i + c, u] = v[i, 8 * c:8 * c + 8]

    sums(0)
    sums(1)

    fi[mine] = fo[spot]

    @pl.loop(1, 8)
    def _(k):
        q = (spot + k) % 8
        remote(fo.at[q], fi.at[mine], ssem.at[12], rsem.at[12], at_spot(q)).start()

    remote(fi.at[pl.ds(0, 7)], fi.at[pl.ds(0, 7)], ssem.at[12], rsem.at[12], (x, sib)).wait()
    for i in range(4):
        for u, blocks in enumerate(((0, 3), (1, 2))):
            pair = swap_pack(fi[2 * i, u], fi[2 * i + 1, u], left[0:8])
            for block, v in zip(blocks, pair):
                wob[:, INNER * block + 128 * i:INNER * block + 128 * i + 128] = v
    outs[2].start()
    outs[3].start()

    remote(rows(dkvb, 0, 15 * PAD), rows(dkvb, 0, 15 * PAD), ssem.at[0], rsem.at[0], (x, sib)).wait_send()
    remote(rows(dkvb, 0, 7 * PAD), rows(dkvb, 0, 7 * PAD), ssem.at[1], rsem.at[1], (x, sib)).wait_send()
    remote(rows(dkvb, 0, 16 * PAD), rows(dkvb, 0, 16 * PAD), ssem.at[5], rsem.at[5], (x, sib)).wait_send()
    remote(al.at[:, pl.ds(0, 3)], al.at[:, pl.ds(0, 3)], ssem.at[2], rsem.at[2], (x, sib)).wait_send()
    for c in outs:
        c.wait()


def hand_out(*refs):
    came, gone, held, sems = refs[0:4], refs[4:8], refs[8:12], refs[12]
    ins = [pltpu.make_async_copy(came[i], held[i], sems.at[i]) for i in range(4)]
    outs = [pltpu.make_async_copy(held[i], gone[i], sems.at[4 + i]) for i in range(4)]
    for c in ins:
        c.start()
    for i in range(4):
        ins[i].wait()
        outs[i].start()
    for c in outs:
        c.wait()


def shards(activations, qkv_weight, out_weight, out_grad):
    any_spec = pl.BlockSpec(memory_space=pl.ANY)
    V = pltpu.VMEM
    scratch = [
        V((2, 8, PAD, D), BF),
        V((2, D, 8 * PAD), BF),
        V((D, 3 * INNER), BF),
        V((INNER, D), BF),
        V((8 * PAD, 128), BF),
        V((8 * PAD, 128), BF),
        V((KEYS, 256), BF),
        V((8 * PAD, 128), BF),
        V((8 * PAD, 256), BF),
        V((3 * PAD, KEYS), F32),
        V((3 * PAD, KEYS), BF),
        V((3 * PAD, 128), F32),
        V((3 * PAD, 256), F32),
        V((3 * PAD, 128), F32),
        V((128, 3 * PAD), BF),
        V((128, KEYS), F32),
        V((KEYS, 128), BF),
        V((KEYS, 128), BF),
        V((8 * PAD, 128), BF),
        V((8 * PAD, 128), BF),
        V((16 * PAD, 128), BF),
        V((4, 4, PAD, 128), BF),
        V((8 * PAD, 128), BF),
        V((16 * PAD, 128), BF),
        V((8 * PAD, 128), BF),
        V((2, 16, 4, 16, 128), BF),
        V((2, 15, 4, 16, 128), BF),
        V((8, 2, 8, 128), F32),
        V((8, 2, 8, 128), F32),
        V((TOK, D), BF),
        V((TOK, D), BF),
        V((8, 2 * D), F32),
        pltpu.SemaphoreType.DMA((8,)),
        pltpu.SemaphoreType.DMA((13,)),
        pltpu.SemaphoreType.DMA((13,)),
        pltpu.SemaphoreType.DMA((16,)),
        pltpu.SemaphoreType.DMA((3,)),
        pltpu.SemaphoreType.DMA((4,)),
    ]
    made = pl.pallas_call(
        kernel,
        out_shape=(
            jax.ShapeDtypeStruct((1, TOK, D), BF),
            jax.ShapeDtypeStruct((1, TOK, D), BF),
            jax.ShapeDtypeStruct((8, 3 * INNER), F32),
            jax.ShapeDtypeStruct((8, INNER), F32),
        ),
        in_specs=[any_spec] * 4,
        out_specs=(any_spec,) * 4,
        scratch_shapes=scratch,
        compiler_params=pltpu.CompilerParams(
            collective_id=0, has_side_effects=True, vmem_limit_bytes=56 * 1024 * 1024),
        name="attention_sublayer",
    )(activations, qkv_weight, out_weight, out_grad)
    att, ing, wq, wo = pl.pallas_call(
        hand_out,
        out_shape=tuple(jax.ShapeDtypeStruct(a.shape, a.dtype) for a in made),
        in_specs=[any_spec] * 4,
        out_specs=(any_spec,) * 4,
        scratch_shapes=[V(a.shape, a.dtype) for a in made] + [pltpu.SemaphoreType.DMA((8,))],
        name="hand_out",
    )(*made)
    return att, ing, wq, wo.T


def solution(mesh):
    return jax.shard_map(
        shards,
        mesh=mesh,
        in_specs=(P("dp", "seq", None), P(), P(), P("dp", "seq", None)),
        out_specs=(
            P("dp", "seq", None),
            P("dp", "seq", None),
            P(("dp", "seq"), None),
            P(None, ("dp", "seq")),
        ),
        check_vma=False,
    )
```

```python
import functools
import math

import jax
import jax.numpy as jnp
import numpy as np
from jax import lax
from jax.experimental import pallas as pl
from jax.experimental.pallas import tpu as pltpu
from jax.sharding import PartitionSpec as P

MESH = pl.DeviceIdType.MESH
BF = jnp.bfloat16
F32 = jnp.float32

HEADS = 8
SEQ = 32
TOK = 136
PAD = 144
KEYS = SEQ * PAD
D = 1024
INNER = 512
SIDES = (1, 2, 3, 4, 5, 8, 9, 10, 14, 16, 20, 24, 32, 40)
ENDS = [int(v) for v in np.cumsum([a * a for a in SIDES])]
STARTS = [0] + ENDS[:-1]
FAR = 1 << 20
BIG = 1e30
TILES = ((224, 208), (144, 144), (224, 208))
ONE = 15
TWO = 16
BATCHES = (
    (0, 3, 4608, 2304, 22, 32),
    (3, 2, 3072, 1536, 14, 22),
    (5, 3, 1920, 1920, 0, 14),
)
NT = (((1,), (1,)), ((), ()))


def dot(a, b):
    return jnp.dot(a, b, preferred_element_type=F32)


def dot_nt(a, b):
    return lax.dot_general(a, b, NT, preferred_element_type=F32)


def lane_bounds(rows):
    lane = lax.broadcasted_iota(jnp.int32, (rows, 128), 1)
    lo = jnp.full((rows, 128), -1, jnp.int32)
    hi = jnp.full((rows, 128), -1, jnp.int32)
    for i, (a, b) in enumerate(zip(STARTS, ENDS)):
        lo = jnp.where(lane == i, a, lo)
        hi = jnp.where(lane == i, b, hi)
    lo = jnp.where(lane == 14, FAR, lo)
    hi = jnp.where(lane == 14, FAR + 1, hi)
    ones = (lane == ONE) | (lane == TWO)
    lo = jnp.where(ones, 0, lo)
    hi = jnp.where(ones, ENDS[-1], hi)
    return lo, hi


def swap_pack(a, b, left):
    return (
        jnp.where(left, a, pltpu.roll(b, 64, 1)),
        jnp.where(left, pltpu.roll(a, 64, 1), b),
    )


def kernel(act_h, wqkv_h, wout_h, og_h, att_o, ing_o, wq_o, wo_o,
           al, alT, wqkv, wout, sendkv, sendqg, kvx, qg, qx, pbuf, acc, dq,
           qgT, dkT, dkvb, sibr, resb, rqc, rkv, catp, cgx, fb, fr, fo, fi,
           attb, ingb, wob, lsem, ssem, rsem, ksem, dsem, xsem):
    x = lax.axis_index("dp")
    s = lax.axis_index("seq")
    head, quarter = s // 4, s % 4
    pos, core = s // 2, s % 2
    sib = s + 1 - 2 * core
    spot = 2 * x + core

    cin = [
        pltpu.make_async_copy(act_h.at[0], al.at[0, spot, pl.ds(0, TOK)], lsem.at[0]),
        pltpu.make_async_copy(wqkv_h, wqkv, lsem.at[1]),
        pltpu.make_async_copy(og_h.at[0], al.at[1, spot, pl.ds(0, TOK)], lsem.at[2]),
        pltpu.make_async_copy(wout_h, wout, lsem.at[3]),
    ]
    for c in cin:
        c.start()

    bar = pltpu.get_barrier_semaphore()

    @pl.loop(1, 16)
    def _(k):
        pl.semaphore_signal(bar, inc=1, device_id=(x, 2 * ((pos + k) % 16) + core), device_id_type=MESH)

    def at_spot(q):
        return (q // 2, 2 * pos + q % 2)

    @pl.loop(1, 8)
    def _(k):
        pl.semaphore_signal(bar, inc=1, device_id=at_spot((spot + k) % 8), device_id_type=MESH)

    for i in range(2):
        al[i, spot, TOK:PAD, :] = jnp.zeros((PAD - TOK, D), BF)

    def remote(src, dst, send, recv, dev):
        return pltpu.make_async_remote_copy(
            src_ref=src, dst_ref=dst, send_sem=send, recv_sem=recv, device_id=dev, device_id_type=MESH)

    def rows(ref, first, count=PAD):
        return ref.at[pl.ds(pl.multiple_of(first, 16), count)]

    def kvslot(g):
        return kvx.at[pl.ds(pl.multiple_of(g * PAD, 16), PAD), pl.ds(0, 128)]

    left = lax.broadcasted_iota(jnp.int32, (PAD, 128), 1) < 64

    cin[0].wait()
    cin[1].wait()
    kp = dot(al[0, spot], wqkv[:, INNER:2 * INNER])
    vp = dot(al[0, spot], wqkv[:, 2 * INNER:])
    for i in range(4):
        a, b = swap_pack(kp[:, 128 * i:128 * i + 128], vp[:, 128 * i:128 * i + 128], left)
        sendkv[(2 * i) * PAD:(2 * i + 1) * PAD, :] = a.astype(BF)
        sendkv[(2 * i + 1) * PAD:(2 * i + 2) * PAD, :] = b.astype(BF)

    cin[2].wait()
    cin[3].wait()
    qp = dot(al[0, spot], wqkv[:, 0:INNER])
    gp = dot_nt(al[1, spot], wout[...])
    for i in range(4):
        a, b = swap_pack(qp[:, 128 * i:128 * i + 128], gp[:, 128 * i:128 * i + 128], left)
        sendqg[(2 * i) * PAD:(2 * i + 1) * PAD, :] = a.astype(BF)
        sendqg[(2 * i + 1) * PAD:(2 * i + 2) * PAD, :] = b.astype(BF)

    lo, hi = lane_bounds(PAD)
    place = lax.broadcasted_iota(jnp.int32, (PAD, 128), 0)

    @pl.loop(0, SEQ)
    def _(g):
        t = jnp.where(place < TOK, place + g * TOK, FAR)
        kvx[pl.ds(pl.multiple_of(g * PAD, 16), PAD), 128:256] = jnp.where(
            (t >= lo) & (t < hi), 1.0, 0.0).astype(BF)

    pl.semaphore_wait(bar, 22)
    own_kv = pltpu.make_async_copy(rows(sendkv, head * PAD), kvslot(s), lsem.at[4])
    own_kv.start()
    remote(rows(sendkv, head * PAD), kvslot(s), ssem.at[3], rsem.at[3], (x, sib)).start()

    @pl.loop(1, 16)
    def _(k):
        to = (pos + k) % 16
        remote(rows(sendkv, (to // 2) * PAD), kvslot(s), ssem.at[0], ksem.at[pos], (x, 2 * to + core)).start()

    @pl.loop(1, 4)
    def _(k):
        remote(al.at[:, spot], al.at[:, spot], ssem.at[2], xsem.at[x], ((x + k) % 4, s)).start()

    remote(al.at[:, spot], al.at[:, spot], ssem.at[7], rsem.at[7], (x, sib)).start()

    slot = 7 - s // 4
    own_qg = pltpu.make_async_copy(rows(sendqg, head * PAD), rows(qg, slot * PAD), lsem.at[5])
    own_qg.start()

    @pl.loop(1, 8)
    def _(k):
        to = (head + k) % 8
        remote(rows(sendqg, to * PAD), rows(qg, slot * PAD), ssem.at[1], rsem.at[1], (x, 4 * to + quarter)).start()

    @pl.loop(1, 16)
    def _(k):
        frm = (pos + 16 - k) % 16
        g = 2 * frm + core
        remote(kvslot(g), kvslot(g), ssem.at[0], ksem.at[frm], (x, sib)).wait_recv()
        remote(kvslot(g), kvslot(g), ssem.at[3], rsem.at[3], (x, sib)).start()

    own_kv.wait()
    own_qg.wait()
    remote(rows(dkvb, 0, 7 * PAD), rows(dkvb, 0, 7 * PAD), ssem.at[1], rsem.at[1], (x, sib)).wait_recv()

    @pl.loop(0, 8)
    def _(j):
        g = 4 * (7 - j) + quarter
        t = jnp.where(place < TOK, place + g * TOK, ENDS[-1] - 1)
        r = pl.ds(pl.multiple_of(j * PAD, 16), PAD)
        qx[r, 128:256] = jnp.where(lo > t, -BIG, 0.0).astype(BF)
        qx[r, 0:128] = jnp.where(left, qg[r, :].astype(F32) * 0.125, 0.0).astype(BF)

    remote(rows(dkvb, 0, 16 * PAD), rows(dkvb, 0, 16 * PAD), ssem.at[3], rsem.at[3], (x, sib)).wait()

    part = 2 * head + (pos % 2)

    def finish(lo_group, hi_group):
        lo_row, hi_row = lo_group * PAD, hi_group * PAD
        for blk in range(lo_row // 128, -(-hi_row // 128)):
            a, b = max(lo_row - 128 * blk, 0), min(hi_row - 128 * blk, 128)
            v = dkT[:, 128 * blk:128 * blk + 128].T
            dkvb[128 * blk + a:128 * blk + b, :] = v[a:b].astype(BF)

    def to_sibling(number, lo_group, hi_group):
        @pl.loop(lo_group // 2, hi_group // 2)
        def _(k):
            g = 2 * k + 1 - core
            remote(rows(dkvb, g * PAD), rows(sibr, g * PAD), ssem.at[5], dsem.at[number], (x, sib)).start()

    def to_owners(number, lo_group, hi_group):
        n = (hi_group - lo_group) // 2 * PAD
        remote(rows(dkvb, 0, n), rows(sibr, 0, n), ssem.at[5], dsem.at[number], (x, sib)).wait_recv()

        @pl.loop(lo_group // 2, hi_group // 2)
        def _(k):
            g = 2 * k + core
            r = pl.ds(pl.multiple_of(g * PAD, 16), PAD)
            dkvb[r, :] = (dkvb[r, :].astype(F32) + sibr[r, :].astype(F32)).astype(BF)

            @pl.when(k != pos)
            def _():
                remote(rows(dkvb, g * PAD), rows(rkv, part * PAD), ssem.at[6], rsem.at[6], (x, g)).start()

            @pl.when(k == pos)
            def _():
                pltpu.make_async_copy(rows(dkvb, g * PAD), rows(rkv, part * PAD), lsem.at[7]).start()

    for number, (slot0, slots, keys, CHUNK, lo_group, hi_group) in enumerate(BATCHES):
        row0, count = slot0 * PAD, slots * PAD
        rr = slice(row0, row0 + count)
        ends = np.cumsum((0,) + TILES[number])
        scores = [dot_nt(qx[row0:row0 + ends[1], :], kvx[0:keys, :])]
        for i, (a, b) in enumerate(zip(ends[:-1], ends[1:])):
            if i + 2 < len(ends):
                scores.append(dot_nt(qx[row0 + b:row0 + ends[i + 2], :], kvx[0:keys, :]))
            row_max = jnp.max(scores[i], axis=1, keepdims=True)
            p = jnp.exp(scores[i] - row_max).astype(BF)
            pbuf[a:b, 0:keys] = p
            acc[a:b, :] = dot(p, kvx[0:keys, :])
            if i == 0 and number > 0:
                to_owners(number - 1, *BATCHES[number - 1][4:])
        if number == 2:
            @pl.loop(1, 4)
            def _(k):
                frm = (x + k) % 4
                q = 2 * frm + core
                remote(al.at[:, q], al.at[:, q], ssem.at[2], xsem.at[frm], (x, sib)).wait_recv()
                remote(al.at[:, q], al.at[:, q], ssem.at[7], rsem.at[7], (x, sib)).start()

        lane = lax.broadcasted_iota(jnp.int32, (count, 128), 1)
        near = lane < 64
        inv = 1.0 / acc[0:count, 128 + ONE:128 + ONE + 1]
        ctx = (acc[0:count, 0:128] * inv).astype(BF)
        qrow = qg[rr, :].astype(F32)
        dots = jnp.sum(jnp.where(near, 0.0, ctx.astype(F32) * qrow), axis=1, keepdims=True)
        dhi = dots.astype(BF).astype(F32)
        dlo = dots - dhi
        qx[rr, 0:128] = jnp.where(near, 0.0, qrow).astype(BF)
        qx[rr, 128:256] = jnp.where(lane == ONE, -dhi, jnp.where(lane == TWO, -dlo, 0.0)).astype(BF)
        qn = qrow * jnp.where(near, 0.125 * inv, inv)
        qgT[:, 0:count] = qn.T.astype(BF)
        dq[0:count, :] = jnp.zeros((count, 128), F32)

        parts = [slice(c * CHUNK, (c + 1) * CHUNK) for c in range(keys // CHUNK)]
        dpd = [dot_nt(qx[rr, :], kvx[parts[0], :])]
        ds = []
        for c, kk in enumerate(parts):
            if c + 1 < len(parts):
                dpd.append(dot_nt(qx[rr, :], kvx[parts[c + 1], :]))
            p = pbuf[0:count, kk]
            ds.append((p.astype(F32) * dpd[c]).astype(BF))
            if number < 2:
                dq[0:count, :] += dot(ds[c], kvx[kk, 0:128])
            dk = dot(qgT[0:64, 0:count], ds[c])
            dv = dot(qgT[64:128, 0:count], p)
            if number == 0:
                dkT[0:64, kk] = dk
                dkT[64:128, kk] = dv
            else:
                dkT[0:64, kk] += dk
                dkT[64:128, kk] += dv

        if number == 2:
            finish(lo_group, hi_group)
            to_sibling(number, lo_group, hi_group)
            for c, kk in enumerate(parts):
                dq[0:count, :] += dot(ds[c], kvx[kk, 0:128])
        resb[rr, :] = jnp.where(near, dq[0:count, :] * (0.125 * inv), ctx.astype(F32)).astype(BF)

        for j in range(slot0, slot0 + slots):
            to = 7 - j

            @pl.when(head != to)
            def _():
                remote(rows(resb, j * PAD), rows(rqc, head * PAD), ssem.at[4], rsem.at[4],
                       (x, 4 * to + quarter)).start()

            @pl.when(head == to)
            def _():
                pltpu.make_async_copy(rows(resb, j * PAD), rows(rqc, head * PAD), lsem.at[6]).start()

        if number < 2:
            finish(lo_group, hi_group)
            to_sibling(number, lo_group, hi_group)
    to_owners(len(BATCHES) - 1, *BATCHES[-1][4:])

    remote(al.at[:, pl.ds(0, 4)], al.at[:, pl.ds(0, 4)], ssem.at[7], rsem.at[7], (x, sib)).wait()

    def transpose_inputs(i):
        for j in range(8):
            alT[i, 128 * j:128 * j + 128, :] = al[i, :, :, 128 * j:128 * j + 128].reshape(8 * PAD, 128).T

    transpose_inputs(0)

    @pl.when(core == 1)
    def _():
        transpose_inputs(1)

    pltpu.make_async_copy(rows(resb, 0), rows(rqc, 0), lsem.at[6]).wait()
    remote(rows(rqc, 0, 7 * PAD), rows(rqc, 0, 7 * PAD), ssem.at[4], rsem.at[4], (x, sib)).wait()
    for i in range(4):
        a = rqc[(2 * i) * PAD:(2 * i + 1) * PAD, :].astype(F32)
        b = rqc[(2 * i + 1) * PAD:(2 * i + 2) * PAD, :].astype(F32)
        q_pair, c_pair = swap_pack(a, b, left)
        catp[0, i] = q_pair.astype(BF)
        catp[3, i] = c_pair.astype(BF)

    def wide(i):
        return jnp.concatenate([catp[i, j] for j in range(4)], axis=1)

    def exchange(u, blocks):
        own = pltpu.make_async_copy(catp.at[blocks[0] + (blocks[1] - blocks[0]) * core, x], cgx.at[u, spot], lsem.at[4 + u])
        own.start()

        @pl.loop(1, 8)
        def _(k):
            q = (spot + k) % 8
            block = blocks[0] + (blocks[1] - blocks[0]) * (q % 2)
            remote(catp.at[block, q // 2], cgx.at[u, spot], ssem.at[8 + u], rsem.at[8 + u], at_spot(q)).start()

        return own

    def partial_sums(u, own, lhs):
        own.wait()
        seven = cgx.at[u, pl.ds(0, 7)]
        remote(seven, seven, ssem.at[8 + u], rsem.at[8 + u], (x, sib)).wait()
        right = cgx[u].reshape(8 * PAD, 128)
        for i in range(4):
            f = dot(alT[lhs, 256 * i:256 * i + 256, :], right)
            fb[u, :, i] = f.astype(BF).reshape(16, 16, 128)

        @pl.loop(1, 16)
        def _(k):
            to = (pos + k) % 16
            remote(fb.at[u, to], fr.at[u, k - 1], ssem.at[10 + u], rsem.at[10 + u], (x, 2 * to + core)).start()

    def sums(u):
        remote(fr.at[u], fr.at[u], ssem.at[10 + u], rsem.at[10 + u], (x, sib)).wait()
        v = fb[u, pos].astype(F32)
        for k in range(15):
            v += fr[u, k].astype(F32)
        for i in range(4):
            for c in range(2):
                fo[2 * i + c, u] = v[i, 8 * c:8 * c + 8]

    early = exchange(0, (0, 3))
    att = dot(wide(3), wout[...])
    attb[...] = att[0:TOK].astype(BF)
    outs = [
        pltpu.make_async_copy(attb, att_o.at[0], lsem.at[0]),
        pltpu.make_async_copy(ingb, ing_o.at[0], lsem.at[1]),
        pltpu.make_async_copy(wob.at[:, pl.ds(0, 3 * INNER)], wq_o, lsem.at[2]),
        pltpu.make_async_copy(wob.at[:, pl.ds(3 * INNER, INNER)], wo_o, lsem.at[3]),
    ]
    outs[0].start()

    pltpu.make_async_copy(rows(dkvb, 0), rows(rkv, 0), lsem.at[7]).wait()
    remote(rows(rkv, 0, 15 * PAD), rows(rkv, 0, 15 * PAD), ssem.at[6], rsem.at[6], (x, sib)).wait()
    for i in range(4):
        a = rkv[(4 * i) * PAD:(4 * i + 1) * PAD, :].astype(F32) + rkv[(4 * i + 1) * PAD:(4 * i + 2) * PAD, :].astype(F32)
        b = rkv[(4 * i + 2) * PAD:(4 * i + 3) * PAD, :].astype(F32) + rkv[(4 * i + 3) * PAD:(4 * i + 4) * PAD, :].astype(F32)
        k_pair, v_pair = swap_pack(a, b, left)
        catp[1, i] = k_pair.astype(BF)
        catp[2, i] = v_pair.astype(BF)

    late = exchange(1, (1, 2))
    ing = dot_nt(wide(0), wqkv[:, 0:INNER])
    ing += dot_nt(wide(1), wqkv[:, INNER:2 * INNER])
    ing += dot_nt(wide(2), wqkv[:, 2 * INNER:])
    ingb[...] = ing[0:TOK].astype(BF)
    outs[1].start()
    partial_sums(0, early, core)
    partial_sums(1, late, 0)
    sums(0)
    sums(1)

    fi[spot] = fo[spot]

    @pl.loop(1, 8)
    def _(k):
        q = (spot + k) % 8
        remote(fo.at[q], fi.at[spot], ssem.at[12], rsem.at[12], at_spot(q)).start()

    remote(fi.at[pl.ds(0, 7)], fi.at[pl.ds(0, 7)], ssem.at[12], rsem.at[12], (x, sib)).wait()
    for i in range(4):
        for block, (c, u) in enumerate(((0, 0), (0, 1), (1, 1), (1, 0))):
            wob[:, INNER * block + 128 * i:INNER * block + 128 * i + 128] = fi[2 * i + c, u]
    outs[2].start()
    outs[3].start()

    remote(rows(dkvb, 0, 15 * PAD), rows(dkvb, 0, 15 * PAD), ssem.at[0], rsem.at[0], (x, sib)).wait_send()
    remote(rows(dkvb, 0, 7 * PAD), rows(dkvb, 0, 7 * PAD), ssem.at[1], rsem.at[1], (x, sib)).wait_send()
    remote(rows(dkvb, 0, 16 * PAD), rows(dkvb, 0, 16 * PAD), ssem.at[5], rsem.at[5], (x, sib)).wait_send()
    remote(al.at[:, pl.ds(0, 3)], al.at[:, pl.ds(0, 3)], ssem.at[2], rsem.at[2], (x, sib)).wait_send()
    for c in outs:
        c.wait()


def hand_out(*refs):
    came, gone, held, sems = refs[0:4], refs[4:8], refs[8:12], refs[12]
    ins = [pltpu.make_async_copy(came[i], held[i], sems.at[i]) for i in range(4)]
    outs = [pltpu.make_async_copy(held[i], gone[i], sems.at[4 + i]) for i in range(4)]
    for c in ins:
        c.start()
    for i in range(4):
        ins[i].wait()
        outs[i].start()
    for c in outs:
        c.wait()


def shards(activations, qkv_weight, out_weight, out_grad):
    any_spec = pl.BlockSpec(memory_space=pl.ANY)
    V = pltpu.VMEM
    scratch = [
        V((2, 8, PAD, D), BF),
        V((2, D, 8 * PAD), BF),
        V((D, 3 * INNER), BF),
        V((INNER, D), BF),
        V((8 * PAD, 128), BF),
        V((8 * PAD, 128), BF),
        V((KEYS, 256), BF),
        V((8 * PAD, 128), BF),
        V((8 * PAD, 256), BF),
        V((3 * PAD, KEYS), BF),
        V((3 * PAD, 256), F32),
        V((3 * PAD, 128), F32),
        V((128, 3 * PAD), BF),
        V((128, KEYS), F32),
        V((KEYS, 128), BF),
        V((KEYS, 128), BF),
        V((8 * PAD, 128), BF),
        V((8 * PAD, 128), BF),
        V((16 * PAD, 128), BF),
        V((4, 4, PAD, 128), BF),
        V((2, 8, PAD, 128), BF),
        V((2, 16, 4, 16, 128), BF),
        V((2, 15, 4, 16, 128), BF),
        V((8, 2, 8, 128), F32),
        V((8, 2, 8, 128), F32),
        V((TOK, D), BF),
        V((TOK, D), BF),
        V((8, 2 * D), F32),
        pltpu.SemaphoreType.DMA((8,)),
        pltpu.SemaphoreType.DMA((13,)),
        pltpu.SemaphoreType.DMA((13,)),
        pltpu.SemaphoreType.DMA((16,)),
        pltpu.SemaphoreType.DMA((3,)),
        pltpu.SemaphoreType.DMA((4,)),
    ]
    made = pl.pallas_call(
        kernel,
        out_shape=(
            jax.ShapeDtypeStruct((1, TOK, D), BF),
            jax.ShapeDtypeStruct((1, TOK, D), BF),
            jax.ShapeDtypeStruct((8, 3 * INNER), F32),
            jax.ShapeDtypeStruct((8, INNER), F32),
        ),
        in_specs=[any_spec] * 4,
        out_specs=(any_spec,) * 4,
        scratch_shapes=scratch,
        compiler_params=pltpu.CompilerParams(
            collective_id=0, has_side_effects=True, vmem_limit_bytes=56 * 1024 * 1024),
        name="attention_sublayer",
    )(activations, qkv_weight, out_weight, out_grad)
    att, ing, wq, wo = pl.pallas_call(
        hand_out,
        out_shape=tuple(jax.ShapeDtypeStruct(a.shape, a.dtype) for a in made),
        in_specs=[any_spec] * 4,
        out_specs=(any_spec,) * 4,
        scratch_shapes=[V(a.shape, a.dtype) for a in made] + [pltpu.SemaphoreType.DMA((8,))],
        name="hand_out",
    )(*made)
    return att, ing, wq, wo.T


def solution(mesh):
    return jax.shard_map(
        shards,
        mesh=mesh,
        in_specs=(P("dp", "seq", None), P(), P(), P("dp", "seq", None)),
        out_specs=(
            P("dp", "seq", None),
            P("dp", "seq", None),
            P(("dp", "seq"), None),
            P(None, ("dp", "seq")),
        ),
        check_vma=False,
    )
```

```python
import functools
import math

import jax
import jax.numpy as jnp
import numpy as np
from jax import lax
from jax.experimental import pallas as pl
from jax.experimental.pallas import tpu as pltpu
from jax.sharding import PartitionSpec as P

MESH = pl.DeviceIdType.MESH
BF = jnp.bfloat16
F32 = jnp.float32

HEADS = 8
SEQ = 32
TOK = 136
PAD = 144
KEYS = SEQ * PAD
D = 1024
INNER = 512
SIDES = (1, 2, 3, 4, 5, 8, 9, 10, 14, 16, 20, 24, 32, 40)
ENDS = [int(v) for v in np.cumsum([a * a for a in SIDES])]
STARTS = [0] + ENDS[:-1]
FAR = 1 << 20
BIG = 1e30
TILES = ((224, 208), (144, 144), (224, 208))
ONE = 15
TWO = 16
BATCHES = (
    (0, 3, 4608, 2304, 22, 32),
    (3, 2, 3072, 1536, 14, 22),
    (5, 3, 1920, 1920, 0, 14),
)
NT = (((1,), (1,)), ((), ()))


def dot(a, b):
    return jnp.dot(a, b, preferred_element_type=F32)


def dot_nt(a, b):
    return lax.dot_general(a, b, NT, preferred_element_type=F32)


def lane_bounds(rows):
    lane = lax.broadcasted_iota(jnp.int32, (rows, 128), 1)
    lo = jnp.full((rows, 128), -1, jnp.int32)
    hi = jnp.full((rows, 128), -1, jnp.int32)
    for i, (a, b) in enumerate(zip(STARTS, ENDS)):
        lo = jnp.where(lane == i, a, lo)
        hi = jnp.where(lane == i, b, hi)
    lo = jnp.where(lane == 14, FAR, lo)
    hi = jnp.where(lane == 14, FAR + 1, hi)
    ones = (lane == ONE) | (lane == TWO)
    lo = jnp.where(ones, 0, lo)
    hi = jnp.where(ones, ENDS[-1], hi)
    return lo, hi


def swap_pack(a, b, left):
    return (
        jnp.where(left, a, pltpu.roll(b, 64, 1)),
        jnp.where(left, pltpu.roll(a, 64, 1), b),
    )


def kernel(act_h, wqkv_h, wout_h, og_h, att_o, ing_o, wq_o, wo_o,
           al, alT, wqkv, wout, sendkv, sendqg, kvx, qg, qx, pbuf, acc, dq,
           qgT, dkT, dkvb, sibr, resb, rqc, rkv, catp, cgx, fb, fr, fo, fi,
           attb, ingb, wob, lsem, ssem, rsem, ksem, dsem, xsem):
    x = lax.axis_index("dp")
    s = lax.axis_index("seq")
    head, quarter = s // 4, s % 4
    pos, core = s // 2, s % 2
    sib = s + 1 - 2 * core
    spot = 2 * x + core

    cin = [
        pltpu.make_async_copy(act_h.at[0], al.at[0, spot, pl.ds(0, TOK)], lsem.at[0]),
        pltpu.make_async_copy(wqkv_h, wqkv, lsem.at[1]),
        pltpu.make_async_copy(og_h.at[0], al.at[1, spot, pl.ds(0, TOK)], lsem.at[2]),
        pltpu.make_async_copy(wout_h, wout, lsem.at[3]),
    ]
    for c in cin:
        c.start()

    bar = pltpu.get_barrier_semaphore()

    @pl.loop(1, 16)
    def _(k):
        pl.semaphore_signal(bar, inc=1, device_id=(x, 2 * ((pos + k) % 16) + core), device_id_type=MESH)

    def at_spot(q):
        return (q // 2, 2 * pos + q % 2)

    @pl.loop(1, 8)
    def _(k):
        pl.semaphore_signal(bar, inc=1, device_id=at_spot((spot + k) % 8), device_id_type=MESH)

    for i in range(2):
        al[i, spot, TOK:PAD, :] = jnp.zeros((PAD - TOK, D), BF)

    def remote(src, dst, send, recv, dev):
        return pltpu.make_async_remote_copy(
            src_ref=src, dst_ref=dst, send_sem=send, recv_sem=recv, device_id=dev, device_id_type=MESH)

    def rows(ref, first, count=PAD):
        return ref.at[pl.ds(pl.multiple_of(first, 16), count)]

    def kvslot(g):
        return kvx.at[pl.ds(pl.multiple_of(g * PAD, 16), PAD), pl.ds(0, 128)]

    left = lax.broadcasted_iota(jnp.int32, (PAD, 128), 1) < 64

    cin[0].wait()
    cin[1].wait()
    kp = dot(al[0, spot], wqkv[:, INNER:2 * INNER])
    vp = dot(al[0, spot], wqkv[:, 2 * INNER:])
    for i in range(4):
        a, b = swap_pack(kp[:, 128 * i:128 * i + 128], vp[:, 128 * i:128 * i + 128], left)
        sendkv[(2 * i) * PAD:(2 * i + 1) * PAD, :] = a.astype(BF)
        sendkv[(2 * i + 1) * PAD:(2 * i + 2) * PAD, :] = b.astype(BF)

    cin[2].wait()
    cin[3].wait()
    qp = dot(al[0, spot], wqkv[:, 0:INNER])
    gp = dot_nt(al[1, spot], wout[...])
    for i in range(4):
        a, b = swap_pack(qp[:, 128 * i:128 * i + 128], gp[:, 128 * i:128 * i + 128], left)
        sendqg[(2 * i) * PAD:(2 * i + 1) * PAD, :] = a.astype(BF)
        sendqg[(2 * i + 1) * PAD:(2 * i + 2) * PAD, :] = b.astype(BF)

    lo, hi = lane_bounds(PAD)
    place = lax.broadcasted_iota(jnp.int32, (PAD, 128), 0)

    @pl.loop(0, SEQ)
    def _(g):
        t = jnp.where(place < TOK, place + g * TOK, FAR)
        kvx[pl.ds(pl.multiple_of(g * PAD, 16), PAD), 128:256] = jnp.where(
            (t >= lo) & (t < hi), 1.0, 0.0).astype(BF)

    pl.semaphore_wait(bar, 22)
    own_kv = pltpu.make_async_copy(rows(sendkv, head * PAD), kvslot(s), lsem.at[4])
    own_kv.start()
    remote(rows(sendkv, head * PAD), kvslot(s), ssem.at[3], rsem.at[3], (x, sib)).start()

    @pl.loop(1, 16)
    def _(k):
        to = (pos + k) % 16
        remote(rows(sendkv, (to // 2) * PAD), kvslot(s), ssem.at[0], ksem.at[pos], (x, 2 * to + core)).start()

    @pl.loop(1, 4)
    def _(k):
        remote(al.at[:, spot], al.at[:, spot], ssem.at[2], xsem.at[x], ((x + k) % 4, s)).start()

    remote(al.at[:, spot], al.at[:, spot], ssem.at[7], rsem.at[7], (x, sib)).start()

    slot = 7 - s // 4
    own_qg = pltpu.make_async_copy(rows(sendqg, head * PAD), rows(qg, slot * PAD), lsem.at[5])
    own_qg.start()

    @pl.loop(1, 8)
    def _(k):
        to = (head + k) % 8
        remote(rows(sendqg, to * PAD), rows(qg, slot * PAD), ssem.at[1], rsem.at[1], (x, 4 * to + quarter)).start()

    @pl.loop(1, 16)
    def _(k):
        frm = (pos + 16 - k) % 16
        g = 2 * frm + core
        remote(kvslot(g), kvslot(g), ssem.at[0], ksem.at[frm], (x, sib)).wait_recv()
        remote(kvslot(g), kvslot(g), ssem.at[3], rsem.at[3], (x, sib)).start()

    own_kv.wait()
    own_qg.wait()
    remote(rows(dkvb, 0, 7 * PAD), rows(dkvb, 0, 7 * PAD), ssem.at[1], rsem.at[1], (x, sib)).wait_recv()

    @pl.loop(0, 8)
    def _(j):
        g = 4 * (7 - j) + quarter
        t = jnp.where(place < TOK, place + g * TOK, ENDS[-1] - 1)
        r = pl.ds(pl.multiple_of(j * PAD, 16), PAD)
        qx[r, 128:256] = jnp.where(lo > t, -BIG, 0.0).astype(BF)
        qx[r, 0:128] = jnp.where(left, qg[r, :].astype(F32) * 0.125, 0.0).astype(BF)

    remote(rows(dkvb, 0, 16 * PAD), rows(dkvb, 0, 16 * PAD), ssem.at[3], rsem.at[3], (x, sib)).wait()

    part = 2 * head + (pos % 2)

    def finish(lo_group, hi_group):
        lo_row, hi_row = lo_group * PAD, hi_group * PAD
        for blk in range(lo_row // 128, -(-hi_row // 128)):
            a, b = max(lo_row - 128 * blk, 0), min(hi_row - 128 * blk, 128)
            v = dkT[:, 128 * blk:128 * blk + 128].T
            dkvb[128 * blk + a:128 * blk + b, :] = v[a:b].astype(BF)

    def to_sibling(number, lo_group, hi_group):
        @pl.loop(lo_group // 2, hi_group // 2)
        def _(k):
            g = 2 * k + 1 - core
            remote(rows(dkvb, g * PAD), rows(sibr, g * PAD), ssem.at[5], dsem.at[number], (x, sib)).start()

    def to_owners(number, lo_group, hi_group):
        n = (hi_group - lo_group) // 2 * PAD
        remote(rows(dkvb, 0, n), rows(sibr, 0, n), ssem.at[5], dsem.at[number], (x, sib)).wait_recv()

        @pl.loop(lo_group // 2, hi_group // 2)
        def _(k):
            g = 2 * k + core
            r = pl.ds(pl.multiple_of(g * PAD, 16), PAD)
            dkvb[r, :] = (dkvb[r, :].astype(F32) + sibr[r, :].astype(F32)).astype(BF)

            @pl.when(k != pos)
            def _():
                remote(rows(dkvb, g * PAD), rows(rkv, part * PAD), ssem.at[6], rsem.at[6], (x, g)).start()

            @pl.when(k == pos)
            def _():
                pltpu.make_async_copy(rows(dkvb, g * PAD), rows(rkv, part * PAD), lsem.at[7]).start()

    for number, (slot0, slots, keys, CHUNK, lo_group, hi_group) in enumerate(BATCHES):
        row0, count = slot0 * PAD, slots * PAD
        rr = slice(row0, row0 + count)
        ends = np.cumsum((0,) + TILES[number])
        scores = [dot_nt(qx[row0:row0 + ends[1], :], kvx[0:keys, :])]
        for i, (a, b) in enumerate(zip(ends[:-1], ends[1:])):
            if i + 2 < len(ends):
                scores.append(dot_nt(qx[row0 + b:row0 + ends[i + 2], :], kvx[0:keys, :]))
            row_max = jnp.max(scores[i], axis=1, keepdims=True)
            p = jnp.exp(scores[i] - row_max).astype(BF)
            pbuf[a:b, 0:keys] = p
            acc[a:b, :] = dot(p, kvx[0:keys, :])
        if number > 0:
            to_owners(number - 1, *BATCHES[number - 1][4:])
        lane = lax.broadcasted_iota(jnp.int32, (count, 128), 1)
        near = lane < 64
        inv = 1.0 / acc[0:count, 128 + ONE:128 + ONE + 1]
        ctx = (acc[0:count, 0:128] * inv).astype(BF)
        qrow = qg[rr, :].astype(F32)
        dots = jnp.sum(jnp.where(near, 0.0, ctx.astype(F32) * qrow), axis=1, keepdims=True)
        dhi = dots.astype(BF).astype(F32)
        dlo = dots - dhi
        qx[rr, 0:128] = jnp.where(near, 0.0, qrow).astype(BF)
        qx[rr, 128:256] = jnp.where(lane == ONE, -dhi, jnp.where(lane == TWO, -dlo, 0.0)).astype(BF)
        qn = qrow * jnp.where(near, 0.125 * inv, inv)
        qgT[:, 0:count] = qn.T.astype(BF)
        dq[0:count, :] = jnp.zeros((count, 128), F32)

        parts = [slice(c * CHUNK, (c + 1) * CHUNK) for c in range(keys // CHUNK)]
        dpd = [dot_nt(qx[rr, :], kvx[parts[0], :])]
        ds = []
        for c, kk in enumerate(parts):
            if c + 1 < len(parts):
                dpd.append(dot_nt(qx[rr, :], kvx[parts[c + 1], :]))
            p = pbuf[0:count, kk]
            ds.append((p.astype(F32) * dpd[c]).astype(BF))
            dq[0:count, :] += dot(ds[c], kvx[kk, 0:128])
            dk = dot(qgT[0:64, 0:count], ds[c])
            dv = dot(qgT[64:128, 0:count], p)
            if number == 0:
                dkT[0:64, kk] = dk
                dkT[64:128, kk] = dv
            else:
                dkT[0:64, kk] += dk
                dkT[64:128, kk] += dv

        resb[rr, :] = jnp.where(near, dq[0:count, :] * (0.125 * inv), ctx.astype(F32)).astype(BF)

        for j in range(slot0, slot0 + slots):
            to = 7 - j

            @pl.when(head != to)
            def _():
                remote(rows(resb, j * PAD), rows(rqc, head * PAD), ssem.at[4], rsem.at[4],
                       (x, 4 * to + quarter)).start()

            @pl.when(head == to)
            def _():
                pltpu.make_async_copy(rows(resb, j * PAD), rows(rqc, head * PAD), lsem.at[6]).start()

        finish(lo_group, hi_group)
        to_sibling(number, lo_group, hi_group)

    to_owners(len(BATCHES) - 1, *BATCHES[-1][4:])

    @pl.loop(1, 4)
    def _(k):
        frm = (x + k) % 4
        q = 2 * frm + core
        remote(al.at[:, q], al.at[:, q], ssem.at[2], xsem.at[frm], (x, sib)).wait_recv()
        remote(al.at[:, q], al.at[:, q], ssem.at[7], rsem.at[7], (x, sib)).start()

    remote(al.at[:, pl.ds(0, 4)], al.at[:, pl.ds(0, 4)], ssem.at[7], rsem.at[7], (x, sib)).wait()

    def transpose_inputs(i):
        for j in range(8):
            alT[i, 128 * j:128 * j + 128, :] = al[i, :, :, 128 * j:128 * j + 128].reshape(8 * PAD, 128).T

    transpose_inputs(0)

    @pl.when(core == 1)
    def _():
        transpose_inputs(1)

    pltpu.make_async_copy(rows(resb, 0), rows(rqc, 0), lsem.at[6]).wait()
    remote(rows(rqc, 0, 7 * PAD), rows(rqc, 0, 7 * PAD), ssem.at[4], rsem.at[4], (x, sib)).wait()
    for i in range(4):
        a = rqc[(2 * i) * PAD:(2 * i + 1) * PAD, :].astype(F32)
        b = rqc[(2 * i + 1) * PAD:(2 * i + 2) * PAD, :].astype(F32)
        q_pair, c_pair = swap_pack(a, b, left)
        catp[0, i] = q_pair.astype(BF)
        catp[3, i] = c_pair.astype(BF)

    def wide(i):
        return jnp.concatenate([catp[i, j] for j in range(4)], axis=1)

    def exchange(u, blocks):
        own = pltpu.make_async_copy(catp.at[blocks[0] + (blocks[1] - blocks[0]) * core, x], cgx.at[u, spot], lsem.at[4 + u])
        own.start()

        @pl.loop(1, 8)
        def _(k):
            q = (spot + k) % 8
            block = blocks[0] + (blocks[1] - blocks[0]) * (q % 2)
            remote(catp.at[block, q // 2], cgx.at[u, spot], ssem.at[8 + u], rsem.at[8 + u], at_spot(q)).start()

        return own

    def partial_sums(u, own, lhs):
        own.wait()
        seven = cgx.at[u, pl.ds(0, 7)]
        remote(seven, seven, ssem.at[8 + u], rsem.at[8 + u], (x, sib)).wait()
        right = cgx[u].reshape(8 * PAD, 128)
        for i in range(4):
            f = dot(alT[lhs, 256 * i:256 * i + 256, :], right)
            fb[u, :, i] = f.astype(BF).reshape(16, 16, 128)

        @pl.loop(1, 16)
        def _(k):
            to = (pos + k) % 16
            remote(fb.at[u, to], fr.at[u, k - 1], ssem.at[10 + u], rsem.at[10 + u], (x, 2 * to + core)).start()

    def sums(u):
        remote(fr.at[u], fr.at[u], ssem.at[10 + u], rsem.at[10 + u], (x, sib)).wait()
        v = fb[u, pos].astype(F32)
        for k in range(15):
            v += fr[u, k].astype(F32)
        for i in range(4):
            for c in range(2):
                fo[2 * i + c, u] = v[i, 8 * c:8 * c + 8]

    early = exchange(0, (0, 3))
    att = dot(wide(3), wout[...])
    attb[...] = att[0:TOK].astype(BF)
    outs = [
        pltpu.make_async_copy(attb, att_o.at[0], lsem.at[0]),
        pltpu.make_async_copy(ingb, ing_o.at[0], lsem.at[1]),
        pltpu.make_async_copy(wob.at[:, pl.ds(0, 3 * INNER)], wq_o, lsem.at[2]),
        pltpu.make_async_copy(wob.at[:, pl.ds(3 * INNER, INNER)], wo_o, lsem.at[3]),
    ]
    outs[0].start()

    pltpu.make_async_copy(rows(dkvb, 0), rows(rkv, 0), lsem.at[7]).wait()
    remote(rows(rkv, 0, 15 * PAD), rows(rkv, 0, 15 * PAD), ssem.at[6], rsem.at[6], (x, sib)).wait()
    for i in range(4):
        a = rkv[(4 * i) * PAD:(4 * i + 1) * PAD, :].astype(F32) + rkv[(4 * i + 1) * PAD:(4 * i + 2) * PAD, :].astype(F32)
        b = rkv[(4 * i + 2) * PAD:(4 * i + 3) * PAD, :].astype(F32) + rkv[(4 * i + 3) * PAD:(4 * i + 4) * PAD, :].astype(F32)
        k_pair, v_pair = swap_pack(a, b, left)
        catp[1, i] = k_pair.astype(BF)
        catp[2, i] = v_pair.astype(BF)

    late = exchange(1, (1, 2))
    ing = dot_nt(wide(0), wqkv[:, 0:INNER])
    ing += dot_nt(wide(1), wqkv[:, INNER:2 * INNER])
    ing += dot_nt(wide(2), wqkv[:, 2 * INNER:])
    ingb[...] = ing[0:TOK].astype(BF)
    outs[1].start()
    partial_sums(0, early, core)
    partial_sums(1, late, 0)
    sums(0)
    sums(1)

    fi[spot] = fo[spot]

    @pl.loop(1, 8)
    def _(k):
        q = (spot + k) % 8
        remote(fo.at[q], fi.at[spot], ssem.at[12], rsem.at[12], at_spot(q)).start()

    remote(fi.at[pl.ds(0, 7)], fi.at[pl.ds(0, 7)], ssem.at[12], rsem.at[12], (x, sib)).wait()
    for i in range(4):
        for block, (c, u) in enumerate(((0, 0), (0, 1), (1, 1), (1, 0))):
            wob[:, INNER * block + 128 * i:INNER * block + 128 * i + 128] = fi[2 * i + c, u]
    outs[2].start()
    outs[3].start()

    remote(rows(dkvb, 0, 15 * PAD), rows(dkvb, 0, 15 * PAD), ssem.at[0], rsem.at[0], (x, sib)).wait_send()
    remote(rows(dkvb, 0, 7 * PAD), rows(dkvb, 0, 7 * PAD), ssem.at[1], rsem.at[1], (x, sib)).wait_send()
    remote(rows(dkvb, 0, 16 * PAD), rows(dkvb, 0, 16 * PAD), ssem.at[5], rsem.at[5], (x, sib)).wait_send()
    remote(al.at[:, pl.ds(0, 3)], al.at[:, pl.ds(0, 3)], ssem.at[2], rsem.at[2], (x, sib)).wait_send()
    for c in outs:
        c.wait()


def hand_out(*refs):
    came, gone, held, sems = refs[0:4], refs[4:8], refs[8:12], refs[12]
    ins = [pltpu.make_async_copy(came[i], held[i], sems.at[i]) for i in range(4)]
    outs = [pltpu.make_async_copy(held[i], gone[i], sems.at[4 + i]) for i in range(4)]
    for c in ins:
        c.start()
    for i in range(4):
        ins[i].wait()
        outs[i].start()
    for c in outs:
        c.wait()


def shards(activations, qkv_weight, out_weight, out_grad):
    any_spec = pl.BlockSpec(memory_space=pl.ANY)
    V = pltpu.VMEM
    scratch = [
        V((2, 8, PAD, D), BF),
        V((2, D, 8 * PAD), BF),
        V((D, 3 * INNER), BF),
        V((INNER, D), BF),
        V((8 * PAD, 128), BF),
        V((8 * PAD, 128), BF),
        V((KEYS, 256), BF),
        V((8 * PAD, 128), BF),
        V((8 * PAD, 256), BF),
        V((3 * PAD, KEYS), BF),
        V((3 * PAD, 256), F32),
        V((3 * PAD, 128), F32),
        V((128, 3 * PAD), BF),
        V((128, KEYS), F32),
        V((KEYS, 128), BF),
        V((KEYS, 128), BF),
        V((8 * PAD, 128), BF),
        V((8 * PAD, 128), BF),
        V((16 * PAD, 128), BF),
        V((4, 4, PAD, 128), BF),
        V((2, 8, PAD, 128), BF),
        V((2, 16, 4, 16, 128), BF),
        V((2, 15, 4, 16, 128), BF),
        V((8, 2, 8, 128), F32),
        V((8, 2, 8, 128), F32),
        V((TOK, D), BF),
        V((TOK, D), BF),
        V((8, 2 * D), F32),
        pltpu.SemaphoreType.DMA((8,)),
        pltpu.SemaphoreType.DMA((13,)),
        pltpu.SemaphoreType.DMA((13,)),
        pltpu.SemaphoreType.DMA((16,)),
        pltpu.SemaphoreType.DMA((3,)),
        pltpu.SemaphoreType.DMA((4,)),
    ]
    made = pl.pallas_call(
        kernel,
        out_shape=(
            jax.ShapeDtypeStruct((1, TOK, D), BF),
            jax.ShapeDtypeStruct((1, TOK, D), BF),
            jax.ShapeDtypeStruct((8, 3 * INNER), F32),
            jax.ShapeDtypeStruct((8, INNER), F32),
        ),
        in_specs=[any_spec] * 4,
        out_specs=(any_spec,) * 4,
        scratch_shapes=scratch,
        compiler_params=pltpu.CompilerParams(
            collective_id=0, has_side_effects=True, vmem_limit_bytes=56 * 1024 * 1024),
        name="attention_sublayer",
    )(activations, qkv_weight, out_weight, out_grad)
    att, ing, wq, wo = pl.pallas_call(
        hand_out,
        out_shape=tuple(jax.ShapeDtypeStruct(a.shape, a.dtype) for a in made),
        in_specs=[any_spec] * 4,
        out_specs=(any_spec,) * 4,
        scratch_shapes=[V(a.shape, a.dtype) for a in made] + [pltpu.SemaphoreType.DMA((8,))],
        name="hand_out",
    )(*made)
    return att, ing, wq, wo.T


def solution(mesh):
    return jax.shard_map(
        shards,
        mesh=mesh,
        in_specs=(P("dp", "seq", None), P(), P(), P("dp", "seq", None)),
        out_specs=(
            P("dp", "seq", None),
            P("dp", "seq", None),
            P(("dp", "seq"), None),
            P(None, ("dp", "seq")),
        ),
        check_vma=False,
    )
```

```python
import functools
import math

import jax
import jax.numpy as jnp
import numpy as np
from jax import lax
from jax.experimental import pallas as pl
from jax.experimental.pallas import tpu as pltpu
from jax.sharding import PartitionSpec as P

MESH = pl.DeviceIdType.MESH
BF = jnp.bfloat16
F32 = jnp.float32

HEADS = 8
SEQ = 32
TOK = 136
PAD = 144
KEYS = SEQ * PAD
D = 1024
INNER = 512
SIDES = (1, 2, 3, 4, 5, 8, 9, 10, 14, 16, 20, 24, 32, 40)
ENDS = [int(v) for v in np.cumsum([a * a for a in SIDES])]
STARTS = [0] + ENDS[:-1]
FAR = 1 << 20
BIG = 1e30
TILES = ((224, 208), (144, 144), (224, 208))
ONE = 15
TWO = 16
BATCHES = (
    (0, 3, 4608, 2304, 22, 32),
    (3, 2, 3072, 1536, 14, 22),
    (5, 3, 1920, 1920, 0, 14),
)
NT = (((1,), (1,)), ((), ()))


def dot(a, b):
    return jnp.dot(a, b, preferred_element_type=F32)


def dot_nt(a, b):
    return lax.dot_general(a, b, NT, preferred_element_type=F32)


def lane_bounds(rows):
    lane = lax.broadcasted_iota(jnp.int32, (rows, 128), 1)
    lo = jnp.full((rows, 128), -1, jnp.int32)
    hi = jnp.full((rows, 128), -1, jnp.int32)
    for i, (a, b) in enumerate(zip(STARTS, ENDS)):
        lo = jnp.where(lane == i, a, lo)
        hi = jnp.where(lane == i, b, hi)
    lo = jnp.where(lane == 14, FAR, lo)
    hi = jnp.where(lane == 14, FAR + 1, hi)
    ones = (lane == ONE) | (lane == TWO)
    lo = jnp.where(ones, 0, lo)
    hi = jnp.where(ones, ENDS[-1], hi)
    return lo, hi


def swap_pack(a, b, left):
    return (
        jnp.where(left, a, pltpu.roll(b, 64, 1)),
        jnp.where(left, pltpu.roll(a, 64, 1), b),
    )


def kernel(act_h, wqkv_h, wout_h, og_h, att_o, ing_o, wq_o, wo_o,
           al, alT, wqkv, wout, sendkv, sendqg, kvx, qg, qx, pbuf, acc, dq,
           qgT, dkT, dkvb, sibr, resb, rqc, rkv, catp, cgx, fb, fr, fo, fi,
           attb, ingb, wob, lsem, ssem, rsem, ksem, dsem, xsem):
    x = lax.axis_index("dp")
    s = lax.axis_index("seq")
    head, quarter = s // 4, s % 4
    pos, core = s // 2, s % 2
    sib = s + 1 - 2 * core
    spot = 2 * x + core

    cin = [
        pltpu.make_async_copy(act_h.at[0], al.at[0, spot, pl.ds(0, TOK)], lsem.at[0]),
        pltpu.make_async_copy(wqkv_h, wqkv, lsem.at[1]),
        pltpu.make_async_copy(og_h.at[0], al.at[1, spot, pl.ds(0, TOK)], lsem.at[2]),
        pltpu.make_async_copy(wout_h, wout, lsem.at[3]),
    ]
    for c in cin:
        c.start()

    bar = pltpu.get_barrier_semaphore()

    @pl.loop(1, 16)
    def _(k):
        pl.semaphore_signal(bar, inc=1, device_id=(x, 2 * ((pos + k) % 16) + core), device_id_type=MESH)

    def at_spot(q):
        return (q // 2, 2 * pos + q % 2)

    @pl.loop(1, 8)
    def _(k):
        pl.semaphore_signal(bar, inc=1, device_id=at_spot((spot + k) % 8), device_id_type=MESH)

    for i in range(2):
        al[i, spot, TOK:PAD, :] = jnp.zeros((PAD - TOK, D), BF)

    def remote(src, dst, send, recv, dev):
        return pltpu.make_async_remote_copy(
            src_ref=src, dst_ref=dst, send_sem=send, recv_sem=recv, device_id=dev, device_id_type=MESH)

    def rows(ref, first, count=PAD):
        return ref.at[pl.ds(pl.multiple_of(first, 16), count)]

    def kvslot(g):
        return kvx.at[pl.ds(pl.multiple_of(g * PAD, 16), PAD), pl.ds(0, 128)]

    left = lax.broadcasted_iota(jnp.int32, (PAD, 128), 1) < 64

    cin[0].wait()
    cin[1].wait()
    kp = dot(al[0, spot], wqkv[:, INNER:2 * INNER])
    vp = dot(al[0, spot], wqkv[:, 2 * INNER:])
    for i in range(4):
        a, b = swap_pack(kp[:, 128 * i:128 * i + 128], vp[:, 128 * i:128 * i + 128], left)
        sendkv[(2 * i) * PAD:(2 * i + 1) * PAD, :] = a.astype(BF)
        sendkv[(2 * i + 1) * PAD:(2 * i + 2) * PAD, :] = b.astype(BF)

    cin[2].wait()
    cin[3].wait()
    qp = dot(al[0, spot], wqkv[:, 0:INNER])
    gp = dot_nt(al[1, spot], wout[...])
    for i in range(4):
        a, b = swap_pack(qp[:, 128 * i:128 * i + 128], gp[:, 128 * i:128 * i + 128], left)
        sendqg[(2 * i) * PAD:(2 * i + 1) * PAD, :] = a.astype(BF)
        sendqg[(2 * i + 1) * PAD:(2 * i + 2) * PAD, :] = b.astype(BF)

    lo, hi = lane_bounds(PAD)
    place = lax.broadcasted_iota(jnp.int32, (PAD, 128), 0)

    @pl.loop(0, SEQ)
    def _(g):
        t = jnp.where(place < TOK, place + g * TOK, FAR)
        kvx[pl.ds(pl.multiple_of(g * PAD, 16), PAD), 128:256] = jnp.where(
            (t >= lo) & (t < hi), 1.0, 0.0).astype(BF)

    pl.semaphore_wait(bar, 22)
    own_kv = pltpu.make_async_copy(rows(sendkv, head * PAD), kvslot(s), lsem.at[4])
    own_kv.start()
    remote(rows(sendkv, head * PAD), kvslot(s), ssem.at[3], rsem.at[3], (x, sib)).start()

    @pl.loop(1, 16)
    def _(k):
        to = (pos + k) % 16
        remote(rows(sendkv, (to // 2) * PAD), kvslot(s), ssem.at[0], ksem.at[pos], (x, 2 * to + core)).start()

    @pl.loop(1, 4)
    def _(k):
        remote(al.at[:, spot], al.at[:, spot], ssem.at[2], xsem.at[x], ((x + k) % 4, s)).start()

    remote(al.at[:, spot], al.at[:, spot], ssem.at[7], rsem.at[7], (x, sib)).start()

    slot = 7 - s // 4
    own_qg = pltpu.make_async_copy(rows(sendqg, head * PAD), rows(qg, slot * PAD), lsem.at[5])
    own_qg.start()

    @pl.loop(1, 8)
    def _(k):
        to = (head + k) % 8
        remote(rows(sendqg, to * PAD), rows(qg, slot * PAD), ssem.at[1], rsem.at[1], (x, 4 * to + quarter)).start()

    @pl.loop(1, 16)
    def _(k):
        frm = (pos + 16 - k) % 16
        g = 2 * frm + core
        remote(kvslot(g), kvslot(g), ssem.at[0], ksem.at[frm], (x, sib)).wait_recv()
        remote(kvslot(g), kvslot(g), ssem.at[3], rsem.at[3], (x, sib)).start()

    own_kv.wait()
    own_qg.wait()
    remote(rows(dkvb, 0, 7 * PAD), rows(dkvb, 0, 7 * PAD), ssem.at[1], rsem.at[1], (x, sib)).wait_recv()

    @pl.loop(0, 8)
    def _(j):
        g = 4 * (7 - j) + quarter
        t = jnp.where(place < TOK, place + g * TOK, ENDS[-1] - 1)
        r = pl.ds(pl.multiple_of(j * PAD, 16), PAD)
        qx[r, 128:256] = jnp.where(lo > t, -BIG, 0.0).astype(BF)
        qx[r, 0:128] = jnp.where(left, qg[r, :].astype(F32) * 0.125, 0.0).astype(BF)

    remote(rows(dkvb, 0, 16 * PAD), rows(dkvb, 0, 16 * PAD), ssem.at[3], rsem.at[3], (x, sib)).wait()

    part = 2 * head + (pos % 2)

    def finish(lo_group, hi_group):
        lo_row, hi_row = lo_group * PAD, hi_group * PAD
        for blk in range(lo_row // 128, -(-hi_row // 128)):
            a, b = max(lo_row - 128 * blk, 0), min(hi_row - 128 * blk, 128)
            v = dkT[:, 128 * blk:128 * blk + 128].T
            dkvb[128 * blk + a:128 * blk + b, :] = v[a:b].astype(BF)

    def to_sibling(number, lo_group, hi_group):
        @pl.loop(lo_group // 2, hi_group // 2)
        def _(k):
            g = 2 * k + 1 - core
            remote(rows(dkvb, g * PAD), rows(sibr, g * PAD), ssem.at[5], dsem.at[number], (x, sib)).start()

    def to_owners(number, lo_group, hi_group):
        n = (hi_group - lo_group) // 2 * PAD
        remote(rows(dkvb, 0, n), rows(sibr, 0, n), ssem.at[5], dsem.at[number], (x, sib)).wait_recv()

        @pl.loop(lo_group // 2, hi_group // 2)
        def _(k):
            g = 2 * k + core
            r = pl.ds(pl.multiple_of(g * PAD, 16), PAD)
            dkvb[r, :] = (dkvb[r, :].astype(F32) + sibr[r, :].astype(F32)).astype(BF)

            @pl.when(k != pos)
            def _():
                remote(rows(dkvb, g * PAD), rows(rkv, part * PAD), ssem.at[6], rsem.at[6], (x, g)).start()

            @pl.when(k == pos)
            def _():
                pltpu.make_async_copy(rows(dkvb, g * PAD), rows(rkv, part * PAD), lsem.at[7]).start()

    for number, (slot0, slots, keys, CHUNK, lo_group, hi_group) in enumerate(BATCHES):
        row0, count = slot0 * PAD, slots * PAD
        rr = slice(row0, row0 + count)
        ends = np.cumsum((0,) + TILES[number])
        scores = [dot_nt(qx[row0:row0 + ends[1], :], kvx[0:keys, :])]
        for i, (a, b) in enumerate(zip(ends[:-1], ends[1:])):
            if i + 2 < len(ends):
                scores.append(dot_nt(qx[row0 + b:row0 + ends[i + 2], :], kvx[0:keys, :]))
            row_max = jnp.max(scores[i], axis=1, keepdims=True)
            p = jnp.exp(scores[i] - row_max).astype(BF)
            pbuf[a:b, 0:keys] = p
            acc[a:b, :] = dot(p, kvx[0:keys, :])
        if number > 0:
            to_owners(number - 1, *BATCHES[number - 1][4:])
        lane = lax.broadcasted_iota(jnp.int32, (count, 128), 1)
        near = lane < 64
        inv = 1.0 / acc[0:count, 128 + ONE:128 + ONE + 1]
        ctx = (acc[0:count, 0:128] * inv).astype(BF)
        qrow = qg[rr, :].astype(F32)
        dots = jnp.sum(jnp.where(near, 0.0, ctx.astype(F32) * qrow), axis=1, keepdims=True)
        dhi = dots.astype(BF).astype(F32)
        dlo = dots - dhi
        qx[rr, 0:128] = jnp.where(near, 0.0, qrow).astype(BF)
        qx[rr, 128:256] = jnp.where(lane == ONE, -dhi, jnp.where(lane == TWO, -dlo, 0.0)).astype(BF)
        qn = qrow * jnp.where(near, 0.125 * inv, inv)
        qgT[:, 0:count] = qn.T.astype(BF)
        dq[0:count, :] = jnp.zeros((count, 128), F32)

        parts = [slice(c * CHUNK, (c + 1) * CHUNK) for c in range(keys // CHUNK)]
        dpd = [dot_nt(qx[rr, :], kvx[parts[0], :])]
        ds = []
        for c, kk in enumerate(parts):
            if c + 1 < len(parts):
                dpd.append(dot_nt(qx[rr, :], kvx[parts[c + 1], :]))
            p = pbuf[0:count, kk]
            ds.append((p.astype(F32) * dpd[c]).astype(BF))
            dq[0:count, :] += dot(ds[c], kvx[kk, 0:128])
            dk = dot(qgT[0:64, 0:count], ds[c])
            dv = dot(qgT[64:128, 0:count], p)
            if number == 0:
                dkT[0:64, kk] = dk
                dkT[64:128, kk] = dv
            else:
                dkT[0:64, kk] += dk
                dkT[64:128, kk] += dv

        resb[rr, :] = jnp.where(near, dq[0:count, :] * (0.125 * inv), ctx.astype(F32)).astype(BF)

        for j in range(slot0, slot0 + slots):
            to = 7 - j

            @pl.when(head != to)
            def _():
                remote(rows(resb, j * PAD), rows(rqc, head * PAD), ssem.at[4], rsem.at[4],
                       (x, 4 * to + quarter)).start()

            @pl.when(head == to)
            def _():
                pltpu.make_async_copy(rows(resb, j * PAD), rows(rqc, head * PAD), lsem.at[6]).start()

        finish(lo_group, hi_group)
        to_sibling(number, lo_group, hi_group)

    to_owners(len(BATCHES) - 1, *BATCHES[-1][4:])

    @pl.loop(1, 4)
    def _(k):
        frm = (x + k) % 4
        q = 2 * frm + core
        remote(al.at[:, q], al.at[:, q], ssem.at[2], xsem.at[frm], (x, sib)).wait_recv()
        remote(al.at[:, q], al.at[:, q], ssem.at[7], rsem.at[7], (x, sib)).start()

    pltpu.make_async_copy(rows(resb, 0), rows(rqc, 0), lsem.at[6]).wait()
    remote(rows(rqc, 0, 7 * PAD), rows(rqc, 0, 7 * PAD), ssem.at[4], rsem.at[4], (x, sib)).wait()
    for i in range(4):
        a = rqc[(2 * i) * PAD:(2 * i + 1) * PAD, :].astype(F32)
        b = rqc[(2 * i + 1) * PAD:(2 * i + 2) * PAD, :].astype(F32)
        q_pair, c_pair = swap_pack(a, b, left)
        catp[0, i] = q_pair.astype(BF)
        catp[3, i] = c_pair.astype(BF)

    def wide(i):
        return jnp.concatenate([catp[i, j] for j in range(4)], axis=1)

    def exchange(u, blocks):
        own = pltpu.make_async_copy(catp.at[blocks[0] + (blocks[1] - blocks[0]) * core, x], cgx.at[u, spot], lsem.at[4 + u])
        own.start()

        @pl.loop(1, 8)
        def _(k):
            q = (spot + k) % 8
            block = blocks[0] + (blocks[1] - blocks[0]) * (q % 2)
            remote(catp.at[block, q // 2], cgx.at[u, spot], ssem.at[8 + u], rsem.at[8 + u], at_spot(q)).start()

        return own

    def partial_sums(u, own, lhs):
        own.wait()
        seven = cgx.at[u, pl.ds(0, 7)]
        remote(seven, seven, ssem.at[8 + u], rsem.at[8 + u], (x, sib)).wait()
        right = cgx[u].reshape(8 * PAD, 128)
        for i in range(4):
            f = dot(alT[lhs, 256 * i:256 * i + 256, :], right)
            fb[u, :, i] = f.astype(BF).reshape(16, 16, 128)

        @pl.loop(1, 16)
        def _(k):
            to = (pos + k) % 16
            remote(fb.at[u, to], fr.at[u, k - 1], ssem.at[10 + u], rsem.at[10 + u], (x, 2 * to + core)).start()

    def sums(u):
        remote(fr.at[u], fr.at[u], ssem.at[10 + u], rsem.at[10 + u], (x, sib)).wait()
        v = fb[u, pos].astype(F32)
        for k in range(15):
            v += fr[u, k].astype(F32)
        for i in range(4):
            for c in range(2):
                fo[2 * i + c, u] = v[i, 8 * c:8 * c + 8]

    early = exchange(0, (0, 3))
    remote(al.at[:, pl.ds(0, 4)], al.at[:, pl.ds(0, 4)], ssem.at[7], rsem.at[7], (x, sib)).wait()

    def transpose_inputs(i):
        for j in range(8):
            alT[i, 128 * j:128 * j + 128, :] = al[i, :, :, 128 * j:128 * j + 128].reshape(8 * PAD, 128).T

    transpose_inputs(0)

    @pl.when(core == 1)
    def _():
        transpose_inputs(1)

    att = dot(wide(3), wout[...])
    attb[...] = att[0:TOK].astype(BF)
    outs = [
        pltpu.make_async_copy(attb, att_o.at[0], lsem.at[0]),
        pltpu.make_async_copy(ingb, ing_o.at[0], lsem.at[1]),
        pltpu.make_async_copy(wob.at[:, pl.ds(0, 3 * INNER)], wq_o, lsem.at[2]),
        pltpu.make_async_copy(wob.at[:, pl.ds(3 * INNER, INNER)], wo_o, lsem.at[3]),
    ]
    outs[0].start()

    pltpu.make_async_copy(rows(dkvb, 0), rows(rkv, 0), lsem.at[7]).wait()
    remote(rows(rkv, 0, 15 * PAD), rows(rkv, 0, 15 * PAD), ssem.at[6], rsem.at[6], (x, sib)).wait()
    for i in range(4):
        a = rkv[(4 * i) * PAD:(4 * i + 1) * PAD, :].astype(F32) + rkv[(4 * i + 1) * PAD:(4 * i + 2) * PAD, :].astype(F32)
        b = rkv[(4 * i + 2) * PAD:(4 * i + 3) * PAD, :].astype(F32) + rkv[(4 * i + 3) * PAD:(4 * i + 4) * PAD, :].astype(F32)
        k_pair, v_pair = swap_pack(a, b, left)
        catp[1, i] = k_pair.astype(BF)
        catp[2, i] = v_pair.astype(BF)

    late = exchange(1, (1, 2))
    ing = dot_nt(wide(0), wqkv[:, 0:INNER])
    ing += dot_nt(wide(1), wqkv[:, INNER:2 * INNER])
    ing += dot_nt(wide(2), wqkv[:, 2 * INNER:])
    ingb[...] = ing[0:TOK].astype(BF)
    outs[1].start()
    partial_sums(0, early, core)
    partial_sums(1, late, 0)
    sums(0)
    sums(1)

    fi[spot] = fo[spot]

    @pl.loop(1, 8)
    def _(k):
        q = (spot + k) % 8
        remote(fo.at[q], fi.at[spot], ssem.at[12], rsem.at[12], at_spot(q)).start()

    remote(fi.at[pl.ds(0, 7)], fi.at[pl.ds(0, 7)], ssem.at[12], rsem.at[12], (x, sib)).wait()
    for i in range(4):
        for block, (c, u) in enumerate(((0, 0), (0, 1), (1, 1), (1, 0))):
            wob[:, INNER * block + 128 * i:INNER * block + 128 * i + 128] = fi[2 * i + c, u]
    outs[2].start()
    outs[3].start()

    remote(rows(dkvb, 0, 15 * PAD), rows(dkvb, 0, 15 * PAD), ssem.at[0], rsem.at[0], (x, sib)).wait_send()
    remote(rows(dkvb, 0, 7 * PAD), rows(dkvb, 0, 7 * PAD), ssem.at[1], rsem.at[1], (x, sib)).wait_send()
    remote(rows(dkvb, 0, 16 * PAD), rows(dkvb, 0, 16 * PAD), ssem.at[5], rsem.at[5], (x, sib)).wait_send()
    remote(al.at[:, pl.ds(0, 3)], al.at[:, pl.ds(0, 3)], ssem.at[2], rsem.at[2], (x, sib)).wait_send()
    for c in outs:
        c.wait()


def hand_out(*refs):
    came, gone, held, sems = refs[0:4], refs[4:8], refs[8:12], refs[12]
    ins = [pltpu.make_async_copy(came[i], held[i], sems.at[i]) for i in range(4)]
    outs = [pltpu.make_async_copy(held[i], gone[i], sems.at[4 + i]) for i in range(4)]
    for c in ins:
        c.start()
    for i in range(4):
        ins[i].wait()
        outs[i].start()
    for c in outs:
        c.wait()


def shards(activations, qkv_weight, out_weight, out_grad):
    any_spec = pl.BlockSpec(memory_space=pl.ANY)
    V = pltpu.VMEM
    scratch = [
        V((2, 8, PAD, D), BF),
        V((2, D, 8 * PAD), BF),
        V((D, 3 * INNER), BF),
        V((INNER, D), BF),
        V((8 * PAD, 128), BF),
        V((8 * PAD, 128), BF),
        V((KEYS, 256), BF),
        V((8 * PAD, 128), BF),
        V((8 * PAD, 256), BF),
        V((3 * PAD, KEYS), BF),
        V((3 * PAD, 256), F32),
        V((3 * PAD, 128), F32),
        V((128, 3 * PAD), BF),
        V((128, KEYS), F32),
        V((KEYS, 128), BF),
        V((KEYS, 128), BF),
        V((8 * PAD, 128), BF),
        V((8 * PAD, 128), BF),
        V((16 * PAD, 128), BF),
        V((4, 4, PAD, 128), BF),
        V((2, 8, PAD, 128), BF),
        V((2, 16, 4, 16, 128), BF),
        V((2, 15, 4, 16, 128), BF),
        V((8, 2, 8, 128), F32),
        V((8, 2, 8, 128), F32),
        V((TOK, D), BF),
        V((TOK, D), BF),
        V((8, 2 * D), F32),
        pltpu.SemaphoreType.DMA((8,)),
        pltpu.SemaphoreType.DMA((13,)),
        pltpu.SemaphoreType.DMA((13,)),
        pltpu.SemaphoreType.DMA((16,)),
        pltpu.SemaphoreType.DMA((3,)),
        pltpu.SemaphoreType.DMA((4,)),
    ]
    made = pl.pallas_call(
        kernel,
        out_shape=(
            jax.ShapeDtypeStruct((1, TOK, D), BF),
            jax.ShapeDtypeStruct((1, TOK, D), BF),
            jax.ShapeDtypeStruct((8, 3 * INNER), F32),
            jax.ShapeDtypeStruct((8, INNER), F32),
        ),
        in_specs=[any_spec] * 4,
        out_specs=(any_spec,) * 4,
        scratch_shapes=scratch,
        compiler_params=pltpu.CompilerParams(
            collective_id=0, has_side_effects=True, vmem_limit_bytes=56 * 1024 * 1024),
        name="attention_sublayer",
    )(activations, qkv_weight, out_weight, out_grad)
    att, ing, wq, wo = pl.pallas_call(
        hand_out,
        out_shape=tuple(jax.ShapeDtypeStruct(a.shape, a.dtype) for a in made),
        in_specs=[any_spec] * 4,
        out_specs=(any_spec,) * 4,
        scratch_shapes=[V(a.shape, a.dtype) for a in made] + [pltpu.SemaphoreType.DMA((8,))],
        name="hand_out",
    )(*made)
    return att, ing, wq, wo.T


def solution(mesh):
    return jax.shard_map(
        shards,
        mesh=mesh,
        in_specs=(P("dp", "seq", None), P(), P(), P("dp", "seq", None)),
        out_specs=(
            P("dp", "seq", None),
            P("dp", "seq", None),
            P(("dp", "seq"), None),
            P(None, ("dp", "seq")),
        ),
        check_vma=False,
    )
```
